128 devices in a mesh: row: 4 (over z), col: 32 (over x, y, core).
Axes of the slice: x: 4, y: 4, z: 4, core: 2. Of those that a mesh axis runs over, the one named last changes fastest.
Arguments:
- splat_params: float32 [10, 8388608], P(None, ('row', 'col')), as said below
- list_owner: int32 [512, 1024, 1], P(('row', 'col')), may hold values from 0 to 127; in each aligned block of 4096 rows (0 to 4095, 4096 to 8191, ..., all dimensions but the last counted through in order) at most 64 rows name the same one
- list_slot: int32 [512, 1024], P(('row', 'col')), may hold values from 0 to 65535
- list_length: int32 [512], P(('row', 'col')), may hold values from 512 to 1024, as said below
- target: float32 [4, 512, 256], P(None, ('row', 'col')), may hold values from 0 to 1
Outputs:
- rendered: float32 [4, 512, 256], P(None, ('row', 'col'))
- splat_grads: float32 [10, 8388608], P(None, ('row', 'col'))
The draws below stay inside these ranges and needn't reach their ends.
Inputs may be any that keep to these rules, and one draw needn't show every extreme that they name: `list_owner`: within the entries of one device's tiles (aligned blocks of 4096 entries), no owner is named more than 64 times, a bound that some block reaches. `list_length`: some tile has exactly 1024 live entries; every tile has at least 512. `splat_params`: conic entries satisfy a > 0, c > 0 and b * b < a * c; opacity lies in (0, 0.02]; colours and depth lie in [0, 1].
All inputs are finite; a program needn't handle non-finite values.
Results may differ from the reference program's by a relative error of at most 0.0003.
Values sent between devices are 32-bit elements; how exact they have to be, the bound alone decides.
No kernel may reach another device: no remote copies, remote signals or barrier semaphores. Data moves between devices by JAX's collectives and lax.ppermute only.
A program may use at most 128 MiB of HBM per device.

```python
import math
import jax
import jax.numpy as jnp
import numpy as np
from jax import lax

SIDE = 16
PIX = 256
K = 1024
TILE_DEV = 4
G_DEV = 65536
TILES = 512
GROUP_TILES = 128
SPLATS = 8388608
CAP = 64
DEVICES = 128


def log_uniform(key, shape, low, high):
    return jnp.exp(jax.random.uniform(key, shape, jnp.float32, jnp.log(low), jnp.log(high)))


def draw_splat_params(key, part):
    keys = jax.random.split(key, 8)
    shape = (SPLATS,)
    mean_x = jax.random.uniform(keys[0], shape, jnp.float32, -2.0, 18.0)
    mean_y = jax.random.uniform(keys[1], shape, jnp.float32, -2.0, 18.0)
    conic_a = log_uniform(keys[2], shape, 0.05, 0.5)
    conic_c = log_uniform(keys[3], shape, 0.05, 0.5)
    conic_b = jax.random.uniform(keys[4], shape, jnp.float32, -0.6, 0.6) * jnp.sqrt(conic_a * conic_c)
    opacity = log_uniform(keys[5], shape, 0.002, 0.02)
    colours = jax.random.uniform(keys[6], (3, SPLATS), jnp.float32)
    depth = log_uniform(keys[7], shape, 0.05, 1.0)
    geometry = jnp.stack([mean_x, mean_y, conic_a, conic_b, conic_c, opacity])
    return jnp.concatenate([geometry, colours, depth[None, :]], axis=0)


def draw_list_length(key, part):
    tile_index = jnp.arange(TILES, dtype=jnp.int32)
    groups = TILES // GROUP_TILES
    group = tile_index // GROUP_TILES
    heavy = jax.random.randint(jax.random.fold_in(key, 11), (), 0, groups)
    is_heavy = group == heavy
    longest = jnp.where(is_heavy, K, 3 * K // 4).astype(jnp.int32)
    shortest = jnp.where(is_heavy, 7 * K // 8, K // 2).astype(jnp.int32)
    lengths = jax.random.randint(jax.random.fold_in(key, 12), (TILES,), shortest, longest + 1)
    return jnp.where(tile_index == heavy * GROUP_TILES, K, lengths).astype(jnp.int32)


def place_ends(array, rng, least, high):
    dims = array.shape
    spot = [jax.random.randint(jax.random.fold_in(rng, axis), (), 0, dims[axis]) for axis in range(len(dims))]
    array = array.at[tuple(spot)].set(least)
    longest = dims.index(max(dims))
    spot[longest] = (spot[longest] + 1) % dims[longest]
    return array.at[tuple(spot)].set(high)


def block_scale(own_key, dims, cuts, low, top_value):
    factor_of = 1.0
    for axis_at, blocks in cuts:
        draws = jax.random.uniform(jax.random.fold_in(jax.random.fold_in(own_key, 6), axis_at), (blocks,), jnp.float32, low / len(cuts), top_value / len(cuts))
        factor_of = factor_of * jnp.repeat(jnp.exp(draws), dims[axis_at] // blocks).reshape((-1,) + (1,) * (len(dims) - 1 - axis_at))
    return factor_of


def shared_out(rng, own, number, rows, count, top, most, lean):
    order = jax.random.permutation(rng, count)
    crowded, common = shares(count, rows * top, most, lean, True), shares(count, rows * top, most, lean, False)
    places = jnp.arange(count)

    def named(sizes, turn):
        used = int((sizes > 0).sum())
        fixed = max(1, used // 4)
        moved = fixed + (places - fixed + turn * (used - fixed)) % max(1, count - fixed)
        return jnp.zeros((count,), jnp.int32).at[order[jnp.where(places < fixed, places, moved)]].set(jnp.asarray(sizes, jnp.int32))

    sizes = jnp.where(number % 4 == 0, named(crowded, number // 4), named(common, number - number // 4 - 1))
    mixed = jax.random.permutation(jax.random.fold_in(own, 3), count)
    source_of, receiver = mixed[0:count // 2 * 2:2], mixed[1:count // 2 * 2:2]
    slack = jnp.minimum(sizes[source_of] - 1, most - sizes[receiver]) // 2
    slack = jnp.where((source_of == order[0]) | (receiver == order[0]) | (sizes[receiver] == 0), 0, jnp.maximum(slack, 0))
    moved = jax.random.randint(jax.random.fold_in(own, 4), (count // 2,), 0, 1 << 20) % (slack + 1)
    sizes = sizes.at[source_of].add(-moved).at[receiver].add(moved)
    labels = jnp.searchsorted(jnp.cumsum(sizes), jnp.arange(rows * top), side="right").astype(jnp.int32)
    table = labels.reshape(top, rows).T
    table = table[jax.random.permutation(jax.random.fold_in(own, 1), rows)]
    turn = jax.random.randint(jax.random.fold_in(own, 2), (rows, 1), 0, top)
    return jnp.take_along_axis(table, (jnp.arange(top)[None, :] + turn) % top, axis=1)


def shares(amount, total, most, skew, full):
    loads = [(1 << 20) // math.isqrt(standing ** skew) + 1 for standing in range(1, amount + 1)]
    largest = most if full else min(most, max(-(-total // amount), total * loads[0] // sum(loads)))
    least = 1 if total - largest >= amount - 1 else 0
    counts, rest = [largest] + [least] * (amount - 1), total - largest - least * (amount - 1)
    while rest > 0:
        free = [i for i in range(1, amount) if counts[i] < largest] or [i for i in range(1, amount) if counts[i] < most]
        whole, left = sum([loads[i] for i in free]), rest
        for i in free:
            extra = min(most - counts[i], max(1, left * loads[i] // whole), rest)
            counts[i] = counts[i] + extra
            rest = rest - extra
    return np.array(counts)


def setup_inputs(seed: int = 0) -> dict:
    seeds = jax.random.split(jax.random.key(seed), 6)
    splat_params = draw_splat_params(jax.random.fold_in(seeds[5], 71), 0)
    list_owner_keys = jax.random.split(jax.random.fold_in(seeds[1], 1), TILES * K // (TILE_DEV * K))
    list_owner_turns = jax.random.permutation(jax.random.fold_in(seeds[1], 3), TILES * K // (TILE_DEV * K))
    list_owner = jax.vmap(lambda own, number: shared_out(jax.random.fold_in(seeds[1], 2), own, number, TILE_DEV * K, DEVICES, 1, CAP, 2))(list_owner_keys, list_owner_turns).reshape((TILES, K, 1))
    list_slot = place_ends(jax.random.randint(seeds[2], (TILES, K), 0, G_DEV), jax.random.fold_in(seeds[2], 1), 0, G_DEV - 1).astype(jnp.int32)
    list_length = draw_list_length(jax.random.fold_in(seeds[5], 71), 0)
    target = jnp.clip(1.0 * jax.random.uniform(seeds[4], (4, TILES, PIX), jnp.float32) ** block_scale(seeds[4], (4, TILES, PIX), ((1, 128),), -0.2, 0.2), 0.0, 1.0)
    return dict(splat_params=splat_params, list_owner=list_owner, list_slot=list_slot, list_length=list_length, target=target)


precise = lax.Precision.HIGHEST


def render_tile(values, length, tile_target):
    pixel_index = jnp.arange(PIX)
    pixel_x = (pixel_index % SIDE).astype(jnp.float32) + 0.5
    pixel_y = (pixel_index // SIDE).astype(jnp.float32) + 0.5
    live_mask = (jnp.arange(K) < length).astype(jnp.float32)
    mean_x = values[0]
    mean_y = values[1]
    conic_a = values[2]
    conic_b = values[3]
    conic_c = values[4]
    opacity = values[5] * live_mask
    colours = values[6:10]
    offset_x = pixel_x[:, None] - mean_x[None, :]
    offset_y = pixel_y[:, None] - mean_y[None, :]
    exponent = 0.5 * (conic_a * offset_x * offset_x + conic_c * offset_y * offset_y) + conic_b * offset_x * offset_y
    falloff = jnp.exp(-exponent)
    alphas = opacity[None, :] * falloff
    log_keep = jnp.log1p(-alphas)
    log_trans = jnp.cumsum(log_keep, axis=1) - log_keep
    transmit = jnp.exp(log_trans)
    weight = alphas * transmit
    rendered = jnp.dot(colours, weight.T, precision=precise)
    grad_image = 2.0 * (rendered - tile_target)
    grad_colours = jnp.dot(grad_image, weight, precision=precise)
    shading = jnp.dot(grad_image.T, colours, precision=precise)
    spent_sum = weight * shading
    before = jnp.cumsum(spent_sum, axis=1)
    grand_total = jnp.sum(grad_image * rendered, axis=0)
    grad_alpha = transmit * shading - (grand_total[:, None] - before) / (1.0 - alphas)
    grad_power = -grad_alpha * alphas
    grad_mean_x = jnp.sum(-grad_power * (conic_a * offset_x + conic_b * offset_y), axis=0)
    grad_mean_y = jnp.sum(-grad_power * (conic_c * offset_y + conic_b * offset_x), axis=0)
    grad_a = jnp.sum(grad_power * 0.5 * offset_x * offset_x, axis=0)
    grad_b = jnp.sum(grad_power * offset_x * offset_y, axis=0)
    grad_c = jnp.sum(grad_power * 0.5 * offset_y * offset_y, axis=0)
    grad_opacity = jnp.sum(grad_alpha * falloff, axis=0) * live_mask
    geometry_grads = jnp.stack([grad_mean_x, grad_mean_y, grad_a, grad_b, grad_c, grad_opacity])
    return rendered, jnp.concatenate([geometry_grads, grad_colours], axis=0)


def reference(splat_params, list_owner, list_slot, list_length, target):
    splat_ids = (list_owner[:, :, 0] * G_DEV + list_slot).astype(jnp.int32)

    def render_one(tile_step):
        values = jnp.take(splat_params, splat_ids[tile_step], axis=1)
        return render_tile(values, list_length[tile_step], target[:, tile_step, :])

    images, entry_grads = lax.map(render_one, jnp.arange(TILES, dtype=jnp.int32))
    rendered = jnp.transpose(images, (1, 0, 2))
    flat_grads = jnp.transpose(entry_grads, (1, 0, 2)).reshape(10, TILES * K)
    splat_grads = jnp.zeros((10, SPLATS), jnp.float32).at[:, splat_ids.reshape(-1)].add(flat_grads)
    return rendered, splat_grads
```

```python
import jax
import jax.numpy as jnp
from jax import lax
from jax.experimental import pallas as pl
from jax.experimental.pallas import tpu as pltpu
from jax.sharding import PartitionSpec as P

AXES = ("row", "col")
DEVS = 128
RANKS = 64
TILES = 4
SEGS = 128
STEPS = 8
ROWS = TILES * STEPS
WIRE = 5
LOG2E = 1.4426950408889634
F32 = jnp.float32
BF16 = jnp.bfloat16


def iota(shape, dim):
    return lax.broadcasted_iota(jnp.int32, shape, dim)


def dot(a, b):
    return lax.dot_general(a, b, (((1,), (0,)), ((), ())), preferred_element_type=F32)


def dot_nt(a, b):
    return lax.dot_general(a, b, (((1,), (1,)), ((), ())), preferred_element_type=F32)


def split(x, parts):
    out = []
    for _ in range(parts - 1):
        head = x.astype(BF16)
        out.append(head)
        x = x - head.astype(F32)
    out.append(x.astype(BF16))
    return out


def onehot_rows(row, count):
    wide = jnp.broadcast_to(row, (count, row.shape[1]))
    return wide == iota(wide.shape, 0).astype(F32)


def route_kernel(length_ref, owner_ref, slot_ref, request_ref, owner_out, rank_out):
    lane = iota((STEPS, SEGS), 1)
    step = iota((STEPS, SEGS), 0)
    picks = (lane & (STEPS - 1)) == step
    pieces = []
    for r in range(STEPS):
        rows = []
        slot_rows = []
        for t in range(TILES):
            own = jnp.broadcast_to(owner_ref[t * STEPS + r : t * STEPS + r + 1, :], (STEPS, SEGS))
            rows.append(jnp.where(picks, own, 0))
            slot = slot_ref[t : t + 1, r * SEGS : (r + 1) * SEGS]
            slot_rows.append(jnp.where(picks, jnp.broadcast_to(slot, (STEPS, SEGS)), 0))
        rows += [s >> 8 for s in slot_rows] + [s & 255 for s in slot_rows]
        pieces.append(jnp.concatenate(rows, axis=0).astype(F32).astype(BF16))
    spread = jnp.concatenate(pieces, axis=1)
    place = ((iota((STEPS * SEGS, SEGS), 0) >> 3) == iota((STEPS * SEGS, SEGS), 1)).astype(F32)
    moved = dot(spread, place.astype(BF16))
    lane = iota((ROWS, SEGS), 1)
    row = iota((ROWS, SEGS), 0)
    length = jnp.full((ROWS, SEGS), length_ref[0], jnp.int32)
    for t in range(1, TILES):
        length = jnp.where((row >> 3) == t, length_ref[t], length)
    live = (lane * STEPS + (row & (STEPS - 1))) < length
    owners = jnp.where(live, moved[0:ROWS], -1.0)
    high = moved[ROWS : 2 * ROWS]
    low = moved[2 * ROWS : 3 * ROWS]
    owner_out[...] = owners
    before = (iota((256, 256), 0) < iota((256, 256), 1)).astype(F32).astype(BF16)
    before = jnp.concatenate([before, jnp.ones((256, 256), BF16)], axis=1)
    rank_of = (iota((2 * RANKS, 256), 0) & (RANKS - 1)).astype(F32)
    upper = iota((2 * RANKS, 256), 0) < RANKS
    carry = jnp.zeros((DEVS, 256), F32)
    request = jnp.zeros((2 * RANKS, DEVS), F32)
    for n in range(ROWS // 2):
        pair = lambda x: jnp.concatenate([x[2 * n : 2 * n + 1], x[2 * n + 1 : 2 * n + 2]], axis=1)
        hot = onehot_rows(pair(owners), DEVS)
        hot16 = hot.astype(F32).astype(BF16)
        counted = dot(hot16, before)
        rank = jnp.sum(jnp.where(hot, counted[:, :256] + carry, 0.0), axis=0, keepdims=True)
        carry = carry + counted[:, 256:]
        rank_out[2 * n : 2 * n + 1, :] = rank[:, :SEGS]
        rank_out[2 * n + 1 : 2 * n + 2, :] = rank[:, SEGS:]
        values = jnp.where(upper, pair(high), pair(low))
        values = jnp.where(rank_of == rank, values, 0.0)
        request = request + dot_nt(values.astype(BF16), hot16)
    slots = request[:RANKS] * 256.0 + request[RANKS:]
    slots = jnp.concatenate([slots, slots], axis=0).T
    full = jnp.where(iota((DEVS, DEVS), 1) < RANKS, slots, carry[:, :DEVS])
    request_ref[...] = full.astype(jnp.int32)


def gather_kernel(asked_ref, params_ref, out_ref, held_ref):
    lane8 = iota((8, 128), 1)
    lane2 = iota((2, 128), 1)
    left = iota((WIRE, 128), 1) < RANKS

    def pair(j, carry):
        held_ref[...] = jnp.zeros((16, 128), F32)
        for side in range(2):
            src = 2 * j + side
            count = asked_ref[src, RANKS]
            for chunk in range(RANKS // 8):

                @pl.when(count > chunk * 8)
                def _():
                    top = jnp.zeros((8, 128), F32)
                    low = jnp.zeros((2, 128), F32)
                    for i in range(8):
                        rank = chunk * 8 + i
                        spot = side * RANKS + rank
                        slot = asked_ref[src, rank]
                        base = pl.multiple_of((slot >> 7) << 7, 128)
                        turn = (spot - slot) & 127
                        a = pltpu.roll(params_ref[0:8, pl.ds(base, 128)], turn, 1)
                        b = pltpu.roll(params_ref[8:10, pl.ds(base, 128)], turn, 1)
                        top = jnp.where(lane8 == spot, a, top)
                        low = jnp.where(lane2 == spot, b, low)
                    held_ref[0:8, :] += top
                    held_ref[8:10, :] += low

        first = held_ref[0:WIRE, :]
        second = held_ref[WIRE : 2 * WIRE, :]
        even = jnp.where(left, first, pltpu.roll(second, RANKS, 1))
        odd = jnp.where(left, pltpu.roll(first, RANKS, 1), second)
        out_ref[pl.ds(j * 2 * WIRE, 2 * WIRE), :] = jnp.concatenate([even, odd], axis=0)
        return carry

    lax.fori_loop(0, DEVS // 2, pair, 0)


CHAINS = 4


def scatter_kernel(asked_ref, wire_ref, out_ref, held_ref, *more):
    totals = (out_ref,) + more
    left = iota((WIRE, 128), 1) < RANKS
    lane8 = iota((8, 128), 1)
    lane2 = iota((2, 128), 1)
    width = 1024

    def clear(i, carry):
        at = pl.ds(pl.multiple_of(i * width, width), width)
        for ref in totals:
            ref[:, at] = jnp.zeros((10, width), F32)
        return carry

    lax.fori_loop(0, out_ref.shape[1] // width, clear, 0)

    def pair(j, carry):
        both = wire_ref[pl.ds(j * 2 * WIRE, 2 * WIRE), :]
        even = both[:WIRE]
        odd = both[WIRE:]
        held_ref[0:WIRE, :] = jnp.where(left, even, pltpu.roll(odd, RANKS, 1))
        held_ref[WIRE : 2 * WIRE, :] = jnp.where(left, pltpu.roll(even, RANKS, 1), odd)
        for side in range(2):
            src = 2 * j + side
            count = asked_ref[src, RANKS]
            for chunk in range(RANKS // 8):

                @pl.when(count > chunk * 8)
                def _():
                    top = held_ref[0:8, :]
                    low = held_ref[8:10, :]
                    for group in range(8 // CHAINS):
                        news = []
                        for i in range(CHAINS):
                            rank = chunk * 8 + group * CHAINS + i
                            spot = side * RANKS + rank
                            slot = asked_ref[src, rank]
                            base = pl.multiple_of((slot >> 7) << 7, 128)
                            at = slot & 127
                            turn = (slot - spot) & 127
                            a = jnp.where(lane8 == at, pltpu.roll(top, turn, 1), 0.0)
                            b = jnp.where(lane2 == at, pltpu.roll(low, turn, 1), 0.0)
                            news.append((base, a, b))
                        olds = [
                            (ref[0:8, pl.ds(base, 128)], ref[8:10, pl.ds(base, 128)])
                            for ref, (base, a, b) in zip(totals, news)
                        ]
                        for ref, (base, a, b), (old_a, old_b) in zip(totals, news, olds):
                            ref[0:8, pl.ds(base, 128)] = old_a + a
                            ref[8:10, pl.ds(base, 128)] = old_b + b

        return carry

    lax.fori_loop(0, DEVS // 2, pair, 0)

    def close(i, carry):
        at = pl.ds(pl.multiple_of(i * width, width), width)
        total = out_ref[:, at]
        for ref in more:
            total = total + ref[:, at]
        out_ref[:, at] = total
        return carry

    lax.fori_loop(0, out_ref.shape[1] // width, close, 0)


def render_kernel(
    wire_ref, owner_ref, rank_ref, target_ref, image_ref, out_ref,
    hot_ref, left_ref, value_ref, fall_ref, flow_ref, sum_ref, keep_ref, reach_ref, behind_ref,
    shade_ref, column_ref, picture_ref, across_ref, tilt_ref, grad_ref, spread_ref,
):
    for c in range(WIRE):
        block = wire_ref[pl.ds(c, DEVS, stride=WIRE), :].T
        parts = split(block, 3)
        left_ref[c * 128 : (c + 1) * 128, :] = jnp.concatenate(parts, axis=1)
    rank_of = iota((RANKS, 256), 0).astype(F32)

    def fetch(n, carry):
        at = pl.ds(pl.multiple_of(n * 256, 256), 256)
        owner = jnp.concatenate([owner_ref[pl.ds(2 * n, 1), :], owner_ref[pl.ds(2 * n + 1, 1), :]], axis=1)
        rank = jnp.concatenate([rank_ref[pl.ds(2 * n, 1), :], rank_ref[pl.ds(2 * n + 1, 1), :]], axis=1)
        hot = onehot_rows(owner, DEVS).astype(F32).astype(BF16)
        hot_ref[:, at] = hot
        mine = rank_of == rank
        found = dot(left_ref[...], jnp.concatenate([hot, hot, hot], axis=0))
        for c in range(WIRE):
            for h in range(2):
                block = found[c * 128 + h * RANKS : c * 128 + (h + 1) * RANKS]
                got = jnp.sum(jnp.where(mine, block, 0.0), axis=0, keepdims=True)
                v = c + WIRE * h
                value_ref[v, pl.ds(2 * n, 1), :] = got[:, :SEGS]
                value_ref[v, pl.ds(2 * n + 1, 1), :] = got[:, SEGS:]
        return carry

    lax.fori_loop(0, ROWS // 2, fetch, 0)

    flat = jnp.concatenate([target_ref[ch] for ch in range(4)] + [jnp.zeros((112, 256), F32)], axis=0)
    column_ref[...] = jnp.concatenate([flat[:, :128].T, flat[:, 128:].T], axis=0)
    picture_ref[...] = jnp.zeros((256, 128), F32)
    earlier = (iota((128, 128), 0) < iota((128, 128), 1)).astype(F32).astype(BF16)
    later = (iota((128, 128), 0) > iota((128, 128), 1)).astype(F32).astype(BF16)
    ones = jnp.ones((256, 128), BF16)
    earlier = jnp.concatenate([earlier, earlier, earlier], axis=0)
    later = jnp.concatenate([later, later], axis=0)
    pixel_x = iota((16, SEGS), 0).astype(F32) + 0.5

    def tile(t, carry):
        first = t * STEPS
        for k in range(STEPS):
            value = lambda v: value_ref[v, pl.ds(first + k, 1), :]
            offset_x = pixel_x - value(0)
            across_ref[k] = (-0.5 * LOG2E) * value(2) * offset_x * offset_x
            tilt_ref[k] = -LOG2E * value(3) * offset_x

        def forward(n, carry):
            for half in range(2):
                y = 2 * n + half
                pixel_y = y.astype(F32) + 0.5
                keep = jnp.ones((16, SEGS), F32)
                sums = [jnp.zeros((16, SEGS), F32) for _ in range(4)]
                at = pl.ds(pl.multiple_of(y * 16, 16), 16)
                for k in range(STEPS):
                    value = lambda v: value_ref[v, pl.ds(first + k, 1), :]
                    offset_y = pixel_y - value(1)
                    down = (-0.5 * LOG2E) * value(4) * offset_y * offset_y
                    fall = jnp.exp2(across_ref[k] + down + tilt_ref[k] * offset_y)
                    flow = fall * keep
                    weight = value(5) * flow
                    keep = keep - weight
                    for ch in range(4):
                        sums[ch] = sums[ch] + value(6 + ch) * weight
                    fall_ref[k, at, :] = fall
                    flow_ref[k, at, :] = flow
                keep_ref[at, :] = keep
                for ch in range(4):
                    sum_ref[ch, at, :] = sums[ch]
            return carry

        lax.fori_loop(0, 8, forward, 0)

        keep = keep_ref[...]
        logs = jnp.concatenate(split(jnp.log(keep), 3), axis=1)
        reach = jnp.exp(dot(logs, earlier))
        reach_ref[...] = reach
        spent = jnp.zeros((256, SEGS), F32)
        for ch in range(4):
            part = sum_ref[ch] * reach
            rendered = dot(jnp.concatenate(split(part, 2), axis=1), ones)
            here = iota((256, 128), 1) == ch * TILES + t
            wanted = jnp.sum(jnp.where(here, column_ref[...], 0.0), axis=1, keepdims=True)
            shade = 2.0 * (rendered - wanted)
            picture_ref[...] = jnp.where(here, rendered, picture_ref[...])
            shade_ref[ch] = shade
            spent = spent + shade * part
        rest = dot(jnp.concatenate(split(spent, 2), axis=1), later)
        behind_ref[...] = rest / (reach * keep)

        for k in reversed(range(STEPS)):
            value = lambda v: value_ref[v, pl.ds(first + k, 1), :]
            mean_y = jnp.broadcast_to(value(1), (8, SEGS))
            opacity = jnp.broadcast_to(value(5), (8, SEGS))
            colours = [jnp.broadcast_to(value(6 + ch), (8, SEGS)) for ch in range(4)]

            def backward(n, sums):
                zero, one, two, tints = sums
                zero, one, two, tints = list(zero), list(one), list(two), list(tints)
                for quarter in range(2):
                    y = 2 * n + quarter
                    offset_y = y.astype(F32) + 0.5 - mean_y
                    for half in range(2):
                        at = pl.ds(pl.multiple_of(y * 16 + half * 8, 8), 8)
                        shades = [shade_ref[ch, at, :] for ch in range(4)]
                        flow = flow_ref[k, at, :] * reach_ref[at, :]
                        lit = (shades[0] * colours[0] + shades[1] * colours[1]) + (
                            shades[2] * colours[2] + shades[3] * colours[3]
                        )
                        behind = behind_ref[at, :]
                        gap = lit - behind
                        behind_ref[at, :] = behind + opacity * fall_ref[k, at, :] * gap
                        grad = flow * gap
                        slope = grad * offset_y
                        zero[half] = zero[half] + grad
                        one[half] = one[half] + slope
                        two[half] = two[half] + slope * offset_y
                        for ch in range(4):
                            tints[ch] = tints[ch] + flow * shades[ch]
                return (tuple(zero), tuple(one), tuple(two), tuple(tints))

            blank = jnp.zeros((8, SEGS), F32)
            zero, one, two, tints = lax.fori_loop(
                0, 8, backward, ((blank,) * 2, (blank,) * 2, (blank,) * 2, (blank,) * 4)
            )
            total = lambda x: jnp.sum(x, axis=0, keepdims=True)
            offset_x = pixel_x - value(0)
            near, far = offset_x[:8], offset_x[8:]
            sum_0 = total(zero[0] + zero[1])
            slope_x = (near * zero[0], far * zero[1])
            sum_x = total(slope_x[0] + slope_x[1])
            sum_xx = total(near * slope_x[0] + far * slope_x[1])
            sum_y = total(one[0] + one[1])
            sum_xy = total(near * one[0] + far * one[1])
            sum_yy = total(two[0] + two[1])
            opacity = value(5)
            grads = [
                opacity * (value(2) * sum_x + value(3) * sum_y),
                opacity * (value(4) * sum_y + value(3) * sum_x),
                -0.5 * opacity * sum_xx,
                -opacity * sum_xy,
                -0.5 * opacity * sum_yy,
                sum_0,
            ] + [opacity * total(tint) for tint in tints]
            for v in range(10):
                grad_ref[v, pl.ds(first + k, 1), :] = grads[v]
        return carry

    lax.fori_loop(0, TILES, tile, 0)

    picture = picture_ref[...]
    picture = jnp.concatenate([picture[:128].T, picture[128:].T], axis=1)
    for ch in range(4):
        image_ref[ch] = picture[ch * TILES : (ch + 1) * TILES, :]

    spread_ref[...] = jnp.zeros((WIRE * 128, DEVS), F32)

    def spread(n, carry):
        at = pl.ds(pl.multiple_of(n * 256, 256), 256)
        rank = jnp.concatenate([rank_ref[pl.ds(2 * n, 1), :], rank_ref[pl.ds(2 * n + 1, 1), :]], axis=1)
        mine = rank_of == rank
        hot = hot_ref[:, at]
        rows = []
        for c in range(WIRE):
            for h in range(2):
                v = c + WIRE * h
                grad = jnp.concatenate(
                    [grad_ref[v, pl.ds(2 * n, 1), :], grad_ref[v, pl.ds(2 * n + 1, 1), :]], axis=1
                )
                rows.append(jnp.where(mine, grad, 0.0))
        heads, tails = split(jnp.concatenate(rows, axis=0), 2)
        spread_ref[...] += dot_nt(
            jnp.concatenate([heads, tails], axis=1), jnp.concatenate([hot, hot], axis=1)
        )
        return carry

    lax.fori_loop(0, ROWS // 2, spread, 0)
    for c in range(WIRE):
        out_ref[pl.ds(c, DEVS, stride=WIRE), :] = spread_ref[c * 128 : (c + 1) * 128, :].T


def vmem():
    return pl.BlockSpec(memory_space=pltpu.VMEM)


def smem():
    return pl.BlockSpec(memory_space=pltpu.SMEM)


def call(kernel, name, in_specs, outs, scratch, limit):
    return pl.pallas_call(
        kernel,
        name=name,
        out_shape=outs,
        in_specs=in_specs,
        out_specs=jax.tree.map(lambda _: vmem(), outs),
        scratch_shapes=scratch,
        compiler_params=pltpu.CompilerParams(vmem_limit_bytes=limit),
    )


def exchange(x):
    width = x.shape[0] * x.shape[1] // DEVS
    moved = lax.all_to_all(x.reshape(DEVS, 1, width), AXES, split_axis=0, concat_axis=0, tiled=True)
    return moved.reshape(x.shape)


def body(splat_params, list_owner, list_slot, list_length, target):
    shape = jax.ShapeDtypeStruct
    wire = shape((DEVS * WIRE, 128), F32)
    route = call(
        route_kernel, "route", [smem(), vmem(), vmem()],
        (shape((DEVS, 128), jnp.int32), shape((ROWS, SEGS), F32), shape((ROWS, SEGS), F32)), [], 32 << 20,
    )
    request, owners, ranks = route(list_length, list_owner.reshape(ROWS, SEGS), list_slot)
    asked = exchange(request)
    gather = call(gather_kernel, "gather", [smem(), vmem()], wire, [pltpu.VMEM((16, 128), F32)], 32 << 20)
    replies = exchange(gather(asked, splat_params))
    field = pltpu.VMEM((256, SEGS), F32)
    deep = pltpu.VMEM((STEPS, 256, SEGS), F32)
    render = call(
        render_kernel, "render", [vmem()] * 4, (shape(target.shape, F32), wire),
        [
            pltpu.VMEM((DEVS, ROWS * SEGS), BF16), pltpu.VMEM((WIRE * 128, 384), BF16),
            pltpu.VMEM((10, ROWS, SEGS), F32), deep, deep, pltpu.VMEM((4, 256, SEGS), F32), field, field, field,
            pltpu.VMEM((4, 256, SEGS), F32), field, field,
            pltpu.VMEM((STEPS, 16, SEGS), F32), pltpu.VMEM((STEPS, 16, SEGS), F32),
            pltpu.VMEM((10, ROWS, SEGS), F32), pltpu.VMEM((WIRE * 128, DEVS), F32),
        ],
        40 << 20,
    )
    images, outgoing = render(replies, owners, ranks, target)
    incoming = exchange(outgoing)
    scatter = call(
        scatter_kernel, "scatter", [smem(), vmem()], shape(splat_params.shape, F32),
        [pltpu.VMEM((16, 128), F32)] + [pltpu.VMEM(splat_params.shape, F32)] * (CHAINS - 1), 48 << 20,
    )
    return (images, scatter(asked, incoming))


def solution(mesh):
    in_specs = (
        P(None, AXES),
        P(AXES, None, None),
        P(AXES, None),
        P(AXES),
        P(None, AXES, None),
    )
    out_specs = (P(None, AXES, None), P(None, AXES))
    return jax.shard_map(body, mesh=mesh, in_specs=in_specs, out_specs=out_specs, check_vma=False)
```

```python
import jax
import jax.numpy as jnp
from jax import lax
from jax.experimental import pallas as pl
from jax.experimental.pallas import tpu as pltpu
from jax.sharding import PartitionSpec as P

AXES = ("row", "col")
DEVS = 128
RANKS = 64
TILES = 4
SEGS = 128
STEPS = 8
ROWS = TILES * STEPS
WIRE = 5
GROUP = 16
BLOCK = 16
CHUNK = 16
CHAINS = 4
LOG2E = 1.4426950408889634
F32 = jnp.float32
BF16 = jnp.bfloat16


def iota(shape, dim):
    return lax.broadcasted_iota(jnp.int32, shape, dim)


def dot(a, b):
    return lax.dot_general(a, b, (((1,), (0,)), ((), ())), preferred_element_type=F32)


def dot_nt(a, b):
    return lax.dot_general(a, b, (((1,), (1,)), ((), ())), preferred_element_type=F32)


def split(x, parts):
    out = []
    for _ in range(parts - 1):
        head = x.astype(BF16)
        out.append(head)
        x = x - head.astype(F32)
    out.append(x.astype(BF16))
    return out


def onehot_rows(row, count):
    wide = jnp.broadcast_to(row, (count, row.shape[1]))
    return wide == iota(wide.shape, 0).astype(F32)


def route_kernel(length_ref, owner_ref, slot_ref, request_ref, owner_out, rank_out):
    lane = iota((STEPS, SEGS), 1)
    step = iota((STEPS, SEGS), 0)
    picks = (lane & (STEPS - 1)) == step
    pieces = []
    for r in range(STEPS):
        rows = []
        slot_rows = []
        for t in range(TILES):
            own = jnp.broadcast_to(owner_ref[t * STEPS + r : t * STEPS + r + 1, :], (STEPS, SEGS))
            rows.append(jnp.where(picks, own, 0))
            slot = slot_ref[t : t + 1, r * SEGS : (r + 1) * SEGS]
            slot_rows.append(jnp.where(picks, jnp.broadcast_to(slot, (STEPS, SEGS)), 0))
        rows += [s >> 8 for s in slot_rows] + [s & 255 for s in slot_rows]
        pieces.append(jnp.concatenate(rows, axis=0).astype(F32).astype(BF16))
    spread = jnp.concatenate(pieces, axis=1)
    place = ((iota((STEPS * SEGS, SEGS), 0) >> 3) == iota((STEPS * SEGS, SEGS), 1)).astype(F32)
    moved = dot(spread, place.astype(BF16))
    lane = iota((ROWS, SEGS), 1)
    row = iota((ROWS, SEGS), 0)
    length = jnp.full((ROWS, SEGS), length_ref[0], jnp.int32)
    for t in range(1, TILES):
        length = jnp.where((row >> 3) == t, length_ref[t], length)
    live = (lane * STEPS + (row & (STEPS - 1))) < length
    owners = jnp.where(live, moved[0:ROWS], -1.0)
    high = moved[ROWS : 2 * ROWS]
    low = moved[2 * ROWS : 3 * ROWS]
    owner_out[...] = owners
    before = (iota((256, 256), 0) < iota((256, 256), 1)).astype(F32).astype(BF16)
    before = jnp.concatenate([before, jnp.ones((256, 256), BF16)], axis=1)
    rank_of = (iota((2 * RANKS, 256), 0) & (RANKS - 1)).astype(F32)
    upper = iota((2 * RANKS, 256), 0) < RANKS
    carry = jnp.zeros((DEVS, 256), F32)
    request = jnp.zeros((2 * RANKS, DEVS), F32)
    for n in range(ROWS // 2):
        pair = lambda x: jnp.concatenate([x[2 * n : 2 * n + 1], x[2 * n + 1 : 2 * n + 2]], axis=1)
        hot = onehot_rows(pair(owners), DEVS)
        hot16 = hot.astype(F32).astype(BF16)
        counted = dot(hot16, before)
        rank = jnp.sum(jnp.where(hot, counted[:, :256] + carry, 0.0), axis=0, keepdims=True)
        carry = carry + counted[:, 256:]
        rank_out[2 * n : 2 * n + 1, :] = rank[:, :SEGS]
        rank_out[2 * n + 1 : 2 * n + 2, :] = rank[:, SEGS:]
        values = jnp.where(upper, pair(high), pair(low))
        values = jnp.where(rank_of == rank, values, 0.0)
        request = request + dot_nt(values.astype(BF16), hot16)
    slots = request[:RANKS] * 256.0 + request[RANKS:]
    slots = jnp.concatenate([slots, slots], axis=0).T
    full = jnp.where(iota((DEVS, DEVS), 1) < RANKS, slots, carry[:, :DEVS])
    request_ref[...] = full.astype(jnp.int32)


def pack_kernel(*refs):
    out_ref = refs[-1]
    pad = jnp.zeros((GROUP - 10, 128), F32)
    for n in range(refs[0].shape[1] // 128):
        blocks = []
        for ref in refs[:-1]:
            blocks += [ref[:, n * 128 : (n + 1) * 128], pad]
        out_ref[n * 128 : (n + 1) * 128, :] = jnp.concatenate(blocks, axis=0).T


def lane_groups(asked, table_rows):
    return lax.div(asked, table_rows).astype(F32).T[:RANKS].astype(BF16)


def group_of_lane():
    return iota((RANKS, 128), 1) >> 4


def everywhere(x):
    x = x + pltpu.roll(x, 64, 1)
    x = x + pltpu.roll(x, 32, 1)
    return x + pltpu.roll(x, 16, 1)


def sources_to_lanes(groups, block):
    source = iota((DEVS, BLOCK * 128), 0)
    wanted = block * BLOCK + (iota((DEVS, BLOCK * 128), 1) >> 7)
    return dot(groups, (source == wanted).astype(F32).astype(BF16)).astype(jnp.int32)


def gather_kernel(asked_ref, asked_vec_ref, table_ref, out_ref, group_ref, row_ref):
    left = iota((WIRE, 128), 1) < RANKS
    mask = table_ref.shape[0] - 1
    group_ref[...] = lane_groups(asked_vec_ref[...], table_ref.shape[0])
    row_ref[...] = jnp.zeros(row_ref.shape, F32)

    def block(b, carry):
        def source(q, carry):
            src = b * BLOCK + q
            count = asked_ref[src, RANKS]
            for chunk in range(RANKS // CHUNK):

                @pl.when(count > chunk * CHUNK)
                def _():
                    for i in range(CHUNK):
                        rank = chunk * CHUNK + i
                        row = asked_ref[src, rank] & mask
                        row_ref[pl.ds(q * RANKS + rank, 1), :] = table_ref[pl.ds(row, 1), :]

            return carry

        lax.fori_loop(0, BLOCK, source, 0)
        groups = sources_to_lanes(group_ref[...], b)
        halves = []
        for half in range(2):
            merged = jnp.zeros((RANKS, 128), F32)
            for q in range(8):
                n = half * 8 + q
                rows = row_ref[n * RANKS : (n + 1) * RANKS, :]
                rows = jnp.where(group_of_lane() == groups[:, n * 128 : (n + 1) * 128], rows, 0.0)
                merged = jnp.where(group_of_lane() == q, everywhere(rows), merged)
            halves.append(merged)
        turned = jnp.concatenate(halves, axis=0).T
        evens, odds = [], []
        for q in range(8):
            first = turned[q * GROUP : q * GROUP + WIRE]
            second = turned[q * GROUP + WIRE : q * GROUP + 2 * WIRE]
            evens.append(jnp.where(left, first, pltpu.roll(second, RANKS, 1)))
            odds.append(jnp.where(left, pltpu.roll(first, RANKS, 1), second))
        at = pl.multiple_of(b * BLOCK * WIRE, 8)
        out_ref[pl.ds(at, BLOCK * WIRE), :] = jnp.concatenate(evens + odds, axis=0)
        return carry

    lax.fori_loop(0, DEVS // BLOCK, block, 0)


def scatter_kernel(asked_ref, asked_vec_ref, wire_ref, out_ref, group_ref, row_ref, turn_ref, *totals):
    left = iota((WIRE, 128), 1) < RANKS
    table_rows = totals[0].shape[0]
    mask = table_rows - 1
    group_ref[...] = lane_groups(asked_vec_ref[...], table_rows)
    turn_ref[...] = jnp.zeros((128, 128), F32)

    def clear(i, carry):
        for ref in totals:
            ref[pl.ds(pl.multiple_of(i * 128, 128), 128), :] = jnp.zeros((128, 128), F32)
        return carry

    lax.fori_loop(0, table_rows // 128, clear, 0)

    def block(b, carry):
        at = pl.multiple_of(b * BLOCK * WIRE, 8)
        wire = wire_ref[pl.ds(at, BLOCK * WIRE), :]
        for q in range(8):
            even = wire[q * WIRE : (q + 1) * WIRE]
            odd = wire[(q + 8) * WIRE : (q + 9) * WIRE]
            turn_ref[q * GROUP : q * GROUP + WIRE, :] = jnp.where(left, even, pltpu.roll(odd, RANKS, 1))
            turn_ref[q * GROUP + WIRE : q * GROUP + 2 * WIRE, :] = jnp.where(left, pltpu.roll(even, RANKS, 1), odd)
        turned = turn_ref[...].T
        groups = sources_to_lanes(group_ref[...], b)
        for n in range(BLOCK):
            rows = turned[(n // 8) * RANKS : (n // 8 + 1) * RANKS]
            rows = everywhere(jnp.where(group_of_lane() == n % 8, rows, 0.0))
            row_ref[n * RANKS : (n + 1) * RANKS, :] = jnp.where(
                group_of_lane() == groups[:, n * 128 : (n + 1) * 128], rows, 0.0
            )

        def source(q, carry):
            src = b * BLOCK + q
            count = asked_ref[src, RANKS]
            for chunk in range(RANKS // CHUNK):

                @pl.when(count > chunk * CHUNK)
                def _():
                    for turn in range(CHUNK // CHAINS):
                        olds = []
                        for i, ref in enumerate(totals):
                            rank = chunk * CHUNK + turn * CHAINS + i
                            row = asked_ref[src, rank] & mask
                            new = row_ref[pl.ds(q * RANKS + rank, 1), :]
                            olds.append((row, new + ref[pl.ds(row, 1), :]))
                        for ref, (row, total) in zip(totals, olds):
                            ref[pl.ds(row, 1), :] = total

            return carry

        lax.fori_loop(0, BLOCK, source, 0)
        return carry

    lax.fori_loop(0, DEVS // BLOCK, block, 0)

    def close(i, carry):
        at = pl.ds(pl.multiple_of(i * 128, 128), 128)
        total = totals[0][at, :]
        for ref in totals[1:]:
            total = total + ref[at, :]
        total = total.T
        for g in range(8):
            lanes = pl.ds(pl.multiple_of(g * table_rows + i * 128, 128), 128)
            out_ref[:, lanes] = total[g * GROUP : g * GROUP + 10]
        return carry

    lax.fori_loop(0, table_rows // 128, close, 0)


def render_kernel(
    wire_ref, owner_ref, rank_ref, target_ref, image_ref, out_ref,
    hot_ref, left_ref, value_ref, fall_ref, flow_ref, sum_ref, keep_ref, reach_ref, behind_ref,
    shade_ref, column_ref, picture_ref, across_ref, tilt_ref, grad_ref, spread_ref,
):
    for c in range(WIRE):
        block = wire_ref[pl.ds(c, DEVS, stride=WIRE), :].T
        parts = split(block, 3)
        left_ref[c * 128 : (c + 1) * 128, :] = jnp.concatenate(parts, axis=1)
    rank_of = iota((RANKS, 256), 0).astype(F32)

    def fetch(n, carry):
        at = pl.ds(pl.multiple_of(n * 256, 256), 256)
        owner = jnp.concatenate([owner_ref[pl.ds(2 * n, 1), :], owner_ref[pl.ds(2 * n + 1, 1), :]], axis=1)
        rank = jnp.concatenate([rank_ref[pl.ds(2 * n, 1), :], rank_ref[pl.ds(2 * n + 1, 1), :]], axis=1)
        hot = onehot_rows(owner, DEVS).astype(F32).astype(BF16)
        hot_ref[:, at] = hot
        mine = rank_of == rank
        found = dot(left_ref[...], jnp.concatenate([hot, hot, hot], axis=0))
        for c in range(WIRE):
            for h in range(2):
                block = found[c * 128 + h * RANKS : c * 128 + (h + 1) * RANKS]
                got = jnp.sum(jnp.where(mine, block, 0.0), axis=0, keepdims=True)
                v = c + WIRE * h
                value_ref[v, pl.ds(2 * n, 1), :] = got[:, :SEGS]
                value_ref[v, pl.ds(2 * n + 1, 1), :] = got[:, SEGS:]
        return carry

    lax.fori_loop(0, ROWS // 2, fetch, 0)

    flat = jnp.concatenate([target_ref[ch] for ch in range(4)] + [jnp.zeros((112, 256), F32)], axis=0)
    column_ref[...] = jnp.concatenate([flat[:, :128].T, flat[:, 128:].T], axis=0)
    picture_ref[...] = jnp.zeros((256, 128), F32)
    earlier = (iota((128, 128), 0) < iota((128, 128), 1)).astype(F32).astype(BF16)
    later = (iota((128, 128), 0) > iota((128, 128), 1)).astype(F32).astype(BF16)
    ones = jnp.ones((256, 128), BF16)
    earlier = jnp.concatenate([earlier, earlier, earlier], axis=0)
    later = jnp.concatenate([later, later], axis=0)
    pixel_x = iota((16, SEGS), 0).astype(F32) + 0.5

    def tile(t, carry):
        first = t * STEPS
        for k in range(STEPS):
            value = lambda v: value_ref[v, pl.ds(first + k, 1), :]
            offset_x = pixel_x - value(0)
            across_ref[k] = (-0.5 * LOG2E) * value(2) * offset_x * offset_x
            tilt_ref[k] = -LOG2E * value(3) * offset_x

        def forward(n, carry):
            for half in range(2):
                y = 2 * n + half
                pixel_y = y.astype(F32) + 0.5
                keep = jnp.ones((16, SEGS), F32)
                sums = [jnp.zeros((16, SEGS), F32) for _ in range(4)]
                at = pl.ds(pl.multiple_of(y * 16, 16), 16)
                for k in range(STEPS):
                    value = lambda v: value_ref[v, pl.ds(first + k, 1), :]
                    offset_y = pixel_y - value(1)
                    down = (-0.5 * LOG2E) * value(4) * offset_y * offset_y
                    fall = jnp.exp2(across_ref[k] + down + tilt_ref[k] * offset_y)
                    flow = fall * keep
                    weight = value(5) * flow
                    keep = keep - weight
                    for ch in range(4):
                        sums[ch] = sums[ch] + value(6 + ch) * weight
                    fall_ref[k, at, :] = fall
                    flow_ref[k, at, :] = flow
                keep_ref[at, :] = keep
                for ch in range(4):
                    sum_ref[ch, at, :] = sums[ch]
            return carry

        lax.fori_loop(0, 8, forward, 0)

        keep = keep_ref[...]
        logs = jnp.concatenate(split(jnp.log(keep), 3), axis=1)
        reach = jnp.exp(dot(logs, earlier))
        reach_ref[...] = reach
        spent = jnp.zeros((256, SEGS), F32)
        for ch in range(4):
            part = sum_ref[ch] * reach
            rendered = dot(jnp.concatenate(split(part, 2), axis=1), ones)
            here = iota((256, 128), 1) == ch * TILES + t
            wanted = jnp.sum(jnp.where(here, column_ref[...], 0.0), axis=1, keepdims=True)
            shade = 2.0 * (rendered - wanted)
            picture_ref[...] = jnp.where(here, rendered, picture_ref[...])
            shade_ref[ch] = shade
            spent = spent + shade * part
        rest = dot(jnp.concatenate(split(spent, 2), axis=1), later)
        behind_ref[...] = rest / (reach * keep)

        for k in reversed(range(STEPS)):
            value = lambda v: value_ref[v, pl.ds(first + k, 1), :]
            mean_y = jnp.broadcast_to(value(1), (8, SEGS))
            opacity = jnp.broadcast_to(value(5), (8, SEGS))
            colours = [jnp.broadcast_to(value(6 + ch), (8, SEGS)) for ch in range(4)]

            def backward(n, sums):
                zero, one, two, tints = sums
                zero, one, two, tints = list(zero), list(one), list(two), list(tints)
                for quarter in range(2):
                    y = 2 * n + quarter
                    offset_y = y.astype(F32) + 0.5 - mean_y
                    for half in range(2):
                        at = pl.ds(pl.multiple_of(y * 16 + half * 8, 8), 8)
                        shades = [shade_ref[ch, at, :] for ch in range(4)]
                        flow = flow_ref[k, at, :] * reach_ref[at, :]
                        lit = (shades[0] * colours[0] + shades[1] * colours[1]) + (
                            shades[2] * colours[2] + shades[3] * colours[3]
                        )
                        behind = behind_ref[at, :]
                        gap = lit - behind
                        behind_ref[at, :] = behind + opacity * fall_ref[k, at, :] * gap
                        grad = flow * gap
                        slope = grad * offset_y
                        zero[half] = zero[half] + grad
                        one[half] = one[half] + slope
                        two[half] = two[half] + slope * offset_y
                        for ch in range(4):
                            tints[ch] = tints[ch] + flow * shades[ch]
                return (tuple(zero), tuple(one), tuple(two), tuple(tints))

            blank = jnp.zeros((8, SEGS), F32)
            zero, one, two, tints = lax.fori_loop(
                0, 8, backward, ((blank,) * 2, (blank,) * 2, (blank,) * 2, (blank,) * 4)
            )
            total = lambda x: jnp.sum(x, axis=0, keepdims=True)
            offset_x = pixel_x - value(0)
            near, far = offset_x[:8], offset_x[8:]
            sum_0 = total(zero[0] + zero[1])
            slope_x = (near * zero[0], far * zero[1])
            sum_x = total(slope_x[0] + slope_x[1])
            sum_xx = total(near * slope_x[0] + far * slope_x[1])
            sum_y = total(one[0] + one[1])
            sum_xy = total(near * one[0] + far * one[1])
            sum_yy = total(two[0] + two[1])
            opacity = value(5)
            grads = [
                opacity * (value(2) * sum_x + value(3) * sum_y),
                opacity * (value(4) * sum_y + value(3) * sum_x),
                -0.5 * opacity * sum_xx,
                -opacity * sum_xy,
                -0.5 * opacity * sum_yy,
                sum_0,
            ] + [opacity * total(tint) for tint in tints]
            for v in range(10):
                grad_ref[v, pl.ds(first + k, 1), :] = grads[v]
        return carry

    lax.fori_loop(0, TILES, tile, 0)

    picture = picture_ref[...]
    picture = jnp.concatenate([picture[:128].T, picture[128:].T], axis=1)
    for ch in range(4):
        image_ref[ch] = picture[ch * TILES : (ch + 1) * TILES, :]

    spread_ref[...] = jnp.zeros((WIRE * 128, DEVS), F32)

    def spread(n, carry):
        at = pl.ds(pl.multiple_of(n * 256, 256), 256)
        rank = jnp.concatenate([rank_ref[pl.ds(2 * n, 1), :], rank_ref[pl.ds(2 * n + 1, 1), :]], axis=1)
        mine = rank_of == rank
        hot = hot_ref[:, at]
        rows = []
        for c in range(WIRE):
            for h in range(2):
                v = c + WIRE * h
                grad = jnp.concatenate(
                    [grad_ref[v, pl.ds(2 * n, 1), :], grad_ref[v, pl.ds(2 * n + 1, 1), :]], axis=1
                )
                rows.append(jnp.where(mine, grad, 0.0))
        heads, tails = split(jnp.concatenate(rows, axis=0), 2)
        spread_ref[...] += dot_nt(
            jnp.concatenate([heads, tails], axis=1), jnp.concatenate([hot, hot], axis=1)
        )
        return carry

    lax.fori_loop(0, ROWS // 2, spread, 0)
    for c in range(WIRE):
        out_ref[pl.ds(c, DEVS, stride=WIRE), :] = spread_ref[c * 128 : (c + 1) * 128, :].T


def vmem():
    return pl.BlockSpec(memory_space=pltpu.VMEM)


def smem():
    return pl.BlockSpec(memory_space=pltpu.SMEM)


def call(kernel, name, in_specs, outs, scratch, limit):
    return pl.pallas_call(
        kernel,
        name=name,
        out_shape=outs,
        in_specs=in_specs,
        out_specs=jax.tree.map(lambda _: vmem(), outs),
        scratch_shapes=scratch,
        compiler_params=pltpu.CompilerParams(vmem_limit_bytes=limit),
    )


def exchange(x):
    width = x.shape[0] * x.shape[1] // DEVS
    moved = lax.all_to_all(x.reshape(DEVS, 1, width), AXES, split_axis=0, concat_axis=0, tiled=True)
    return moved.reshape(x.shape)


def body(splat_params, list_owner, list_slot, list_length, target):
    shape = jax.ShapeDtypeStruct
    wire = shape((DEVS * WIRE, 128), F32)
    route = call(
        route_kernel, "route", [smem(), vmem(), vmem()],
        (shape((DEVS, 128), jnp.int32), shape((ROWS, SEGS), F32), shape((ROWS, SEGS), F32)), [], 32 << 20,
    )
    request, owners, ranks = route(list_length, list_owner.reshape(ROWS, SEGS), list_slot)
    asked = exchange(request)
    rows = splat_params.shape[1] // 8
    step = 1024
    packed = pl.pallas_call(
        pack_kernel,
        name="pack",
        grid=(rows // step,),
        out_shape=shape((rows, 128), F32),
        in_specs=[pl.BlockSpec((10, step), lambda i, g=g: (0, g * (rows // step) + i)) for g in range(8)],
        out_specs=pl.BlockSpec((step, 128), lambda i: (i, 0)),
        compiler_params=pltpu.CompilerParams(vmem_limit_bytes=16 << 20),
    )(*[splat_params] * 8)
    staging = [pltpu.VMEM((RANKS, DEVS), BF16), pltpu.VMEM((BLOCK * RANKS, 128), F32)]
    gather = call(gather_kernel, "gather", [smem(), vmem(), vmem()], wire, staging, 32 << 20)
    replies = exchange(gather(asked, asked, packed))
    field = pltpu.VMEM((256, SEGS), F32)
    deep = pltpu.VMEM((STEPS, 256, SEGS), F32)
    render = call(
        render_kernel, "render", [vmem()] * 4, (shape(target.shape, F32), wire),
        [
            pltpu.VMEM((DEVS, ROWS * SEGS), BF16), pltpu.VMEM((WIRE * 128, 384), BF16),
            pltpu.VMEM((10, ROWS, SEGS), F32), deep, deep, pltpu.VMEM((4, 256, SEGS), F32), field, field, field,
            pltpu.VMEM((4, 256, SEGS), F32), field, field,
            pltpu.VMEM((STEPS, 16, SEGS), F32), pltpu.VMEM((STEPS, 16, SEGS), F32),
            pltpu.VMEM((10, ROWS, SEGS), F32), pltpu.VMEM((WIRE * 128, DEVS), F32),
        ],
        40 << 20,
    )
    images, outgoing = render(replies, owners, ranks, target)
    incoming = exchange(outgoing)
    scatter = call(
        scatter_kernel, "scatter", [smem(), vmem(), vmem()], shape(splat_params.shape, F32),
        staging + [pltpu.VMEM((128, 128), F32)] + [pltpu.VMEM((rows, 128), F32)] * CHAINS, 48 << 20,
    )
    return (images, scatter(asked, asked, incoming))


def solution(mesh):
    in_specs = (
        P(None, AXES),
        P(AXES, None, None),
        P(AXES, None),
        P(AXES),
        P(None, AXES, None),
    )
    out_specs = (P(None, AXES, None), P(None, AXES))
    return jax.shard_map(body, mesh=mesh, in_specs=in_specs, out_specs=out_specs, check_vma=False)
```

```python
import jax
import jax.numpy as jnp
from jax import lax
from jax.experimental import pallas as pl
from jax.experimental.pallas import tpu as pltpu
from jax.sharding import PartitionSpec as P

AXES = ("row", "col")
DEVS = 128
RANKS = 64
TILES = 4
SEGS = 128
STEPS = 8
ROWS = TILES * STEPS
WIRE = 5
GROUP = 16
BLOCK = 16
CHUNKS = ((0, 32), (32, 48), (48, 64))
CLOSE = 1024
CHAINS = 4
LOG2E = 1.4426950408889634
F32 = jnp.float32
BF16 = jnp.bfloat16


def iota(shape, dim):
    return lax.broadcasted_iota(jnp.int32, shape, dim)


def dot(a, b):
    return lax.dot_general(a, b, (((1,), (0,)), ((), ())), preferred_element_type=F32)


def dot_nt(a, b):
    return lax.dot_general(a, b, (((1,), (1,)), ((), ())), preferred_element_type=F32)


def split(x, parts):
    out = []
    for _ in range(parts - 1):
        head = x.astype(BF16)
        out.append(head)
        x = x - head.astype(F32)
    out.append(x.astype(BF16))
    return out


def onehot_rows(row, count):
    wide = jnp.broadcast_to(row, (count, row.shape[1]))
    return wide == iota(wide.shape, 0).astype(F32)


def route_kernel(length_ref, owner_ref, slot_ref, request_ref, owner_out, rank_out):
    lane = iota((STEPS, SEGS), 1)
    step = iota((STEPS, SEGS), 0)
    picks = (lane & (STEPS - 1)) == step
    pieces = []
    for r in range(STEPS):
        rows = []
        slot_rows = []
        for t in range(TILES):
            own = jnp.broadcast_to(owner_ref[t * STEPS + r : t * STEPS + r + 1, :], (STEPS, SEGS))
            rows.append(jnp.where(picks, own, 0))
            slot = slot_ref[t : t + 1, r * SEGS : (r + 1) * SEGS]
            slot_rows.append(jnp.where(picks, jnp.broadcast_to(slot, (STEPS, SEGS)), 0))
        rows += [s >> 8 for s in slot_rows] + [s & 255 for s in slot_rows]
        pieces.append(jnp.concatenate(rows, axis=0).astype(F32).astype(BF16))
    spread = jnp.concatenate(pieces, axis=1)
    place = ((iota((STEPS * SEGS, SEGS), 0) >> 3) == iota((STEPS * SEGS, SEGS), 1)).astype(F32)
    moved = dot(spread, place.astype(BF16))
    lane = iota((ROWS, SEGS), 1)
    row = iota((ROWS, SEGS), 0)
    length = jnp.full((ROWS, SEGS), length_ref[0], jnp.int32)
    for t in range(1, TILES):
        length = jnp.where((row >> 3) == t, length_ref[t], length)
    live = (lane * STEPS + (row & (STEPS - 1))) < length
    owners = jnp.where(live, moved[0:ROWS], -1.0)
    high = moved[ROWS : 2 * ROWS]
    low = moved[2 * ROWS : 3 * ROWS]
    owner_out[...] = owners
    before = (iota((256, 256), 0) < iota((256, 256), 1)).astype(F32).astype(BF16)
    before = jnp.concatenate([before, jnp.ones((256, 256), BF16)], axis=1)
    rank_of = (iota((2 * RANKS, 256), 0) & (RANKS - 1)).astype(F32)
    upper = iota((2 * RANKS, 256), 0) < RANKS
    carry = jnp.zeros((DEVS, 256), F32)
    request = jnp.zeros((2 * RANKS, DEVS), F32)
    for n in range(ROWS // 2):
        pair = lambda x: jnp.concatenate([x[2 * n : 2 * n + 1], x[2 * n + 1 : 2 * n + 2]], axis=1)
        hot = onehot_rows(pair(owners), DEVS)
        hot16 = hot.astype(F32).astype(BF16)
        counted = dot(hot16, before)
        rank = jnp.sum(jnp.where(hot, counted[:, :256] + carry, 0.0), axis=0, keepdims=True)
        carry = carry + counted[:, 256:]
        rank_out[2 * n : 2 * n + 1, :] = rank[:, :SEGS]
        rank_out[2 * n + 1 : 2 * n + 2, :] = rank[:, SEGS:]
        values = jnp.where(upper, pair(high), pair(low))
        values = jnp.where(rank_of == rank, values, 0.0)
        request = request + dot_nt(values.astype(BF16), hot16)
    slots = request[:RANKS] * 256.0 + request[RANKS:]
    slots = jnp.concatenate([slots, slots], axis=0).T
    full = jnp.where(iota((DEVS, DEVS), 1) < RANKS, slots, carry[:, :DEVS])
    request_ref[...] = full.astype(jnp.int32)


def pack_kernel(*refs):
    out_ref = refs[-1]
    pad = jnp.zeros((GROUP - 10, 128), F32)
    for n in range(refs[0].shape[1] // 128):
        blocks = []
        for ref in refs[:-1]:
            blocks += [ref[:, n * 128 : (n + 1) * 128], pad]
        out_ref[n * 128 : (n + 1) * 128, :] = jnp.concatenate(blocks, axis=0).T


def bit_clear(shift):
    return (iota((RANKS, 128), 1) & shift) == 0


def merge_groups(xs):
    xs = [xs[q] for q in (0, 4, 2, 6, 1, 5, 3, 7)]
    for shift in (16, 32, 64):
        half = len(xs) // 2
        low = bit_clear(shift)
        xs = [
            jnp.where(low, x, y) + pltpu.roll(jnp.where(low, y, x), shift, 1)
            for x, y in zip(xs[:half], xs[half:])
        ]
    return xs[0]


def spread_groups(x):
    xs = [x]
    for shift in (64, 32, 16):
        low = bit_clear(shift)
        nexts = []
        for y in xs:
            z = pltpu.roll(y, shift, 1)
            nexts += [jnp.where(low, y, z), jnp.where(low, z, y)]
        xs = nexts
    return xs


def prepare(asked_ref, table_rows, row_number_ref, number_ref, number_sem, group_ref, widen_ref):
    asked = asked_ref[...]
    lane = iota((DEVS, 128), 1)
    row_number_ref[...] = jnp.where(lane < RANKS, asked & (table_rows - 1), asked)
    copy = pltpu.make_async_copy(row_number_ref, number_ref, number_sem)
    copy.start()
    groups = lax.div(asked, table_rows).astype(F32).T[:RANKS]
    for b in range(DEVS // BLOCK):
        turned = groups if b == 0 else pltpu.roll(groups, DEVS - b * BLOCK, 1)
        group_ref[b * RANKS : (b + 1) * RANKS, :] = turned.astype(BF16)
    for n in range(BLOCK):
        widen_ref[:, n * 128 : (n + 1) * 128] = (iota((DEVS, 128), 0) == n).astype(F32).astype(BF16)
    return copy


def wide_groups(group_ref, widen_ref, b):
    at = pl.ds(pl.multiple_of(b * RANKS, RANKS), RANKS)
    return dot(group_ref[at, :], widen_ref[...])


def gather_kernel(
    asked_ref, table_hbm, out_ref, row_number_ref, number_ref, group_ref, widen_ref, row_ref, table_ref, sems
):
    left = iota((WIRE, 128), 1) < RANKS
    fill = pltpu.make_async_copy(table_hbm, table_ref, sems.at[1])
    fill.start()
    copy = prepare(asked_ref, table_ref.shape[0], row_number_ref, number_ref, sems.at[0], group_ref, widen_ref)
    row_ref[...] = jnp.zeros(row_ref.shape, F32)
    copy.wait()
    fill.wait()

    def block(b, carry):
        def source(q, carry):
            src = b * BLOCK + q
            count = number_ref[src, RANKS]
            mine_ref = row_ref.at[pl.ds(pl.multiple_of(q * RANKS, RANKS), RANKS)]
            for first, last in CHUNKS:

                @pl.when(count > first)
                def _():
                    for rank in range(first, last):
                        mine_ref[rank : rank + 1, :] = table_ref[pl.ds(number_ref[src, rank], 1), :]

            return carry

        lax.fori_loop(0, BLOCK, source, 0)
        groups = wide_groups(group_ref, widen_ref, b)
        lane_group = (iota((RANKS, 128), 1) >> 4).astype(F32)
        halves = []
        for half in range(2):
            picked = []
            for n in range(half * 8, half * 8 + 8):
                rows = row_ref[n * RANKS : (n + 1) * RANKS, :]
                picked.append(jnp.where(lane_group == groups[:, n * 128 : (n + 1) * 128], rows, 0.0))
            halves.append(merge_groups(picked))
        turned = jnp.concatenate(halves, axis=0).T
        evens, odds = [], []
        for q in range(8):
            first = turned[q * GROUP : q * GROUP + WIRE]
            second = turned[q * GROUP + WIRE : q * GROUP + 2 * WIRE]
            evens.append(jnp.where(left, first, pltpu.roll(second, RANKS, 1)))
            odds.append(jnp.where(left, pltpu.roll(first, RANKS, 1), second))
        at = pl.multiple_of(b * BLOCK * WIRE, 8)
        out_ref[pl.ds(at, BLOCK * WIRE), :] = jnp.concatenate(evens + odds, axis=0)
        return carry

    lax.fori_loop(0, DEVS // BLOCK, block, 0)


def scatter_kernel(
    asked_ref, wire_ref, out_hbm, row_number_ref, number_ref, group_ref, widen_ref, row_ref,
    turn_ref, out_ref, sems, *totals,
):
    left = iota((WIRE, 128), 1) < RANKS
    table_rows = totals[0].shape[0]
    copy = prepare(asked_ref, table_rows, row_number_ref, number_ref, sems.at[0], group_ref, widen_ref)
    turn_ref[...] = jnp.zeros((128, 128), F32)

    def clear(i, carry):
        for ref in totals:
            ref[pl.ds(pl.multiple_of(i * 256, 256), 256), :] = jnp.zeros((256, 128), F32)
        return carry

    lax.fori_loop(0, table_rows // 256, clear, 0)
    copy.wait()

    def block(b, carry):
        at = pl.multiple_of(b * BLOCK * WIRE, 8)
        wire = wire_ref[pl.ds(at, BLOCK * WIRE), :]
        for q in range(8):
            even = wire[q * WIRE : (q + 1) * WIRE]
            odd = wire[(q + 8) * WIRE : (q + 9) * WIRE]
            turn_ref[q * GROUP : q * GROUP + WIRE, :] = jnp.where(left, even, pltpu.roll(odd, RANKS, 1))
            turn_ref[q * GROUP + WIRE : q * GROUP + 2 * WIRE, :] = jnp.where(left, pltpu.roll(even, RANKS, 1), odd)
        turned = turn_ref[...].T
        groups = wide_groups(group_ref, widen_ref, b)
        lane_group = (iota((RANKS, 128), 1) >> 4).astype(F32)
        for half in range(2):
            spreads = spread_groups(turned[half * RANKS : (half + 1) * RANKS])
            for q in range(8):
                n = half * 8 + q
                row_ref[n * RANKS : (n + 1) * RANKS, :] = jnp.where(
                    lane_group == groups[:, n * 128 : (n + 1) * 128], spreads[q], 0.0
                )

        def source(q, carry):
            src = b * BLOCK + q
            count = number_ref[src, RANKS]
            mine_ref = row_ref.at[pl.ds(pl.multiple_of(q * RANKS, RANKS), RANKS)]
            for first, last in CHUNKS:

                @pl.when(count > first)
                def _():
                    for start in range(first, last, CHAINS):
                        news = []
                        for i, ref in enumerate(totals):
                            row = number_ref[src, start + i]
                            news.append((row, mine_ref[start + i : start + i + 1, :] + ref[pl.ds(row, 1), :]))
                        for ref, (row, total) in zip(totals, news):
                            ref[pl.ds(row, 1), :] = total

            return carry

        lax.fori_loop(0, BLOCK, source, 0)
        return carry

    lax.fori_loop(0, DEVS // BLOCK, block, 0)

    def close(i, carry):
        base = pl.multiple_of(i * CLOSE, CLOSE)
        for n in range(CLOSE // 128):
            at = pl.ds(base + n * 128, 128)
            total = totals[0][at, :]
            for ref in totals[1:]:
                total = total + ref[at, :]
            total = total.T
            for g in range(8):
                out_ref[:, pl.ds(g * table_rows + base + n * 128, 128)] = total[g * GROUP : g * GROUP + 10]
        for g in range(8):
            lanes = pl.ds(pl.multiple_of(g * table_rows + base, CLOSE), CLOSE)
            pltpu.make_async_copy(out_ref.at[:, lanes], out_hbm.at[:, lanes], sems.at[1]).start()
        return carry

    lax.fori_loop(0, table_rows // CLOSE, close, 0)
    pltpu.make_async_copy(out_ref, out_hbm, sems.at[1]).wait()


def render_kernel(
    wire_ref, owner_ref, rank_ref, target_ref, image_ref, out_ref,
    hot_ref, left_ref, value_ref, fall_ref, flow_ref, sum_ref, keep_ref, reach_ref, behind_ref,
    shade_ref, column_ref, picture_ref, across_ref, tilt_ref, grad_ref, spread_ref,
):
    for c in range(WIRE):
        block = wire_ref[pl.ds(c, DEVS, stride=WIRE), :].T
        parts = split(block, 3)
        left_ref[c * 128 : (c + 1) * 128, :] = jnp.concatenate(parts, axis=1)
    rank_of = iota((RANKS, 256), 0).astype(F32)

    def fetch(n, carry):
        at = pl.ds(pl.multiple_of(n * 256, 256), 256)
        owner = jnp.concatenate([owner_ref[pl.ds(2 * n, 1), :], owner_ref[pl.ds(2 * n + 1, 1), :]], axis=1)
        rank = jnp.concatenate([rank_ref[pl.ds(2 * n, 1), :], rank_ref[pl.ds(2 * n + 1, 1), :]], axis=1)
        hot = onehot_rows(owner, DEVS).astype(F32).astype(BF16)
        hot_ref[:, at] = hot
        mine = rank_of == rank
        found = dot(left_ref[...], jnp.concatenate([hot, hot, hot], axis=0))
        for c in range(WIRE):
            for h in range(2):
                block = found[c * 128 + h * RANKS : c * 128 + (h + 1) * RANKS]
                got = jnp.sum(jnp.where(mine, block, 0.0), axis=0, keepdims=True)
                v = c + WIRE * h
                value_ref[v, pl.ds(2 * n, 1), :] = got[:, :SEGS]
                value_ref[v, pl.ds(2 * n + 1, 1), :] = got[:, SEGS:]
        return carry

    lax.fori_loop(0, ROWS // 2, fetch, 0)

    flat = jnp.concatenate([target_ref[ch] for ch in range(4)] + [jnp.zeros((112, 256), F32)], axis=0)
    column_ref[...] = jnp.concatenate([flat[:, :128].T, flat[:, 128:].T], axis=0)
    picture_ref[...] = jnp.zeros((256, 128), F32)
    earlier = (iota((128, 128), 0) < iota((128, 128), 1)).astype(F32).astype(BF16)
    later = (iota((128, 128), 0) > iota((128, 128), 1)).astype(F32).astype(BF16)
    ones = jnp.ones((256, 128), BF16)
    earlier = jnp.concatenate([earlier, earlier, earlier], axis=0)
    later = jnp.concatenate([later, later], axis=0)
    pixel_x = iota((16, SEGS), 0).astype(F32) + 0.5

    def tile(t, carry):
        first = t * STEPS
        for k in range(STEPS):
            value = lambda v: value_ref[v, pl.ds(first + k, 1), :]
            offset_x = pixel_x - value(0)
            across_ref[k] = (-0.5 * LOG2E) * value(2) * offset_x * offset_x
            tilt_ref[k] = -LOG2E * value(3) * offset_x

        def forward(n, carry):
            for half in range(2):
                y = 2 * n + half
                pixel_y = y.astype(F32) + 0.5
                keep = jnp.ones((16, SEGS), F32)
                sums = [jnp.zeros((16, SEGS), F32) for _ in range(4)]
                at = pl.ds(pl.multiple_of(y * 16, 16), 16)
                for k in range(STEPS):
                    value = lambda v: value_ref[v, pl.ds(first + k, 1), :]
                    offset_y = pixel_y - value(1)
                    down = (-0.5 * LOG2E) * value(4) * offset_y * offset_y
                    fall = jnp.exp2(across_ref[k] + down + tilt_ref[k] * offset_y)
                    flow = fall * keep
                    weight = value(5) * flow
                    keep = keep - weight
                    for ch in range(4):
                        sums[ch] = sums[ch] + value(6 + ch) * weight
                    fall_ref[k, at, :] = fall
                    flow_ref[k, at, :] = flow
                keep_ref[at, :] = keep
                for ch in range(4):
                    sum_ref[ch, at, :] = sums[ch]
            return carry

        lax.fori_loop(0, 8, forward, 0)

        keep = keep_ref[...]
        logs = jnp.concatenate(split(jnp.log(keep), 3), axis=1)
        reach = jnp.exp(dot(logs, earlier))
        reach_ref[...] = reach
        spent = jnp.zeros((256, SEGS), F32)
        for ch in range(4):
            part = sum_ref[ch] * reach
            rendered = dot(jnp.concatenate(split(part, 2), axis=1), ones)
            here = iota((256, 128), 1) == ch * TILES + t
            wanted = jnp.sum(jnp.where(here, column_ref[...], 0.0), axis=1, keepdims=True)
            shade = 2.0 * (rendered - wanted)
            picture_ref[...] = jnp.where(here, rendered, picture_ref[...])
            shade_ref[ch] = shade
            spent = spent + shade * part
        rest = dot(jnp.concatenate(split(spent, 2), axis=1), later)
        behind_ref[...] = rest / (reach * keep)

        for k in reversed(range(STEPS)):
            value = lambda v: value_ref[v, pl.ds(first + k, 1), :]
            mean_y = jnp.broadcast_to(value(1), (8, SEGS))
            opacity = jnp.broadcast_to(value(5), (8, SEGS))
            colours = [jnp.broadcast_to(value(6 + ch), (8, SEGS)) for ch in range(4)]

            def backward(n, sums):
                zero, one, two, tints = sums
                zero, one, two, tints = list(zero), list(one), list(two), list(tints)
                for quarter in range(2):
                    y = 2 * n + quarter
                    offset_y = y.astype(F32) + 0.5 - mean_y
                    for half in range(2):
                        at = pl.ds(pl.multiple_of(y * 16 + half * 8, 8), 8)
                        shades = [shade_ref[ch, at, :] for ch in range(4)]
                        flow = flow_ref[k, at, :] * reach_ref[at, :]
                        lit = (shades[0] * colours[0] + shades[1] * colours[1]) + (
                            shades[2] * colours[2] + shades[3] * colours[3]
                        )
                        behind = behind_ref[at, :]
                        gap = lit - behind
                        behind_ref[at, :] = behind + opacity * fall_ref[k, at, :] * gap
                        grad = flow * gap
                        slope = grad * offset_y
                        zero[half] = zero[half] + grad
                        one[half] = one[half] + slope
                        two[half] = two[half] + slope * offset_y
                        for ch in range(4):
                            tints[ch] = tints[ch] + flow * shades[ch]
                return (tuple(zero), tuple(one), tuple(two), tuple(tints))

            blank = jnp.zeros((8, SEGS), F32)
            zero, one, two, tints = lax.fori_loop(
                0, 8, backward, ((blank,) * 2, (blank,) * 2, (blank,) * 2, (blank,) * 4)
            )
            total = lambda x: jnp.sum(x, axis=0, keepdims=True)
            offset_x = pixel_x - value(0)
            near, far = offset_x[:8], offset_x[8:]
            sum_0 = total(zero[0] + zero[1])
            slope_x = (near * zero[0], far * zero[1])
            sum_x = total(slope_x[0] + slope_x[1])
            sum_xx = total(near * slope_x[0] + far * slope_x[1])
            sum_y = total(one[0] + one[1])
            sum_xy = total(near * one[0] + far * one[1])
            sum_yy = total(two[0] + two[1])
            opacity = value(5)
            grads = [
                opacity * (value(2) * sum_x + value(3) * sum_y),
                opacity * (value(4) * sum_y + value(3) * sum_x),
                -0.5 * opacity * sum_xx,
                -opacity * sum_xy,
                -0.5 * opacity * sum_yy,
                sum_0,
            ] + [opacity * total(tint) for tint in tints]
            for v in range(10):
                grad_ref[v, pl.ds(first + k, 1), :] = grads[v]
        return carry

    lax.fori_loop(0, TILES, tile, 0)

    picture = picture_ref[...]
    picture = jnp.concatenate([picture[:128].T, picture[128:].T], axis=1)
    for ch in range(4):
        image_ref[ch] = picture[ch * TILES : (ch + 1) * TILES, :]

    spread_ref[...] = jnp.zeros((WIRE * 128, DEVS), F32)

    def spread(n, carry):
        at = pl.ds(pl.multiple_of(n * 256, 256), 256)
        rank = jnp.concatenate([rank_ref[pl.ds(2 * n, 1), :], rank_ref[pl.ds(2 * n + 1, 1), :]], axis=1)
        mine = rank_of == rank
        hot = hot_ref[:, at]
        rows = []
        for c in range(WIRE):
            for h in range(2):
                v = c + WIRE * h
                grad = jnp.concatenate(
                    [grad_ref[v, pl.ds(2 * n, 1), :], grad_ref[v, pl.ds(2 * n + 1, 1), :]], axis=1
                )
                rows.append(jnp.where(mine, grad, 0.0))
        heads, tails = split(jnp.concatenate(rows, axis=0), 2)
        spread_ref[...] += dot_nt(
            jnp.concatenate([heads, tails], axis=1), jnp.concatenate([hot, hot], axis=1)
        )
        return carry

    lax.fori_loop(0, ROWS // 2, spread, 0)
    for c in range(WIRE):
        out_ref[pl.ds(c, DEVS, stride=WIRE), :] = spread_ref[c * 128 : (c + 1) * 128, :].T


def vmem():
    return pl.BlockSpec(memory_space=pltpu.VMEM)


def hbm():
    return pl.BlockSpec(memory_space=pltpu.HBM)


def smem():
    return pl.BlockSpec(memory_space=pltpu.SMEM)


def call(kernel, name, in_specs, outs, scratch, limit):
    return pl.pallas_call(
        kernel,
        name=name,
        out_shape=outs,
        in_specs=in_specs,
        out_specs=jax.tree.map(lambda _: vmem(), outs),
        scratch_shapes=scratch,
        compiler_params=pltpu.CompilerParams(vmem_limit_bytes=limit),
    )


def exchange(x):
    width = x.shape[0] * x.shape[1] // DEVS
    moved = lax.all_to_all(x.reshape(DEVS, 1, width), AXES, split_axis=0, concat_axis=0, tiled=True)
    return moved.reshape(x.shape)


def body(splat_params, list_owner, list_slot, list_length, target):
    shape = jax.ShapeDtypeStruct
    wire = shape((DEVS * WIRE, 128), F32)
    route = call(
        route_kernel, "route", [smem(), vmem(), vmem()],
        (shape((DEVS, 128), jnp.int32), shape((ROWS, SEGS), F32), shape((ROWS, SEGS), F32)), [], 32 << 20,
    )
    request, owners, ranks = route(list_length, list_owner.reshape(ROWS, SEGS), list_slot)
    asked = exchange(request)
    rows = splat_params.shape[1] // 8
    step = 1024
    packed = pl.pallas_call(
        pack_kernel,
        name="pack",
        grid=(rows // step,),
        out_shape=shape((rows, 128), F32),
        in_specs=[pl.BlockSpec((10, step), lambda i, g=g: (0, g * (rows // step) + i)) for g in range(8)],
        out_specs=pl.BlockSpec((step, 128), lambda i: (i, 0)),
        compiler_params=pltpu.CompilerParams(vmem_limit_bytes=61 << 20),
    )(*[splat_params] * 8)
    staging = [
        pltpu.VMEM((DEVS, 128), jnp.int32), pltpu.SMEM((DEVS, 128), jnp.int32),
        pltpu.VMEM((DEVS // BLOCK * RANKS, DEVS), BF16), pltpu.VMEM((DEVS, BLOCK * 128), BF16),
        pltpu.VMEM((BLOCK * RANKS, 128), F32),
    ]
    table = pltpu.VMEM((rows, 128), F32)
    sems = pltpu.SemaphoreType.DMA((2,))
    gather = call(gather_kernel, "gather", [vmem(), hbm()], wire, staging + [table, sems], 60 << 20)
    replies = exchange(gather(asked, packed))
    field = pltpu.VMEM((256, SEGS), F32)
    deep = pltpu.VMEM((STEPS, 256, SEGS), F32)
    render = call(
        render_kernel, "render", [vmem()] * 4, (shape(target.shape, F32), wire),
        [
            pltpu.VMEM((DEVS, ROWS * SEGS), BF16), pltpu.VMEM((WIRE * 128, 384), BF16),
            pltpu.VMEM((10, ROWS, SEGS), F32), deep, deep, pltpu.VMEM((4, 256, SEGS), F32), field, field, field,
            pltpu.VMEM((4, 256, SEGS), F32), field, field,
            pltpu.VMEM((STEPS, 16, SEGS), F32), pltpu.VMEM((STEPS, 16, SEGS), F32),
            pltpu.VMEM((10, ROWS, SEGS), F32), pltpu.VMEM((WIRE * 128, DEVS), F32),
        ],
        40 << 20,
    )
    images, outgoing = render(replies, owners, ranks, target)
    incoming = exchange(outgoing)
    scatter = pl.pallas_call(
        scatter_kernel,
        name="scatter",
        out_shape=shape(splat_params.shape, F32),
        in_specs=[vmem(), vmem()],
        out_specs=hbm(),
        scratch_shapes=staging
        + [pltpu.VMEM((128, 128), F32), pltpu.VMEM(splat_params.shape, F32), sems]
        + [table] * CHAINS,
        compiler_params=pltpu.CompilerParams(vmem_limit_bytes=48 << 20),
    )
    return (images, scatter(asked, incoming))


def solution(mesh):
    in_specs = (
        P(None, AXES),
        P(AXES, None, None),
        P(AXES, None),
        P(AXES),
        P(None, AXES, None),
    )
    out_specs = (P(None, AXES, None), P(None, AXES))
    return jax.shard_map(body, mesh=mesh, in_specs=in_specs, out_specs=out_specs, check_vma=False)
```

```python
import jax
import jax.numpy as jnp
from jax import lax
from jax.experimental import pallas as pl
from jax.experimental.pallas import tpu as pltpu
from jax.sharding import PartitionSpec as P

AXES = ("row", "col")
DEVS = 128
RANKS = 64
TILES = 4
SEGS = 128
STEPS = 8
ROWS = TILES * STEPS
WIRE = 5
GROUP = 16
BLOCK = 16
CHUNKS = ((0, 32), (32, 48), (48, 64))
CLOSE = 1024
CHAINS = 4
LOG2E = 1.4426950408889634
F32 = jnp.float32
BF16 = jnp.bfloat16


def iota(shape, dim):
    return lax.broadcasted_iota(jnp.int32, shape, dim)


def dot(a, b):
    return lax.dot_general(a, b, (((1,), (0,)), ((), ())), preferred_element_type=F32)


def dot_nt(a, b):
    return lax.dot_general(a, b, (((1,), (1,)), ((), ())), preferred_element_type=F32)


def split(x, parts):
    out = []
    for _ in range(parts - 1):
        head = x.astype(BF16)
        out.append(head)
        x = x - head.astype(F32)
    out.append(x.astype(BF16))
    return out


def onehot_rows(row, count):
    wide = jnp.broadcast_to(row, (count, row.shape[1]))
    return wide == iota(wide.shape, 0).astype(F32)


def route_kernel(length_ref, owner_ref, slot_ref, request_ref, owner_out, rank_out):
    lane = iota((STEPS, SEGS), 1)
    step = iota((STEPS, SEGS), 0)
    picks = (lane & (STEPS - 1)) == step
    pieces = []
    for r in range(STEPS):
        rows = []
        slot_rows = []
        for t in range(TILES):
            own = jnp.broadcast_to(owner_ref[t * STEPS + r : t * STEPS + r + 1, :], (STEPS, SEGS))
            rows.append(jnp.where(picks, own, 0))
            slot = slot_ref[t : t + 1, r * SEGS : (r + 1) * SEGS]
            slot_rows.append(jnp.where(picks, jnp.broadcast_to(slot, (STEPS, SEGS)), 0))
        rows += [s >> 8 for s in slot_rows] + [s & 255 for s in slot_rows]
        pieces.append(jnp.concatenate(rows, axis=0).astype(F32).astype(BF16))
    spread = jnp.concatenate(pieces, axis=1)
    place = ((iota((STEPS * SEGS, SEGS), 0) >> 3) == iota((STEPS * SEGS, SEGS), 1)).astype(F32)
    moved = dot(spread, place.astype(BF16))
    lane = iota((ROWS, SEGS), 1)
    row = iota((ROWS, SEGS), 0)
    length = jnp.full((ROWS, SEGS), length_ref[0], jnp.int32)
    for t in range(1, TILES):
        length = jnp.where((row >> 3) == t, length_ref[t], length)
    live = (lane * STEPS + (row & (STEPS - 1))) < length
    owners = jnp.where(live, moved[0:ROWS], -1.0)
    high = moved[ROWS : 2 * ROWS]
    low = moved[2 * ROWS : 3 * ROWS]
    owner_out[...] = owners
    before = (iota((256, 256), 0) < iota((256, 256), 1)).astype(F32).astype(BF16)
    before = jnp.concatenate([before, jnp.ones((256, 256), BF16)], axis=1)
    rank_of = (iota((2 * RANKS, 256), 0) & (RANKS - 1)).astype(F32)
    upper = iota((2 * RANKS, 256), 0) < RANKS
    carry = jnp.zeros((DEVS, 256), F32)
    request = jnp.zeros((2 * RANKS, DEVS), F32)
    for n in range(ROWS // 2):
        pair = lambda x: jnp.concatenate([x[2 * n : 2 * n + 1], x[2 * n + 1 : 2 * n + 2]], axis=1)
        hot = onehot_rows(pair(owners), DEVS)
        hot16 = hot.astype(F32).astype(BF16)
        counted = dot(hot16, before)
        rank = jnp.sum(jnp.where(hot, counted[:, :256] + carry, 0.0), axis=0, keepdims=True)
        carry = carry + counted[:, 256:]
        rank_out[2 * n : 2 * n + 1, :] = rank[:, :SEGS]
        rank_out[2 * n + 1 : 2 * n + 2, :] = rank[:, SEGS:]
        values = jnp.where(upper, pair(high), pair(low))
        values = jnp.where(rank_of == rank, values, 0.0)
        request = request + dot_nt(values.astype(BF16), hot16)
    slots = request[:RANKS] * 256.0 + request[RANKS:]
    slots = jnp.concatenate([slots, slots], axis=0).T
    full = jnp.where(iota((DEVS, DEVS), 1) < RANKS, slots, carry[:, :DEVS])
    request_ref[...] = full.astype(jnp.int32)


def pack_kernel(*refs):
    out_ref = refs[-1]
    pad = jnp.zeros((GROUP - 10, 128), F32)
    for n in range(refs[0].shape[1] // 128):
        blocks = []
        for ref in refs[:-1]:
            blocks += [ref[:, n * 128 : (n + 1) * 128], pad]
        out_ref[n * 128 : (n + 1) * 128, :] = jnp.concatenate(blocks, axis=0).T


def bit_clear(shift):
    return (iota((RANKS, 128), 1) & shift) == 0


def merge_groups(xs):
    xs = [xs[q] for q in (0, 4, 2, 6, 1, 5, 3, 7)]
    for shift in (16, 32, 64):
        half = len(xs) // 2
        low = bit_clear(shift)
        xs = [
            jnp.where(low, x, y) + pltpu.roll(jnp.where(low, y, x), shift, 1)
            for x, y in zip(xs[:half], xs[half:])
        ]
    return xs[0]


def spread_groups(x):
    xs = [x]
    for shift in (64, 32, 16):
        low = bit_clear(shift)
        nexts = []
        for y in xs:
            z = pltpu.roll(y, shift, 1)
            nexts += [jnp.where(low, y, z), jnp.where(low, z, y)]
        xs = nexts
    return xs


def prepare(asked_ref, table_rows, row_number_ref, number_ref, number_sem, group_ref):
    asked = asked_ref[...]
    lane = iota((DEVS, 128), 1)
    row_number_ref[...] = jnp.where(lane < RANKS, asked & (table_rows - 1), asked)
    copy = pltpu.make_async_copy(row_number_ref, number_ref, number_sem)
    copy.start()
    groups = lax.div(asked, table_rows).astype(F32).T[:RANKS]
    for b in range(DEVS // BLOCK):
        turned = groups if b == 0 else pltpu.roll(groups, DEVS - b * BLOCK, 1)
        group_ref[b * RANKS : (b + 1) * RANKS, :] = turned.astype(BF16)
    return copy


def fill_widen(widen_ref):
    for n in range(BLOCK):
        widen_ref[:, n * 128 : (n + 1) * 128] = (iota((DEVS, 128), 0) == n).astype(F32).astype(BF16)


def wide_groups(group_ref, widen_ref, b):
    at = pl.ds(pl.multiple_of(b * RANKS, RANKS), RANKS)
    return dot(group_ref[at, :], widen_ref[...])


def gather_kernel(
    asked_ref, table_hbm, out_ref, row_number_ref, group_ref, number_ref, widen_ref, row_ref, table_ref, sems
):
    left = iota((WIRE, 128), 1) < RANKS
    fill = pltpu.make_async_copy(table_hbm, table_ref, sems.at[1])
    fill.start()
    copy = prepare(asked_ref, table_ref.shape[0], row_number_ref, number_ref, sems.at[0], group_ref)
    fill_widen(widen_ref)
    row_ref[...] = jnp.zeros(row_ref.shape, F32)
    copy.wait()
    fill.wait()

    def block(b, carry):
        def source(q, carry):
            src = b * BLOCK + q
            count = number_ref[src, RANKS]
            mine_ref = row_ref.at[pl.ds(pl.multiple_of(q * RANKS, RANKS), RANKS)]
            for first, last in CHUNKS:

                @pl.when(count > first)
                def _():
                    for rank in range(first, last):
                        mine_ref[rank : rank + 1, :] = table_ref[pl.ds(number_ref[src, rank], 1), :]

            return carry

        lax.fori_loop(0, BLOCK, source, 0)
        groups = wide_groups(group_ref, widen_ref, b)
        lane_group = (iota((RANKS, 128), 1) >> 4).astype(F32)
        halves = []
        for half in range(2):
            picked = []
            for n in range(half * 8, half * 8 + 8):
                rows = row_ref[n * RANKS : (n + 1) * RANKS, :]
                picked.append(jnp.where(lane_group == groups[:, n * 128 : (n + 1) * 128], rows, 0.0))
            halves.append(merge_groups(picked))
        turned = jnp.concatenate(halves, axis=0).T
        evens, odds = [], []
        for q in range(8):
            first = turned[q * GROUP : q * GROUP + WIRE]
            second = turned[q * GROUP + WIRE : q * GROUP + 2 * WIRE]
            evens.append(jnp.where(left, first, pltpu.roll(second, RANKS, 1)))
            odds.append(jnp.where(left, pltpu.roll(first, RANKS, 1), second))
        at = pl.multiple_of(b * BLOCK * WIRE, 8)
        out_ref[pl.ds(at, BLOCK * WIRE), :] = jnp.concatenate(evens + odds, axis=0)
        return carry

    lax.fori_loop(0, DEVS // BLOCK, block, 0)


def scatter_kernel(
    row_number_ref, group_ref, wire_ref, out_hbm, number_ref, widen_ref, row_ref,
    turn_ref, out_ref, sems, *totals,
):
    left = iota((WIRE, 128), 1) < RANKS
    table_rows = totals[0].shape[0]
    copy = pltpu.make_async_copy(row_number_ref, number_ref, sems.at[0])
    copy.start()
    fill_widen(widen_ref)
    turn_ref[...] = jnp.zeros((128, 128), F32)

    def clear(i, carry):
        for ref in totals:
            ref[pl.ds(pl.multiple_of(i * 256, 256), 256), :] = jnp.zeros((256, 128), F32)
        return carry

    lax.fori_loop(0, table_rows // 256, clear, 0)
    copy.wait()

    def block(b, carry):
        at = pl.multiple_of(b * BLOCK * WIRE, 8)
        wire = wire_ref[pl.ds(at, BLOCK * WIRE), :]
        for q in range(8):
            even = wire[q * WIRE : (q + 1) * WIRE]
            odd = wire[(q + 8) * WIRE : (q + 9) * WIRE]
            turn_ref[q * GROUP : q * GROUP + WIRE, :] = jnp.where(left, even, pltpu.roll(odd, RANKS, 1))
            turn_ref[q * GROUP + WIRE : q * GROUP + 2 * WIRE, :] = jnp.where(left, pltpu.roll(even, RANKS, 1), odd)
        turned = turn_ref[...].T
        groups = wide_groups(group_ref, widen_ref, b)
        lane_group = (iota((RANKS, 128), 1) >> 4).astype(F32)
        for half in range(2):
            spreads = spread_groups(turned[half * RANKS : (half + 1) * RANKS])
            for q in range(8):
                n = half * 8 + q
                row_ref[n * RANKS : (n + 1) * RANKS, :] = jnp.where(
                    lane_group == groups[:, n * 128 : (n + 1) * 128], spreads[q], 0.0
                )

        def source(q, carry):
            src = b * BLOCK + q
            count = number_ref[src, RANKS]
            mine_ref = row_ref.at[pl.ds(pl.multiple_of(q * RANKS, RANKS), RANKS)]
            for first, last in CHUNKS:

                @pl.when(count > first)
                def _():
                    for start in range(first, last, CHAINS):
                        news = []
                        for i, ref in enumerate(totals):
                            row = number_ref[src, start + i]
                            news.append((row, mine_ref[start + i : start + i + 1, :] + ref[pl.ds(row, 1), :]))
                        for ref, (row, total) in zip(totals, news):
                            ref[pl.ds(row, 1), :] = total

            return carry

        lax.fori_loop(0, BLOCK, source, 0)
        return carry

    lax.fori_loop(0, DEVS // BLOCK, block, 0)

    def close(i, carry):
        base = pl.multiple_of(i * CLOSE, CLOSE)
        for n in range(CLOSE // 128):
            at = pl.ds(base + n * 128, 128)
            total = totals[0][at, :]
            for ref in totals[1:]:
                total = total + ref[at, :]
            total = total.T
            for g in range(8):
                out_ref[:, pl.ds(g * table_rows + base + n * 128, 128)] = total[g * GROUP : g * GROUP + 10]
        for g in range(8):
            lanes = pl.ds(pl.multiple_of(g * table_rows + base, CLOSE), CLOSE)
            pltpu.make_async_copy(out_ref.at[:, lanes], out_hbm.at[:, lanes], sems.at[1]).start()
        return carry

    lax.fori_loop(0, table_rows // CLOSE, close, 0)
    pltpu.make_async_copy(out_ref, out_hbm, sems.at[1]).wait()


HALF = RANKS // 2
KEYS = 2 * DEVS


def marks_kernel(owner_ref, rank_ref, after_ref, hot_ref, turned_ref, mark_ref):
    rank = rank_ref[...].astype(jnp.int32)
    owner = owner_ref[...]
    key = jnp.where(owner < 0.0, -1.0, owner + ((rank >> 5) * DEVS).astype(F32))
    rest = (rank & (HALF - 1)).astype(F32)
    columns = jnp.concatenate([key, jnp.zeros((128 - ROWS, SEGS), F32)], axis=0).T
    for n in range(ROWS):
        at = slice(n * SEGS, (n + 1) * SEGS)
        hot_ref[:, at] = onehot_rows(key[n : n + 1], KEYS).astype(F32).astype(BF16)
        mark_ref[:, at] = onehot_rows(rest[n : n + 1], HALF).astype(F32).astype(BF16)
        column = jnp.broadcast_to(columns[:, n : n + 1], (SEGS, KEYS))
        turned_ref[at, :] = (column == iota((SEGS, KEYS), 1).astype(F32)).astype(F32).astype(BF16)


def render_kernel(
    wire_ref, hot_ref, turned_ref, mark_ref, target_ref, image_ref, out_ref,
    left_ref, value_ref, fall_ref, flow_ref, sum_ref, keep_ref, reach_ref, behind_ref,
    shade_ref, column_ref, picture_ref, across_ref, tilt_ref, grad_ref, spread_ref,
):
    for c in range(WIRE):
        block = wire_ref[pl.ds(c, DEVS, stride=WIRE), :].T
        parts = split(block, 3)
        for h in range(2):
            v = c + WIRE * h
            for half in range(2):
                rows = slice(h * RANKS + half * HALF, h * RANKS + (half + 1) * HALF)
                for n in range(3):
                    at = n * KEYS + half * DEVS
                    left_ref[v * HALF : (v + 1) * HALF, at : at + DEVS] = parts[n][rows]

    def fetch(n, carry):
        at = pl.ds(pl.multiple_of(n * 256, 256), 256)
        hot = hot_ref[:, at]
        mark = mark_ref[:, at].astype(F32)
        found = dot(left_ref[...], jnp.concatenate([hot, hot, hot], axis=0))
        for v in range(10):
            got = jnp.sum(found[v * HALF : (v + 1) * HALF] * mark, axis=0, keepdims=True)
            value_ref[v, pl.ds(2 * n, 1), :] = got[:, :SEGS]
            value_ref[v, pl.ds(2 * n + 1, 1), :] = got[:, SEGS:]
        return carry

    lax.fori_loop(0, ROWS // 2, fetch, 0)

    flat = jnp.concatenate([target_ref[ch] for ch in range(4)] + [jnp.zeros((112, 256), F32)], axis=0)
    column_ref[...] = jnp.concatenate([flat[:, :128].T, flat[:, 128:].T], axis=0)
    picture_ref[...] = jnp.zeros((256, 128), F32)
    earlier = (iota((128, 128), 0) < iota((128, 128), 1)).astype(F32).astype(BF16)
    later = (iota((128, 128), 0) > iota((128, 128), 1)).astype(F32).astype(BF16)
    ones = jnp.ones((256, 128), BF16)
    earlier = jnp.concatenate([earlier, earlier, earlier], axis=0)
    later = jnp.concatenate([later, later], axis=0)
    pixel_x = iota((16, SEGS), 0).astype(F32) + 0.5

    def tile(t, carry):
        first = t * STEPS
        for k in range(STEPS):
            value = lambda v: value_ref[v, pl.ds(first + k, 1), :]
            offset_x = pixel_x - value(0)
            across_ref[k] = (-0.5 * LOG2E) * value(2) * offset_x * offset_x
            tilt_ref[k] = -LOG2E * value(3) * offset_x

        def forward(n, carry):
            for half in range(2):
                y = 2 * n + half
                pixel_y = y.astype(F32) + 0.5
                keep = jnp.ones((16, SEGS), F32)
                sums = [jnp.zeros((16, SEGS), F32) for _ in range(4)]
                at = pl.ds(pl.multiple_of(y * 16, 16), 16)
                for k in range(STEPS):
                    value = lambda v: value_ref[v, pl.ds(first + k, 1), :]
                    offset_y = pixel_y - value(1)
                    down = (-0.5 * LOG2E) * value(4) * offset_y * offset_y
                    fall = jnp.exp2(across_ref[k] + down + tilt_ref[k] * offset_y)
                    flow = fall * keep
                    weight = value(5) * flow
                    keep = keep - weight
                    for ch in range(4):
                        sums[ch] = sums[ch] + value(6 + ch) * weight
                    fall_ref[k, at, :] = fall
                    flow_ref[k, at, :] = flow
                keep_ref[at, :] = keep
                for ch in range(4):
                    sum_ref[ch, at, :] = sums[ch]
            return carry

        lax.fori_loop(0, 8, forward, 0)

        keep = keep_ref[...]
        logs = jnp.concatenate(split(jnp.log(keep), 3), axis=1)
        reach = jnp.exp(dot(logs, earlier))
        reach_ref[...] = reach
        spent = jnp.zeros((256, SEGS), F32)
        for ch in range(4):
            part = sum_ref[ch] * reach
            rendered = dot(jnp.concatenate(split(part, 2), axis=1), ones)
            here = iota((256, 128), 1) == ch * TILES + t
            wanted = jnp.sum(jnp.where(here, column_ref[...], 0.0), axis=1, keepdims=True)
            shade = 2.0 * (rendered - wanted)
            picture_ref[...] = jnp.where(here, rendered, picture_ref[...])
            shade_ref[ch] = shade
            spent = spent + shade * part
        rest = dot(jnp.concatenate(split(spent, 2), axis=1), later)
        behind_ref[...] = rest / (reach * keep)

        for k in reversed(range(STEPS)):
            value = lambda v: value_ref[v, pl.ds(first + k, 1), :]
            mean_y = jnp.broadcast_to(value(1), (8, SEGS))
            opacity = jnp.broadcast_to(value(5), (8, SEGS))
            colours = [jnp.broadcast_to(value(6 + ch), (8, SEGS)) for ch in range(4)]

            def backward(n, sums):
                zero, one, two, tints = sums
                zero, one, two, tints = list(zero), list(one), list(two), list(tints)
                for quarter in range(2):
                    y = 2 * n + quarter
                    offset_y = y.astype(F32) + 0.5 - mean_y
                    for half in range(2):
                        at = pl.ds(pl.multiple_of(y * 16 + half * 8, 8), 8)
                        shades = [shade_ref[ch, at, :] for ch in range(4)]
                        flow = flow_ref[k, at, :] * reach_ref[at, :]
                        lit = (shades[0] * colours[0] + shades[1] * colours[1]) + (
                            shades[2] * colours[2] + shades[3] * colours[3]
                        )
                        behind = behind_ref[at, :]
                        gap = lit - behind
                        behind_ref[at, :] = behind + opacity * fall_ref[k, at, :] * gap
                        grad = flow * gap
                        slope = grad * offset_y
                        zero[half] = zero[half] + grad
                        one[half] = one[half] + slope
                        two[half] = two[half] + slope * offset_y
                        for ch in range(4):
                            tints[ch] = tints[ch] + flow * shades[ch]
                return (tuple(zero), tuple(one), tuple(two), tuple(tints))

            blank = jnp.zeros((8, SEGS), F32)
            zero, one, two, tints = lax.fori_loop(
                0, 8, backward, ((blank,) * 2, (blank,) * 2, (blank,) * 2, (blank,) * 4)
            )
            total = lambda x: jnp.sum(x, axis=0, keepdims=True)
            offset_x = pixel_x - value(0)
            near, far = offset_x[:8], offset_x[8:]
            sum_0 = total(zero[0] + zero[1])
            slope_x = (near * zero[0], far * zero[1])
            sum_x = total(slope_x[0] + slope_x[1])
            sum_xx = total(near * slope_x[0] + far * slope_x[1])
            sum_y = total(one[0] + one[1])
            sum_xy = total(near * one[0] + far * one[1])
            sum_yy = total(two[0] + two[1])
            opacity = value(5)
            grads = [
                opacity * (value(2) * sum_x + value(3) * sum_y),
                opacity * (value(4) * sum_y + value(3) * sum_x),
                -0.5 * opacity * sum_xx,
                -opacity * sum_xy,
                -0.5 * opacity * sum_yy,
                sum_0,
            ] + [opacity * total(tint) for tint in tints]
            for v in range(10):
                grad_ref[v, pl.ds(first + k, 1), :] = grads[v]
        return carry

    lax.fori_loop(0, TILES, tile, 0)

    picture = picture_ref[...]
    picture = jnp.concatenate([picture[:128].T, picture[128:].T], axis=1)
    for ch in range(4):
        image_ref[ch] = picture[ch * TILES : (ch + 1) * TILES, :]

    spread_ref[...] = jnp.zeros((10 * HALF, KEYS), F32)

    def spread(n, carry):
        at = pl.ds(pl.multiple_of(n * 512, 512), 512)
        mark = mark_ref[:, at].astype(F32)
        heads, tails = [], []
        for v in range(10):
            grad = jnp.concatenate([grad_ref[v, pl.ds(4 * n + i, 1), :] for i in range(4)], axis=1)
            head, tail = split(grad * mark, 2)
            heads.append(head)
            tails.append(tail)
        turned = turned_ref[at, :]
        both = jnp.concatenate([jnp.concatenate(heads, axis=0), jnp.concatenate(tails, axis=0)], axis=1)
        spread_ref[...] += dot(both, jnp.concatenate([turned, turned], axis=0))
        return carry

    lax.fori_loop(0, ROWS // 4, spread, 0)
    for c in range(WIRE):
        rows = []
        for h in range(2):
            for half in range(2):
                v = c + WIRE * h
                rows.append(spread_ref[v * HALF : (v + 1) * HALF, half * DEVS : (half + 1) * DEVS])
        out_ref[pl.ds(c, DEVS, stride=WIRE), :] = jnp.concatenate(rows, axis=0).T


def vmem():
    return pl.BlockSpec(memory_space=pltpu.VMEM)


def hbm():
    return pl.BlockSpec(memory_space=pltpu.HBM)


def smem():
    return pl.BlockSpec(memory_space=pltpu.SMEM)


def call(kernel, name, in_specs, outs, scratch, limit):
    return pl.pallas_call(
        kernel,
        name=name,
        out_shape=outs,
        in_specs=in_specs,
        out_specs=jax.tree.map(lambda _: vmem(), outs),
        scratch_shapes=scratch,
        compiler_params=pltpu.CompilerParams(vmem_limit_bytes=limit),
    )


def exchange(x):
    width = x.shape[0] * x.shape[1] // DEVS
    moved = lax.all_to_all(x.reshape(DEVS, 1, width), AXES, split_axis=0, concat_axis=0, tiled=True)
    return moved.reshape(x.shape)


def body(splat_params, list_owner, list_slot, list_length, target):
    shape = jax.ShapeDtypeStruct
    wire = shape((DEVS * WIRE, 128), F32)
    route = call(
        route_kernel, "route", [smem(), vmem(), vmem()],
        (shape((DEVS, 128), jnp.int32), shape((ROWS, SEGS), F32), shape((ROWS, SEGS), F32)), [], 32 << 20,
    )
    request, owners, ranks = route(list_length, list_owner.reshape(ROWS, SEGS), list_slot)
    asked = exchange(request)
    rows = splat_params.shape[1] // 8
    step = 1024
    packed = pl.pallas_call(
        pack_kernel,
        name="pack",
        grid=(rows // step,),
        out_shape=shape((rows, 128), F32),
        in_specs=[pl.BlockSpec((10, step), lambda i, g=g: (0, g * (rows // step) + i)) for g in range(8)],
        out_specs=pl.BlockSpec((step, 128), lambda i: (i, 0)),
        compiler_params=pltpu.CompilerParams(vmem_limit_bytes=61 << 20),
    )(*[splat_params] * 8)
    staging = [
        pltpu.SMEM((DEVS, 128), jnp.int32), pltpu.VMEM((DEVS, BLOCK * 128), BF16),
        pltpu.VMEM((BLOCK * RANKS, 128), F32),
    ]
    table = pltpu.VMEM((rows, 128), F32)
    sems = pltpu.SemaphoreType.DMA((2,))
    numbers = shape((DEVS, 128), jnp.int32)
    groups = shape((DEVS // BLOCK * RANKS, DEVS), BF16)
    gather = call(gather_kernel, "gather", [vmem(), hbm()], (wire, numbers, groups), staging + [table, sems], 60 << 20)
    found, numbers, groups = gather(asked, packed)
    replies = exchange(found)
    entries = ROWS * SEGS
    marks = call(
        marks_kernel, "marks", [vmem(), vmem(), hbm()],
        (shape((KEYS, entries), BF16), shape((entries, KEYS), BF16), shape((HALF, entries), BF16)), [], 16 << 20,
    )
    hot, turned, mark = marks(owners, ranks, numbers)
    field = pltpu.VMEM((256, SEGS), F32)
    deep = pltpu.VMEM((STEPS, 256, SEGS), F32)
    render = call(
        render_kernel, "render", [vmem()] * 5, (shape(target.shape, F32), wire),
        [
            pltpu.VMEM((10 * HALF, 3 * KEYS), BF16),
            pltpu.VMEM((10, ROWS, SEGS), F32), deep, deep, pltpu.VMEM((4, 256, SEGS), F32), field, field, field,
            pltpu.VMEM((4, 256, SEGS), F32), field, field,
            pltpu.VMEM((STEPS, 16, SEGS), F32), pltpu.VMEM((STEPS, 16, SEGS), F32),
            pltpu.VMEM((10, ROWS, SEGS), F32), pltpu.VMEM((10 * HALF, KEYS), F32),
        ],
        20 << 20,
    )
    images, outgoing = render(replies, hot, turned, mark, target)
    incoming = exchange(outgoing)
    scatter = pl.pallas_call(
        scatter_kernel,
        name="scatter",
        out_shape=shape(splat_params.shape, F32),
        in_specs=[vmem(), vmem(), vmem()],
        out_specs=hbm(),
        scratch_shapes=staging
        + [pltpu.VMEM((128, 128), F32), pltpu.VMEM(splat_params.shape, F32), sems]
        + [table] * CHAINS,
        compiler_params=pltpu.CompilerParams(vmem_limit_bytes=48 << 20),
    )
    return (images, scatter(numbers, groups, incoming))


def solution(mesh):
    in_specs = (
        P(None, AXES),
        P(AXES, None, None),
        P(AXES, None),
        P(AXES),
        P(None, AXES, None),
    )
    out_specs = (P(None, AXES, None), P(None, AXES))
    return jax.shard_map(body, mesh=mesh, in_specs=in_specs, out_specs=out_specs, check_vma=False)
```

```python
import jax
import jax.numpy as jnp
from jax import lax
from jax.experimental import pallas as pl
from jax.experimental.pallas import tpu as pltpu
from jax.sharding import PartitionSpec as P

AXES = ("row", "col")
DEVS = 128
RANKS = 64
TILES = 4
SEGS = 128
STEPS = 8
ROWS = TILES * STEPS
WIRE = 5
GROUP = 16
BLOCK = 16
CHUNKS = ((0, 48), (48, 64))
STRETCH = 1024
UNROLL = 4
SPLIT_UNROLL = 2
FORE = 4
FETCH = 4096
SPREAD = 4096
BACK = 8
CHAINS = 8
LOG2E = 1.4426950408889634
F32 = jnp.float32
BF16 = jnp.bfloat16


def iota(shape, dim):
    return lax.broadcasted_iota(jnp.int32, shape, dim)


def dot(a, b):
    return lax.dot_general(a, b, (((1,), (0,)), ((), ())), preferred_element_type=F32)


def dot_nt(a, b):
    return lax.dot_general(a, b, (((1,), (1,)), ((), ())), preferred_element_type=F32)


def split(x, parts):
    out = []
    for _ in range(parts - 1):
        head = x.astype(BF16)
        out.append(head)
        x = x - head.astype(F32)
    out.append(x.astype(BF16))
    return out


def onehot_rows(row, count):
    wide = jnp.broadcast_to(row, (count, row.shape[1]))
    return wide == iota(wide.shape, 0).astype(F32)


def route_kernel(length_ref, owner_ref, slot_ref, request_ref, owner_out, rank_out):
    lane = iota((STEPS, SEGS), 1)
    step = iota((STEPS, SEGS), 0)
    picks = (lane & (STEPS - 1)) == step
    pieces = []
    for r in range(STEPS):
        rows = []
        slot_rows = []
        for t in range(TILES):
            own = jnp.broadcast_to(owner_ref[t * STEPS + r : t * STEPS + r + 1, :], (STEPS, SEGS))
            rows.append(jnp.where(picks, own, 0))
            slot = slot_ref[t : t + 1, r * SEGS : (r + 1) * SEGS]
            slot_rows.append(jnp.where(picks, jnp.broadcast_to(slot, (STEPS, SEGS)), 0))
        rows += [s >> 8 for s in slot_rows] + [s & 255 for s in slot_rows]
        pieces.append(jnp.concatenate(rows, axis=0).astype(F32).astype(BF16))
    spread = jnp.concatenate(pieces, axis=1)
    place = ((iota((STEPS * SEGS, SEGS), 0) >> 3) == iota((STEPS * SEGS, SEGS), 1)).astype(F32)
    moved = dot(spread, place.astype(BF16))
    lane = iota((ROWS, SEGS), 1)
    row = iota((ROWS, SEGS), 0)
    length = jnp.full((ROWS, SEGS), length_ref[0], jnp.int32)
    for t in range(1, TILES):
        length = jnp.where((row >> 3) == t, length_ref[t], length)
    live = (lane * STEPS + (row & (STEPS - 1))) < length
    owners = jnp.where(live, moved[0:ROWS], -1.0)
    high = moved[ROWS : 2 * ROWS]
    low = moved[2 * ROWS : 3 * ROWS]
    owner_out[...] = owners
    before = (iota((256, 256), 0) < iota((256, 256), 1)).astype(F32).astype(BF16)
    before = jnp.concatenate([before, jnp.ones((256, 256), BF16)], axis=1)
    rank_of = (iota((2 * RANKS, 256), 0) & (RANKS - 1)).astype(F32)
    upper = iota((2 * RANKS, 256), 0) < RANKS
    carry = jnp.zeros((DEVS, 256), F32)
    request = jnp.zeros((2 * RANKS, DEVS), F32)
    for n in range(ROWS // 2):
        pair = lambda x: jnp.concatenate([x[2 * n : 2 * n + 1], x[2 * n + 1 : 2 * n + 2]], axis=1)
        hot = onehot_rows(pair(owners), DEVS)
        hot16 = hot.astype(F32).astype(BF16)
        counted = dot(hot16, before)
        rank = jnp.sum(jnp.where(hot, counted[:, :256] + carry, 0.0), axis=0, keepdims=True)
        carry = carry + counted[:, 256:]
        rank_out[2 * n : 2 * n + 1, :] = rank[:, :SEGS]
        rank_out[2 * n + 1 : 2 * n + 2, :] = rank[:, SEGS:]
        values = jnp.where(upper, pair(high), pair(low))
        values = jnp.where(rank_of == rank, values, 0.0)
        request = request + dot_nt(values.astype(BF16), hot16)
    slots = request[:RANKS] * 256.0 + request[RANKS:]
    slots = jnp.concatenate([slots, slots], axis=0).T
    full = jnp.where(iota((DEVS, DEVS), 1) < RANKS, slots, carry[:, :DEVS])
    request_ref[...] = full.astype(jnp.int32)


def pack_kernel(params_hbm, out_hbm, params_ref, out_ref, in_sems, out_sem):
    width = 8 * STRETCH
    steps = params_ref.shape[1] // width
    pad = jnp.zeros((GROUP - 10, 128), F32)

    def read(i):
        at = pl.ds(pl.multiple_of(i * width, width), width)
        return pltpu.make_async_copy(params_hbm.at[:, at], params_ref.at[:, at], in_sems.at[i])

    for i in range(steps):
        read(i).start()

    def step(i, carry):
        read(i).wait()
        mine_ref = params_ref.at[:, pl.ds(pl.multiple_of(i * width, width), width)]
        rows = pl.ds(pl.multiple_of(i * STRETCH, STRETCH), STRETCH)
        done_ref = out_ref.at[rows]
        for n in range(STRETCH // 128):
            blocks = []
            for g in range(8):
                at = g * STRETCH + n * 128
                blocks += [mine_ref[:, at : at + 128], pad]
            done_ref[n * 128 : (n + 1) * 128, :] = jnp.concatenate(blocks, axis=0).T
        pltpu.make_async_copy(done_ref, out_hbm.at[rows], out_sem).start()
        return carry

    lax.fori_loop(0, steps, step, 0)
    pltpu.make_async_copy(out_ref, out_hbm, out_sem).wait()


def bit_clear(shift):
    return (iota((RANKS, 128), 1) & shift) == 0


def merge_groups(xs):
    xs = [xs[q] for q in (0, 4, 2, 6, 1, 5, 3, 7)]
    for shift in (16, 32, 64):
        half = len(xs) // 2
        low = bit_clear(shift)
        xs = [
            jnp.where(low, x, y) + pltpu.roll(jnp.where(low, y, x), shift, 1)
            for x, y in zip(xs[:half], xs[half:])
        ]
    return xs[0]


def spread_groups(x):
    xs = [x]
    for shift in (64, 32, 16):
        low = bit_clear(shift)
        nexts = []
        for y in xs:
            z = pltpu.roll(y, shift, 1)
            nexts += [jnp.where(low, y, z), jnp.where(low, z, y)]
        xs = nexts
    return xs


def prepare(asked_ref, row_number_ref, number_ref, number_sem, group_ref):
    asked = asked_ref[...]
    lane = iota((DEVS, 128), 1)
    row = ((asked >> 13) << 10) | (asked & (STRETCH - 1))
    row_number_ref[...] = jnp.where(lane < RANKS, row, asked)
    copy = pltpu.make_async_copy(row_number_ref, number_ref, number_sem)
    copy.start()
    group = jnp.where(lane < pltpu.roll(asked, RANKS, 1), (asked >> 10) & 7, 8)
    groups = group.astype(F32).T[:RANKS]
    for b in range(DEVS // BLOCK):
        turned = groups if b == 0 else pltpu.roll(groups, DEVS - b * BLOCK, 1)
        group_ref[b * RANKS : (b + 1) * RANKS, :] = turned.astype(BF16)
    return copy


def fill_widen(widen_ref):
    for n in range(BLOCK):
        widen_ref[:, n * 128 : (n + 1) * 128] = (iota((DEVS, 128), 0) == n).astype(F32).astype(BF16)


def wide_groups(group_ref, widen_ref, b):
    at = pl.ds(pl.multiple_of(b * RANKS, RANKS), RANKS)
    return dot(group_ref[at, :], widen_ref[...])


def gather_kernel(
    asked_ref, table_hbm, out_ref, row_number_ref, group_ref, number_ref, widen_ref, row_ref, table_ref, sems
):
    left = iota((WIRE, 128), 1) < RANKS
    fill = pltpu.make_async_copy(table_hbm, table_ref, sems.at[1])
    fill.start()
    copy = prepare(asked_ref, row_number_ref, number_ref, sems.at[0], group_ref)
    fill_widen(widen_ref)
    copy.wait()
    fill.wait()

    def source(src, carry):
        count = number_ref[src, RANKS]
        mine_ref = row_ref.at[pl.ds(pl.multiple_of(src * RANKS, RANKS), RANKS)]
        for first, last in CHUNKS:

            @pl.when(count > first)
            def _():
                for rank in range(first, last):
                    mine_ref[rank : rank + 1, :] = table_ref[pl.ds(number_ref[src, rank], 1), :]

        return carry

    lax.fori_loop(0, DEVS, source, 0)

    def block(b, carry):
        base = pl.multiple_of(b * BLOCK * RANKS, BLOCK * RANKS)
        groups = wide_groups(group_ref, widen_ref, b)
        lane_group = (iota((RANKS, 128), 1) >> 4).astype(F32)
        halves = []
        for half in range(2):
            picked = []
            for n in range(half * 8, half * 8 + 8):
                rows = row_ref[pl.ds(base + n * RANKS, RANKS), :]
                picked.append(jnp.where(lane_group == groups[:, n * 128 : (n + 1) * 128], rows, 0.0))
            halves.append(merge_groups(picked))
        turned = jnp.concatenate(halves, axis=0).T
        evens, odds = [], []
        for q in range(8):
            first = turned[q * GROUP : q * GROUP + WIRE]
            second = turned[q * GROUP + WIRE : q * GROUP + 2 * WIRE]
            evens.append(jnp.where(left, first, pltpu.roll(second, RANKS, 1)))
            odds.append(jnp.where(left, pltpu.roll(first, RANKS, 1), second))
        at = pl.multiple_of(b * BLOCK * WIRE, 8)
        out_ref[pl.ds(at, BLOCK * WIRE), :] = jnp.concatenate(evens + odds, axis=0)
        return carry

    lax.fori_loop(0, DEVS // BLOCK, block, 0, unroll=UNROLL)


def scatter_kernel(
    row_number_ref, group_ref, wire_ref, out_hbm, number_ref, widen_ref, row_ref, turn_ref, out_ref, sems, *totals
):
    left = iota((WIRE, 128), 1) < RANKS
    table_rows = totals[0].shape[0]
    copy = pltpu.make_async_copy(row_number_ref, number_ref, sems.at[0])
    copy.start()
    fill_widen(widen_ref)
    turn_ref[...] = jnp.zeros(turn_ref.shape, F32)

    def clear(i, carry):
        for ref in totals:
            ref[pl.ds(pl.multiple_of(i * 256, 256), 256), :] = jnp.zeros((256, 128), F32)
        return carry

    lax.fori_loop(0, table_rows // 256, clear, 0)

    def block(b, carry):
        at = pl.multiple_of(b * BLOCK * WIRE, 8)
        base = pl.multiple_of(b * BLOCK * RANKS, BLOCK * RANKS)
        wire = wire_ref[pl.ds(at, BLOCK * WIRE), :]
        mine_ref = turn_ref.at[b]
        for q in range(8):
            even = wire[q * WIRE : (q + 1) * WIRE]
            odd = wire[(q + 8) * WIRE : (q + 9) * WIRE]
            mine_ref[q * GROUP : q * GROUP + WIRE, :] = jnp.where(left, even, pltpu.roll(odd, RANKS, 1))
            mine_ref[q * GROUP + WIRE : q * GROUP + 2 * WIRE, :] = jnp.where(left, pltpu.roll(even, RANKS, 1), odd)
        turned = mine_ref[...].T
        groups = wide_groups(group_ref, widen_ref, b)
        lane_group = (iota((RANKS, 128), 1) >> 4).astype(F32)
        for half in range(2):
            spreads = spread_groups(turned[half * RANKS : (half + 1) * RANKS])
            for q in range(8):
                n = half * 8 + q
                row_ref[pl.ds(base + n * RANKS, RANKS), :] = jnp.where(
                    lane_group == groups[:, n * 128 : (n + 1) * 128], spreads[q], 0.0
                )
        return carry

    lax.fori_loop(0, DEVS // BLOCK, block, 0, unroll=SPLIT_UNROLL)
    copy.wait()

    def source(src, carry):
        count = number_ref[src, RANKS]
        mine_ref = row_ref.at[pl.ds(pl.multiple_of(src * RANKS, RANKS), RANKS)]
        for first, last in CHUNKS:

            @pl.when(count > first)
            def _():
                for start in range(first, last, CHAINS):
                    news = []
                    for i, ref in enumerate(totals[: last - start]):
                        row = number_ref[src, start + i]
                        news.append((row, mine_ref[start + i : start + i + 1, :] + ref[pl.ds(row, 1), :]))
                    for ref, (row, total) in zip(totals, news):
                        ref[pl.ds(row, 1), :] = total

        return carry

    lax.fori_loop(0, DEVS, source, 0)

    def close(i, carry):
        base = pl.multiple_of(i * STRETCH, STRETCH)
        lanes = pl.ds(pl.multiple_of(i * 8 * STRETCH, 8 * STRETCH), 8 * STRETCH)
        mine_ref = out_ref.at[:, lanes]
        for n in range(STRETCH // 128):
            at = pl.ds(base + n * 128, 128)
            total = totals[0][at, :]
            for ref in totals[1:]:
                total = total + ref[at, :]
            total = total.T
            for g in range(8):
                spot = g * STRETCH + n * 128
                mine_ref[:, spot : spot + 128] = total[g * GROUP : g * GROUP + 10]
        pltpu.make_async_copy(mine_ref, out_hbm.at[:, lanes], sems.at[1]).start()
        return carry

    lax.fori_loop(0, table_rows // STRETCH, close, 0)
    pltpu.make_async_copy(out_ref, out_hbm, sems.at[1]).wait()


HALF = RANKS // 2
KEYS = 2 * DEVS


def marks_kernel(owner_ref, rank_ref, after_ref, hot_ref, mark_ref, key_ref):
    rank = rank_ref[...].astype(jnp.int32)
    owner = owner_ref[...]
    key = jnp.where(owner < 0.0, -1.0, owner + ((rank >> 5) * DEVS).astype(F32))
    rest = (rank & (HALF - 1)).astype(F32)
    key_ref[...] = key
    for n in range(ROWS):
        at = slice(n * SEGS, (n + 1) * SEGS)
        hot_ref[:, at] = onehot_rows(key[n : n + 1], KEYS).astype(F32).astype(BF16)
        mark_ref[:, at] = onehot_rows(rest[n : n + 1], HALF).astype(F32).astype(BF16)


def render_kernel(
    wire_ref, hot_ref, mark_ref, key_ref, target_ref, image_ref, out_ref,
    turned_ref,    left_ref, value_ref, fall_ref, flow_ref, sum_ref, keep_ref, reach_ref, behind_ref,
    shade_ref, column_ref, picture_ref, across_ref, tilt_ref, grad_ref, spread_ref,
):
    for c in range(WIRE):
        block = wire_ref[pl.ds(c, DEVS, stride=WIRE), :].T
        parts = split(block, 3)
        for h in range(2):
            v = c + WIRE * h
            for half in range(2):
                rows = slice(h * RANKS + half * HALF, h * RANKS + (half + 1) * HALF)
                for n in range(3):
                    at = n * KEYS + half * DEVS
                    left_ref[v * HALF : (v + 1) * HALF, at : at + DEVS] = parts[n][rows]

    columns = jnp.concatenate([key_ref[...], jnp.zeros((128 - ROWS, SEGS), F32)], axis=0).T
    for n in range(ROWS):
        column = jnp.broadcast_to(columns[:, n : n + 1], (SEGS, KEYS))
        turned_ref[n * SEGS : (n + 1) * SEGS, :] = (column == iota((SEGS, KEYS), 1).astype(F32)).astype(F32).astype(BF16)

    def fetch(n, carry):
        at = pl.ds(pl.multiple_of(n * FETCH, FETCH), FETCH)
        hot = hot_ref[:, at]
        mark = mark_ref[:, at].astype(F32)
        found = dot(left_ref[...], jnp.concatenate([hot, hot, hot], axis=0))
        for v in range(10):
            got = jnp.sum(found[v * HALF : (v + 1) * HALF] * mark, axis=0, keepdims=True)
            for i in range(FETCH // SEGS):
                value_ref[v, pl.ds(n * (FETCH // SEGS) + i, 1), :] = got[:, i * SEGS : (i + 1) * SEGS]
        return carry

    lax.fori_loop(0, ROWS * SEGS // FETCH, fetch, 0)

    flat = jnp.concatenate([target_ref[ch] for ch in range(4)] + [jnp.zeros((112, 256), F32)], axis=0)
    column_ref[...] = jnp.concatenate([flat[:, :128].T, flat[:, 128:].T], axis=0)
    picture_ref[...] = jnp.zeros((256, 128), F32)
    earlier = (iota((128, 128), 0) < iota((128, 128), 1)).astype(F32).astype(BF16)
    later = (iota((128, 128), 0) > iota((128, 128), 1)).astype(F32).astype(BF16)
    ones = jnp.ones((256, 128), BF16)
    earlier = jnp.concatenate([earlier, earlier, earlier], axis=0)
    later = jnp.concatenate([later, later], axis=0)
    pixel_x = iota((16, SEGS), 0).astype(F32) + 0.5

    def tile(t, carry):
        first = t * STEPS
        for k in range(STEPS):
            value = lambda v: value_ref[v, pl.ds(first + k, 1), :]
            offset_x = pixel_x - value(0)
            across_ref[k] = (-0.5 * LOG2E) * value(2) * offset_x * offset_x
            tilt_ref[k] = -LOG2E * value(3) * offset_x

        def forward(n, carry):
            for half in range(2):
                y = 2 * n + half
                pixel_y = y.astype(F32) + 0.5
                keep = jnp.ones((16, SEGS), F32)
                sums = [jnp.zeros((16, SEGS), F32) for _ in range(4)]
                at = pl.ds(pl.multiple_of(y * 16, 16), 16)
                for k in range(STEPS):
                    value = lambda v: value_ref[v, pl.ds(first + k, 1), :]
                    offset_y = pixel_y - value(1)
                    down = (-0.5 * LOG2E) * value(4) * offset_y * offset_y
                    fall = jnp.exp2(across_ref[k] + down + tilt_ref[k] * offset_y)
                    flow = fall * keep
                    weight = value(5) * flow
                    keep = keep - weight
                    for ch in range(4):
                        sums[ch] = sums[ch] + value(6 + ch) * weight
                    fall_ref[k, at, :] = fall
                    flow_ref[k, at, :] = flow
                keep_ref[at, :] = keep
                for ch in range(4):
                    sum_ref[ch, at, :] = sums[ch]
            return carry

        lax.fori_loop(0, 8, forward, 0, unroll=FORE)

        keep = keep_ref[...]
        logs = jnp.concatenate(split(jnp.log(keep), 3), axis=1)
        reach = jnp.exp(dot(logs, earlier))
        reach_ref[...] = reach
        spent = jnp.zeros((256, SEGS), F32)
        for ch in range(4):
            part = sum_ref[ch] * reach
            rendered = dot(jnp.concatenate(split(part, 2), axis=1), ones)
            here = iota((256, 128), 1) == ch * TILES + t
            wanted = jnp.sum(jnp.where(here, column_ref[...], 0.0), axis=1, keepdims=True)
            shade = 2.0 * (rendered - wanted)
            picture_ref[...] = jnp.where(here, rendered, picture_ref[...])
            shade_ref[ch] = shade
            spent = spent + shade * part
        rest = dot(jnp.concatenate(split(spent, 2), axis=1), later)
        behind_ref[...] = rest / (reach * keep)

        for k in reversed(range(STEPS)):
            value = lambda v: value_ref[v, pl.ds(first + k, 1), :]
            mean_y = jnp.broadcast_to(value(1), (8, SEGS))
            opacity = jnp.broadcast_to(value(5), (8, SEGS))
            colours = [jnp.broadcast_to(value(6 + ch), (8, SEGS)) for ch in range(4)]

            def backward(n, sums):
                zero, one, two, tints = sums
                zero, one, two, tints = list(zero), list(one), list(two), list(tints)
                for quarter in range(2):
                    y = 2 * n + quarter
                    offset_y = y.astype(F32) + 0.5 - mean_y
                    for half in range(2):
                        at = pl.ds(pl.multiple_of(y * 16 + half * 8, 8), 8)
                        shades = [shade_ref[ch, at, :] for ch in range(4)]
                        flow = flow_ref[k, at, :] * reach_ref[at, :]
                        lit = (shades[0] * colours[0] + shades[1] * colours[1]) + (
                            shades[2] * colours[2] + shades[3] * colours[3]
                        )
                        behind = behind_ref[at, :]
                        gap = lit - behind
                        behind_ref[at, :] = behind + opacity * fall_ref[k, at, :] * gap
                        grad = flow * gap
                        slope = grad * offset_y
                        zero[half] = zero[half] + grad
                        one[half] = one[half] + slope
                        two[half] = two[half] + slope * offset_y
                        for ch in range(4):
                            tints[ch] = tints[ch] + flow * shades[ch]
                return (tuple(zero), tuple(one), tuple(two), tuple(tints))

            blank = jnp.zeros((8, SEGS), F32)
            zero, one, two, tints = lax.fori_loop(
                0, 8, backward, ((blank,) * 2, (blank,) * 2, (blank,) * 2, (blank,) * 4), unroll=BACK
            )
            total = lambda x: jnp.sum(x, axis=0, keepdims=True)
            offset_x = pixel_x - value(0)
            near, far = offset_x[:8], offset_x[8:]
            sum_0 = total(zero[0] + zero[1])
            slope_x = (near * zero[0], far * zero[1])
            sum_x = total(slope_x[0] + slope_x[1])
            sum_xx = total(near * slope_x[0] + far * slope_x[1])
            sum_y = total(one[0] + one[1])
            sum_xy = total(near * one[0] + far * one[1])
            sum_yy = total(two[0] + two[1])
            opacity = value(5)
            grads = [
                opacity * (value(2) * sum_x + value(3) * sum_y),
                opacity * (value(4) * sum_y + value(3) * sum_x),
                -0.5 * opacity * sum_xx,
                -opacity * sum_xy,
                -0.5 * opacity * sum_yy,
                sum_0,
            ] + [opacity * total(tint) for tint in tints]
            for v in range(10):
                grad_ref[v, pl.ds(first + k, 1), :] = grads[v]
        return carry

    lax.fori_loop(0, TILES, tile, 0)

    picture = picture_ref[...]
    picture = jnp.concatenate([picture[:128].T, picture[128:].T], axis=1)
    for ch in range(4):
        image_ref[ch] = picture[ch * TILES : (ch + 1) * TILES, :]

    spread_ref[...] = jnp.zeros((10 * HALF, KEYS), F32)

    def spread(n, carry):
        at = pl.ds(pl.multiple_of(n * SPREAD, SPREAD), SPREAD)
        mark = mark_ref[:, at].astype(F32)
        heads, tails = [], []
        for v in range(10):
            count = SPREAD // SEGS
            grad = jnp.concatenate([grad_ref[v, pl.ds(count * n + i, 1), :] for i in range(count)], axis=1)
            head, tail = split(grad * mark, 2)
            heads.append(head)
            tails.append(tail)
        turned = turned_ref[at, :]
        both = jnp.concatenate([jnp.concatenate(heads, axis=0), jnp.concatenate(tails, axis=0)], axis=1)
        spread_ref[...] += dot(both, jnp.concatenate([turned, turned], axis=0))
        return carry

    lax.fori_loop(0, ROWS * SEGS // SPREAD, spread, 0)
    for c in range(WIRE):
        rows = []
        for h in range(2):
            for half in range(2):
                v = c + WIRE * h
                rows.append(spread_ref[v * HALF : (v + 1) * HALF, half * DEVS : (half + 1) * DEVS])
        out_ref[pl.ds(c, DEVS, stride=WIRE), :] = jnp.concatenate(rows, axis=0).T


def vmem():
    return pl.BlockSpec(memory_space=pltpu.VMEM)


def hbm():
    return pl.BlockSpec(memory_space=pltpu.HBM)


def smem():
    return pl.BlockSpec(memory_space=pltpu.SMEM)


def call(kernel, name, in_specs, outs, scratch, limit):
    return pl.pallas_call(
        kernel,
        name=name,
        out_shape=outs,
        in_specs=in_specs,
        out_specs=jax.tree.map(lambda _: vmem(), outs),
        scratch_shapes=scratch,
        compiler_params=pltpu.CompilerParams(vmem_limit_bytes=limit),
    )


def exchange(x):
    width = x.shape[0] * x.shape[1] // DEVS
    moved = lax.all_to_all(x.reshape(DEVS, 1, width), AXES, split_axis=0, concat_axis=0, tiled=True)
    return moved.reshape(x.shape)


def body(splat_params, list_owner, list_slot, list_length, target):
    shape = jax.ShapeDtypeStruct
    wire = shape((DEVS * WIRE, 128), F32)
    route = call(
        route_kernel, "route", [smem(), vmem(), vmem()],
        (shape((DEVS, 128), jnp.int32), shape((ROWS, SEGS), F32), shape((ROWS, SEGS), F32)), [], 32 << 20,
    )
    request, owners, ranks = route(list_length, list_owner.reshape(ROWS, SEGS), list_slot)
    asked = exchange(request)
    rows = splat_params.shape[1] // 8
    packed = pl.pallas_call(
        pack_kernel,
        name="pack",
        out_shape=shape((rows, 128), F32),
        in_specs=[hbm()],
        out_specs=hbm(),
        scratch_shapes=[
            pltpu.VMEM(splat_params.shape, F32), pltpu.VMEM((rows, 128), F32),
            pltpu.SemaphoreType.DMA((rows // STRETCH,)), pltpu.SemaphoreType.DMA,
        ],
        compiler_params=pltpu.CompilerParams(vmem_limit_bytes=61 << 20),
    )(splat_params)
    staging = [
        pltpu.SMEM((DEVS, 128), jnp.int32), pltpu.VMEM((DEVS, BLOCK * 128), BF16),
        pltpu.VMEM((DEVS * RANKS, 128), F32),
    ]
    table = pltpu.VMEM((rows, 128), F32)
    sems = pltpu.SemaphoreType.DMA((2,))
    numbers = shape((DEVS, 128), jnp.int32)
    groups = shape((DEVS // BLOCK * RANKS, DEVS), BF16)
    gather = call(gather_kernel, "gather", [vmem(), hbm()], (wire, numbers, groups), staging + [table, sems], 60 << 20)
    found, numbers, groups = gather(asked, packed)
    replies = exchange(found)
    entries = ROWS * SEGS
    marks = call(
        marks_kernel, "marks", [vmem(), vmem(), hbm()],
        (shape((KEYS, entries), BF16), shape((HALF, entries), BF16), shape((ROWS, SEGS), F32)), [], 16 << 20,
    )
    hot, mark, keys = marks(owners, ranks, numbers)
    field = pltpu.VMEM((256, SEGS), F32)
    deep = pltpu.VMEM((STEPS, 256, SEGS), F32)
    render = call(
        render_kernel, "render", [vmem()] * 5, (shape(target.shape, F32), wire),
        [
            pltpu.VMEM((entries, KEYS), BF16), pltpu.VMEM((10 * HALF, 3 * KEYS), BF16),
            pltpu.VMEM((10, ROWS, SEGS), F32), deep, deep, pltpu.VMEM((4, 256, SEGS), F32), field, field, field,
            pltpu.VMEM((4, 256, SEGS), F32), field, field,
            pltpu.VMEM((STEPS, 16, SEGS), F32), pltpu.VMEM((STEPS, 16, SEGS), F32),
            pltpu.VMEM((10, ROWS, SEGS), F32), pltpu.VMEM((10 * HALF, KEYS), F32),
        ],
        24 << 20,
    )
    images, outgoing = render(replies, hot, mark, keys, target)
    incoming = exchange(outgoing)
    scatter = pl.pallas_call(
        scatter_kernel,
        name="scatter",
        out_shape=shape(splat_params.shape, F32),
        in_specs=[vmem(), vmem(), vmem()],
        out_specs=hbm(),
        scratch_shapes=staging
        + [pltpu.VMEM((DEVS // BLOCK, 128, 128), F32), pltpu.VMEM(splat_params.shape, F32), sems]
        + [table] * CHAINS,
        compiler_params=pltpu.CompilerParams(vmem_limit_bytes=56 << 20),
    )
    return (images, scatter(numbers, groups, incoming))


def solution(mesh):
    in_specs = (
        P(None, AXES),
        P(AXES, None, None),
        P(AXES, None),
        P(AXES),
        P(None, AXES, None),
    )
    out_specs = (P(None, AXES, None), P(None, AXES))
    return jax.shard_map(body, mesh=mesh, in_specs=in_specs, out_specs=out_specs, check_vma=False)
```

```python
import jax
import jax.numpy as jnp
from jax import lax
from jax.experimental import pallas as pl
from jax.experimental.pallas import tpu as pltpu
from jax.sharding import PartitionSpec as P

AXES = ("row", "col")
DEVS = 128
RANKS = 64
TILES = 4
SEGS = 128
STEPS = 8
ROWS = TILES * STEPS
WIRE = 5
GROUP = 16
BLOCK = 16
CHUNKS = ((0, 48), (48, 64))
STRETCH = 1024
UNROLL = 4
ROUTE_LIMIT = 63 << 20
SPLIT_UNROLL = 2
FORE = 4
FETCH = 4096
SPREAD = 4096
BACK = 8
CHAINS = 6
LOG2E = 1.4426950408889634
F32 = jnp.float32
BF16 = jnp.bfloat16


def iota(shape, dim):
    return lax.broadcasted_iota(jnp.int32, shape, dim)


def dot(a, b):
    return lax.dot_general(a, b, (((1,), (0,)), ((), ())), preferred_element_type=F32)


def dot_nt(a, b):
    return lax.dot_general(a, b, (((1,), (1,)), ((), ())), preferred_element_type=F32)


def split(x, parts):
    out = []
    for _ in range(parts - 1):
        head = x.astype(BF16)
        out.append(head)
        x = x - head.astype(F32)
    out.append(x.astype(BF16))
    return out


def onehot_rows(row, count):
    wide = jnp.broadcast_to(row, (count, row.shape[1]))
    return wide == iota(wide.shape, 0).astype(F32)


def route_kernel(
    length_hbm, owner_hbm, slot_hbm, request_ref, owner_out, rank_out, length_ref, owner_ref, slot_ref, sems
):
    pairs = ((length_hbm, length_ref), (owner_hbm, owner_ref), (slot_hbm, slot_ref))
    copies = [pltpu.make_async_copy(a, b, sems.at[i]) for i, (a, b) in enumerate(pairs)]
    for copy in copies:
        copy.start()
    for copy in copies:
        copy.wait()
    lane = iota((STEPS, SEGS), 1)
    step = iota((STEPS, SEGS), 0)
    picks = (lane & (STEPS - 1)) == step
    pieces = []
    for r in range(STEPS):
        rows = []
        slot_rows = []
        for t in range(TILES):
            own = jnp.broadcast_to(owner_ref[t * STEPS + r : t * STEPS + r + 1, :], (STEPS, SEGS))
            rows.append(jnp.where(picks, own, 0))
            slot = slot_ref[t : t + 1, r * SEGS : (r + 1) * SEGS]
            slot_rows.append(jnp.where(picks, jnp.broadcast_to(slot, (STEPS, SEGS)), 0))
        rows += [s >> 8 for s in slot_rows] + [s & 255 for s in slot_rows]
        pieces.append(jnp.concatenate(rows, axis=0).astype(F32).astype(BF16))
    spread = jnp.concatenate(pieces, axis=1)
    place = ((iota((STEPS * SEGS, SEGS), 0) >> 3) == iota((STEPS * SEGS, SEGS), 1)).astype(F32)
    moved = dot(spread, place.astype(BF16))
    lane = iota((ROWS, SEGS), 1)
    row = iota((ROWS, SEGS), 0)
    length = jnp.full((ROWS, SEGS), length_ref[0], jnp.int32)
    for t in range(1, TILES):
        length = jnp.where((row >> 3) == t, length_ref[t], length)
    live = (lane * STEPS + (row & (STEPS - 1))) < length
    owners = jnp.where(live, moved[0:ROWS], -1.0)
    high = moved[ROWS : 2 * ROWS]
    low = moved[2 * ROWS : 3 * ROWS]
    owner_out[...] = owners
    before = (iota((256, 256), 0) < iota((256, 256), 1)).astype(F32).astype(BF16)
    before = jnp.concatenate([before, jnp.ones((256, 256), BF16)], axis=1)
    rank_of = (iota((2 * RANKS, 256), 0) & (RANKS - 1)).astype(F32)
    upper = iota((2 * RANKS, 256), 0) < RANKS
    carry = jnp.zeros((DEVS, 256), F32)
    request = jnp.zeros((2 * RANKS, DEVS), F32)
    for n in range(ROWS // 2):
        pair = lambda x: jnp.concatenate([x[2 * n : 2 * n + 1], x[2 * n + 1 : 2 * n + 2]], axis=1)
        hot = onehot_rows(pair(owners), DEVS)
        hot16 = hot.astype(F32).astype(BF16)
        counted = dot(hot16, before)
        rank = jnp.sum(jnp.where(hot, counted[:, :256] + carry, 0.0), axis=0, keepdims=True)
        carry = carry + counted[:, 256:]
        rank_out[2 * n : 2 * n + 1, :] = rank[:, :SEGS]
        rank_out[2 * n + 1 : 2 * n + 2, :] = rank[:, SEGS:]
        values = jnp.where(upper, pair(high), pair(low))
        values = jnp.where(rank_of == rank, values, 0.0)
        request = request + dot_nt(values.astype(BF16), hot16)
    slots = request[:RANKS] * 256.0 + request[RANKS:]
    slots = jnp.concatenate([slots, slots], axis=0).T
    full = jnp.where(iota((DEVS, DEVS), 1) < RANKS, slots, carry[:, :DEVS])
    request_ref[...] = full.astype(jnp.int32)


def pack_kernel(params_hbm, out_hbm, params_ref, out_ref, in_sems, out_sem):
    width = 8 * STRETCH
    steps = params_ref.shape[1] // width
    pad = jnp.zeros((GROUP - 10, 128), F32)

    def read(i):
        at = pl.ds(pl.multiple_of(i * width, width), width)
        return pltpu.make_async_copy(params_hbm.at[:, at], params_ref.at[:, at], in_sems.at[i])

    for i in range(steps):
        read(i).start()

    def step(i, carry):
        read(i).wait()
        mine_ref = params_ref.at[:, pl.ds(pl.multiple_of(i * width, width), width)]
        rows = pl.ds(pl.multiple_of(i * STRETCH, STRETCH), STRETCH)
        done_ref = out_ref.at[rows]
        for n in range(STRETCH // 128):
            blocks = []
            for g in range(8):
                at = g * STRETCH + n * 128
                blocks += [mine_ref[:, at : at + 128], pad]
            done_ref[n * 128 : (n + 1) * 128, :] = jnp.concatenate(blocks, axis=0).T
        pltpu.make_async_copy(done_ref, out_hbm.at[rows], out_sem).start()
        return carry

    lax.fori_loop(0, steps, step, 0)
    pltpu.make_async_copy(out_ref, out_hbm, out_sem).wait()


def bit_clear(shift):
    return (iota((RANKS, 128), 1) & shift) == 0


def merge_groups(xs):
    xs = [xs[q] for q in (0, 4, 2, 6, 1, 5, 3, 7)]
    for shift in (16, 32, 64):
        half = len(xs) // 2
        low = bit_clear(shift)
        xs = [
            jnp.where(low, x, y) + pltpu.roll(jnp.where(low, y, x), shift, 1)
            for x, y in zip(xs[:half], xs[half:])
        ]
    return xs[0]


def spread_groups(x):
    xs = [x]
    for shift in (64, 32, 16):
        low = bit_clear(shift)
        nexts = []
        for y in xs:
            z = pltpu.roll(y, shift, 1)
            nexts += [jnp.where(low, y, z), jnp.where(low, z, y)]
        xs = nexts
    return xs


def prepare(asked_ref, row_number_ref, number_ref, number_sem, group_ref):
    asked = asked_ref[...]
    lane = iota((DEVS, 128), 1)
    row = ((asked >> 13) << 10) | (asked & (STRETCH - 1))
    row_number_ref[...] = jnp.where(lane < RANKS, row, asked)
    copy = pltpu.make_async_copy(row_number_ref, number_ref, number_sem)
    copy.start()
    group = jnp.where(lane < pltpu.roll(asked, RANKS, 1), (asked >> 10) & 7, 8)
    groups = group.astype(F32).T[:RANKS]
    for b in range(DEVS // BLOCK):
        turned = groups if b == 0 else pltpu.roll(groups, DEVS - b * BLOCK, 1)
        group_ref[b * RANKS : (b + 1) * RANKS, :] = turned.astype(BF16)
    return copy


def fill_widen(widen_ref):
    for n in range(BLOCK):
        widen_ref[:, n * 128 : (n + 1) * 128] = (iota((DEVS, 128), 0) == n).astype(F32).astype(BF16)


def wide_groups(group_ref, widen_ref, b):
    at = pl.ds(pl.multiple_of(b * RANKS, RANKS), RANKS)
    return dot(group_ref[at, :], widen_ref[...])


def gather_kernel(
    asked_ref, table_hbm, out_ref, row_number_ref, group_ref, number_ref, widen_ref, row_ref, table_ref, sems
):
    left = iota((WIRE, 128), 1) < RANKS
    fill = pltpu.make_async_copy(table_hbm, table_ref, sems.at[1])
    fill.start()
    copy = prepare(asked_ref, row_number_ref, number_ref, sems.at[0], group_ref)
    fill_widen(widen_ref)
    copy.wait()
    fill.wait()

    def source(src, carry):
        count = number_ref[src, RANKS]
        mine_ref = row_ref.at[pl.ds(pl.multiple_of(src * RANKS, RANKS), RANKS)]
        for first, last in CHUNKS:

            @pl.when(count > first)
            def _():
                for rank in range(first, last):
                    mine_ref[rank : rank + 1, :] = table_ref[pl.ds(number_ref[src, rank], 1), :]

        return carry

    lax.fori_loop(0, DEVS, source, 0)

    def block(b, carry):
        base = pl.multiple_of(b * BLOCK * RANKS, BLOCK * RANKS)
        groups = wide_groups(group_ref, widen_ref, b)
        lane_group = (iota((RANKS, 128), 1) >> 4).astype(F32)
        halves = []
        for half in range(2):
            picked = []
            for n in range(half * 8, half * 8 + 8):
                rows = row_ref[pl.ds(base + n * RANKS, RANKS), :]
                picked.append(jnp.where(lane_group == groups[:, n * 128 : (n + 1) * 128], rows, 0.0))
            halves.append(merge_groups(picked))
        turned = jnp.concatenate(halves, axis=0).T
        evens, odds = [], []
        for q in range(8):
            first = turned[q * GROUP : q * GROUP + WIRE]
            second = turned[q * GROUP + WIRE : q * GROUP + 2 * WIRE]
            evens.append(jnp.where(left, first, pltpu.roll(second, RANKS, 1)))
            odds.append(jnp.where(left, pltpu.roll(first, RANKS, 1), second))
        at = pl.multiple_of(b * BLOCK * WIRE, 8)
        out_ref[pl.ds(at, BLOCK * WIRE), :] = jnp.concatenate(evens + odds, axis=0)
        return carry

    lax.fori_loop(0, DEVS // BLOCK, block, 0, unroll=UNROLL)


def scatter_kernel(
    row_number_ref, group_ref, wire_ref, out_hbm, number_ref, widen_ref, row_ref, turn_ref, out_ref, sems, *totals
):
    left = iota((WIRE, 128), 1) < RANKS
    table_rows = totals[0].shape[0]
    copy = pltpu.make_async_copy(row_number_ref, number_ref, sems.at[0])
    copy.start()
    fill_widen(widen_ref)
    turn_ref[...] = jnp.zeros(turn_ref.shape, F32)

    def clear(i, carry):
        for ref in totals:
            ref[pl.ds(pl.multiple_of(i * 256, 256), 256), :] = jnp.zeros((256, 128), F32)
        return carry

    lax.fori_loop(0, table_rows // 256, clear, 0)

    def block(b, carry):
        at = pl.multiple_of(b * BLOCK * WIRE, 8)
        base = pl.multiple_of(b * BLOCK * RANKS, BLOCK * RANKS)
        wire = wire_ref[pl.ds(at, BLOCK * WIRE), :]
        mine_ref = turn_ref.at[b]
        for q in range(8):
            even = wire[q * WIRE : (q + 1) * WIRE]
            odd = wire[(q + 8) * WIRE : (q + 9) * WIRE]
            mine_ref[q * GROUP : q * GROUP + WIRE, :] = jnp.where(left, even, pltpu.roll(odd, RANKS, 1))
            mine_ref[q * GROUP + WIRE : q * GROUP + 2 * WIRE, :] = jnp.where(left, pltpu.roll(even, RANKS, 1), odd)
        turned = mine_ref[...].T
        groups = wide_groups(group_ref, widen_ref, b)
        lane_group = (iota((RANKS, 128), 1) >> 4).astype(F32)
        for half in range(2):
            spreads = spread_groups(turned[half * RANKS : (half + 1) * RANKS])
            for q in range(8):
                n = half * 8 + q
                row_ref[pl.ds(base + n * RANKS, RANKS), :] = jnp.where(
                    lane_group == groups[:, n * 128 : (n + 1) * 128], spreads[q], 0.0
                )
        return carry

    lax.fori_loop(0, DEVS // BLOCK, block, 0, unroll=SPLIT_UNROLL)
    copy.wait()

    def source(src, carry):
        count = number_ref[src, RANKS]
        mine_ref = row_ref.at[pl.ds(pl.multiple_of(src * RANKS, RANKS), RANKS)]
        for first, last in CHUNKS:

            @pl.when(count > first)
            def _():
                for start in range(first, last, CHAINS):
                    news = []
                    for i, ref in enumerate(totals[: last - start]):
                        row = number_ref[src, start + i]
                        news.append((row, mine_ref[start + i : start + i + 1, :] + ref[pl.ds(row, 1), :]))
                    for ref, (row, total) in zip(totals, news):
                        ref[pl.ds(row, 1), :] = total

        return carry

    lax.fori_loop(0, DEVS, source, 0)

    def close(i, carry):
        base = pl.multiple_of(i * STRETCH, STRETCH)
        lanes = pl.ds(pl.multiple_of(i * 8 * STRETCH, 8 * STRETCH), 8 * STRETCH)
        mine_ref = out_ref.at[:, lanes]
        for n in range(STRETCH // 128):
            at = pl.ds(base + n * 128, 128)
            total = totals[0][at, :]
            for ref in totals[1:]:
                total = total + ref[at, :]
            total = total.T
            for g in range(8):
                spot = g * STRETCH + n * 128
                mine_ref[:, spot : spot + 128] = total[g * GROUP : g * GROUP + 10]
        pltpu.make_async_copy(mine_ref, out_hbm.at[:, lanes], sems.at[1]).start()
        return carry

    lax.fori_loop(0, table_rows // STRETCH, close, 0)
    pltpu.make_async_copy(out_ref, out_hbm, sems.at[1]).wait()


HALF = RANKS // 2
KEYS = 2 * DEVS


def marks_kernel(owner_ref, rank_ref, after_ref, hot_ref, mark_ref, key_ref):
    rank = rank_ref[...].astype(jnp.int32)
    owner = owner_ref[...]
    key = jnp.where(owner < 0.0, -1.0, owner + ((rank >> 5) * DEVS).astype(F32))
    rest = (rank & (HALF - 1)).astype(F32)
    key_ref[...] = key
    for n in range(ROWS):
        at = slice(n * SEGS, (n + 1) * SEGS)
        hot_ref[:, at] = onehot_rows(key[n : n + 1], KEYS).astype(F32).astype(BF16)
        mark_ref[:, at] = onehot_rows(rest[n : n + 1], HALF).astype(F32).astype(BF16)


def render_kernel(
    wire_ref, hot_ref, mark_ref, key_ref, target_ref, image_ref, out_ref,
    turned_ref,    left_ref, value_ref, fall_ref, flow_ref, sum_ref, keep_ref, reach_ref, behind_ref,
    shade_ref, column_ref, picture_ref, across_ref, tilt_ref, grad_ref, spread_ref,
):
    for c in range(WIRE):
        block = wire_ref[pl.ds(c, DEVS, stride=WIRE), :].T
        parts = split(block, 3)
        for h in range(2):
            v = c + WIRE * h
            for half in range(2):
                rows = slice(h * RANKS + half * HALF, h * RANKS + (half + 1) * HALF)
                for n in range(3):
                    at = n * KEYS + half * DEVS
                    left_ref[v * HALF : (v + 1) * HALF, at : at + DEVS] = parts[n][rows]

    columns = jnp.concatenate([key_ref[...], jnp.zeros((128 - ROWS, SEGS), F32)], axis=0).T
    for n in range(ROWS):
        column = jnp.broadcast_to(columns[:, n : n + 1], (SEGS, KEYS))
        turned_ref[n * SEGS : (n + 1) * SEGS, :] = (column == iota((SEGS, KEYS), 1).astype(F32)).astype(F32).astype(BF16)

    def fetch(n, carry):
        at = pl.ds(pl.multiple_of(n * FETCH, FETCH), FETCH)
        hot = hot_ref[:, at]
        mark = mark_ref[:, at].astype(F32)
        found = dot(left_ref[...], jnp.concatenate([hot, hot, hot], axis=0))
        for v in range(10):
            got = jnp.sum(found[v * HALF : (v + 1) * HALF] * mark, axis=0, keepdims=True)
            for i in range(FETCH // SEGS):
                value_ref[v, pl.ds(n * (FETCH // SEGS) + i, 1), :] = got[:, i * SEGS : (i + 1) * SEGS]
        return carry

    lax.fori_loop(0, ROWS * SEGS // FETCH, fetch, 0)

    flat = jnp.concatenate([target_ref[ch] for ch in range(4)] + [jnp.zeros((112, 256), F32)], axis=0)
    column_ref[...] = jnp.concatenate([flat[:, :128].T, flat[:, 128:].T], axis=0)
    picture_ref[...] = jnp.zeros((256, 128), F32)
    earlier = (iota((128, 128), 0) < iota((128, 128), 1)).astype(F32).astype(BF16)
    later = (iota((128, 128), 0) > iota((128, 128), 1)).astype(F32).astype(BF16)
    ones = jnp.ones((256, 128), BF16)
    earlier = jnp.concatenate([earlier, earlier, earlier], axis=0)
    later = jnp.concatenate([later, later], axis=0)
    pixel_x = iota((16, SEGS), 0).astype(F32) + 0.5

    def tile(t, carry):
        first = t * STEPS
        for k in range(STEPS):
            value = lambda v: value_ref[v, pl.ds(first + k, 1), :]
            offset_x = pixel_x - value(0)
            across_ref[k] = (-0.5 * LOG2E) * value(2) * offset_x * offset_x
            tilt_ref[k] = -LOG2E * value(3) * offset_x

        def forward(n, carry):
            for half in range(2):
                y = 2 * n + half
                pixel_y = y.astype(F32) + 0.5
                keep = jnp.ones((16, SEGS), F32)
                sums = [jnp.zeros((16, SEGS), F32) for _ in range(4)]
                at = pl.ds(pl.multiple_of(y * 16, 16), 16)
                for k in range(STEPS):
                    value = lambda v: value_ref[v, pl.ds(first + k, 1), :]
                    offset_y = pixel_y - value(1)
                    down = (-0.5 * LOG2E) * value(4) * offset_y * offset_y
                    fall = jnp.exp2(across_ref[k] + down + tilt_ref[k] * offset_y)
                    flow = fall * keep
                    weight = value(5) * flow
                    keep = keep - weight
                    for ch in range(4):
                        sums[ch] = sums[ch] + value(6 + ch) * weight
                    fall_ref[k, at, :] = fall
                    flow_ref[k, at, :] = flow
                keep_ref[at, :] = keep
                for ch in range(4):
                    sum_ref[ch, at, :] = sums[ch]
            return carry

        lax.fori_loop(0, 8, forward, 0, unroll=FORE)

        keep = keep_ref[...]
        logs = jnp.concatenate(split(jnp.log(keep), 3), axis=1)
        reach = jnp.exp(dot(logs, earlier))
        reach_ref[...] = reach
        spent = jnp.zeros((256, SEGS), F32)
        for ch in range(4):
            part = sum_ref[ch] * reach
            rendered = dot(jnp.concatenate(split(part, 2), axis=1), ones)
            here = iota((256, 128), 1) == ch * TILES + t
            wanted = jnp.sum(jnp.where(here, column_ref[...], 0.0), axis=1, keepdims=True)
            shade = 2.0 * (rendered - wanted)
            picture_ref[...] = jnp.where(here, rendered, picture_ref[...])
            shade_ref[ch] = shade
            spent = spent + shade * part
        rest = dot(jnp.concatenate(split(spent, 2), axis=1), later)
        behind_ref[...] = rest / (reach * keep)

        for k in reversed(range(STEPS)):
            value = lambda v: value_ref[v, pl.ds(first + k, 1), :]
            mean_y = jnp.broadcast_to(value(1), (8, SEGS))
            opacity = jnp.broadcast_to(value(5), (8, SEGS))
            colours = [jnp.broadcast_to(value(6 + ch), (8, SEGS)) for ch in range(4)]

            def backward(n, sums):
                zero, one, two, tints = sums
                zero, one, two, tints = list(zero), list(one), list(two), list(tints)
                for quarter in range(2):
                    y = 2 * n + quarter
                    offset_y = y.astype(F32) + 0.5 - mean_y
                    for half in range(2):
                        at = pl.ds(pl.multiple_of(y * 16 + half * 8, 8), 8)
                        shades = [shade_ref[ch, at, :] for ch in range(4)]
                        flow = flow_ref[k, at, :] * reach_ref[at, :]
                        lit = (shades[0] * colours[0] + shades[1] * colours[1]) + (
                            shades[2] * colours[2] + shades[3] * colours[3]
                        )
                        behind = behind_ref[at, :]
                        gap = lit - behind
                        behind_ref[at, :] = behind + opacity * fall_ref[k, at, :] * gap
                        grad = flow * gap
                        slope = grad * offset_y
                        zero[half] = zero[half] + grad
                        one[half] = one[half] + slope
                        two[half] = two[half] + slope * offset_y
                        for ch in range(4):
                            tints[ch] = tints[ch] + flow * shades[ch]
                return (tuple(zero), tuple(one), tuple(two), tuple(tints))

            blank = jnp.zeros((8, SEGS), F32)
            zero, one, two, tints = lax.fori_loop(
                0, 8, backward, ((blank,) * 2, (blank,) * 2, (blank,) * 2, (blank,) * 4), unroll=BACK
            )
            total = lambda x: jnp.sum(x, axis=0, keepdims=True)
            offset_x = pixel_x - value(0)
            near, far = offset_x[:8], offset_x[8:]
            sum_0 = total(zero[0] + zero[1])
            slope_x = (near * zero[0], far * zero[1])
            sum_x = total(slope_x[0] + slope_x[1])
            sum_xx = total(near * slope_x[0] + far * slope_x[1])
            sum_y = total(one[0] + one[1])
            sum_xy = total(near * one[0] + far * one[1])
            sum_yy = total(two[0] + two[1])
            opacity = value(5)
            grads = [
                opacity * (value(2) * sum_x + value(3) * sum_y),
                opacity * (value(4) * sum_y + value(3) * sum_x),
                -0.5 * opacity * sum_xx,
                -opacity * sum_xy,
                -0.5 * opacity * sum_yy,
                sum_0,
            ] + [opacity * total(tint) for tint in tints]
            for v in range(10):
                grad_ref[v, pl.ds(first + k, 1), :] = grads[v]
        return carry

    lax.fori_loop(0, TILES, tile, 0)

    picture = picture_ref[...]
    picture = jnp.concatenate([picture[:128].T, picture[128:].T], axis=1)
    for ch in range(4):
        image_ref[ch] = picture[ch * TILES : (ch + 1) * TILES, :]

    spread_ref[...] = jnp.zeros((10 * HALF, KEYS), F32)

    def spread(n, carry):
        at = pl.ds(pl.multiple_of(n * SPREAD, SPREAD), SPREAD)
        mark = mark_ref[:, at].astype(F32)
        heads, tails = [], []
        for v in range(10):
            count = SPREAD // SEGS
            grad = jnp.concatenate([grad_ref[v, pl.ds(count * n + i, 1), :] for i in range(count)], axis=1)
            head, tail = split(grad * mark, 2)
            heads.append(head)
            tails.append(tail)
        turned = turned_ref[at, :]
        both = jnp.concatenate([jnp.concatenate(heads, axis=0), jnp.concatenate(tails, axis=0)], axis=1)
        spread_ref[...] += dot(both, jnp.concatenate([turned, turned], axis=0))
        return carry

    lax.fori_loop(0, ROWS * SEGS // SPREAD, spread, 0)
    for c in range(WIRE):
        rows = []
        for h in range(2):
            for half in range(2):
                v = c + WIRE * h
                rows.append(spread_ref[v * HALF : (v + 1) * HALF, half * DEVS : (half + 1) * DEVS])
        out_ref[pl.ds(c, DEVS, stride=WIRE), :] = jnp.concatenate(rows, axis=0).T


def vmem():
    return pl.BlockSpec(memory_space=pltpu.VMEM)


def hbm():
    return pl.BlockSpec(memory_space=pltpu.HBM)


def smem():
    return pl.BlockSpec(memory_space=pltpu.SMEM)


def call(kernel, name, in_specs, outs, scratch, limit):
    return pl.pallas_call(
        kernel,
        name=name,
        out_shape=outs,
        in_specs=in_specs,
        out_specs=jax.tree.map(lambda _: vmem(), outs),
        scratch_shapes=scratch,
        compiler_params=pltpu.CompilerParams(vmem_limit_bytes=limit),
    )


def exchange(x):
    width = x.shape[0] * x.shape[1] // DEVS
    moved = lax.all_to_all(x.reshape(DEVS, 1, width), AXES, split_axis=0, concat_axis=0, tiled=True)
    return moved.reshape(x.shape)


def body(splat_params, list_owner, list_slot, list_length, target):
    shape = jax.ShapeDtypeStruct
    wire = shape((DEVS * WIRE, 128), F32)
    route = call(
        route_kernel, "route", [hbm(), hbm(), hbm()],
        (shape((DEVS, 128), jnp.int32), shape((ROWS, SEGS), F32), shape((ROWS, SEGS), F32)),
        [
            pltpu.SMEM(list_length.shape, jnp.int32), pltpu.VMEM((ROWS, SEGS), jnp.int32),
            pltpu.VMEM(list_slot.shape, jnp.int32), pltpu.SemaphoreType.DMA((3,)),
        ],
        ROUTE_LIMIT,
    )
    request, owners, ranks = route(list_length, list_owner.reshape(ROWS, SEGS), list_slot)
    asked = exchange(request)
    rows = splat_params.shape[1] // 8
    packed = pl.pallas_call(
        pack_kernel,
        name="pack",
        out_shape=shape((rows, 128), F32),
        in_specs=[hbm()],
        out_specs=hbm(),
        scratch_shapes=[
            pltpu.VMEM(splat_params.shape, F32), pltpu.VMEM((rows, 128), F32),
            pltpu.SemaphoreType.DMA((rows // STRETCH,)), pltpu.SemaphoreType.DMA,
        ],
        compiler_params=pltpu.CompilerParams(vmem_limit_bytes=61 << 20),
    )(splat_params)
    staging = [
        pltpu.SMEM((DEVS, 128), jnp.int32), pltpu.VMEM((DEVS, BLOCK * 128), BF16),
        pltpu.VMEM((DEVS * RANKS, 128), F32),
    ]
    table = pltpu.VMEM((rows, 128), F32)
    sems = pltpu.SemaphoreType.DMA((2,))
    numbers = shape((DEVS, 128), jnp.int32)
    groups = shape((DEVS // BLOCK * RANKS, DEVS), BF16)
    gather = call(gather_kernel, "gather", [vmem(), hbm()], (wire, numbers, groups), staging + [table, sems], 60 << 20)
    found, numbers, groups = gather(asked, packed)
    replies = exchange(found)
    entries = ROWS * SEGS
    marks = call(
        marks_kernel, "marks", [vmem(), vmem(), hbm()],
        (shape((KEYS, entries), BF16), shape((HALF, entries), BF16), shape((ROWS, SEGS), F32)), [], 16 << 20,
    )
    hot, mark, keys = marks(owners, ranks, numbers)
    field = pltpu.VMEM((256, SEGS), F32)
    deep = pltpu.VMEM((STEPS, 256, SEGS), F32)
    render = call(
        render_kernel, "render", [vmem()] * 5, (shape(target.shape, F32), wire),
        [
            pltpu.VMEM((entries, KEYS), BF16), pltpu.VMEM((10 * HALF, 3 * KEYS), BF16),
            pltpu.VMEM((10, ROWS, SEGS), F32), deep, deep, pltpu.VMEM((4, 256, SEGS), F32), field, field, field,
            pltpu.VMEM((4, 256, SEGS), F32), field, field,
            pltpu.VMEM((STEPS, 16, SEGS), F32), pltpu.VMEM((STEPS, 16, SEGS), F32),
            pltpu.VMEM((10, ROWS, SEGS), F32), pltpu.VMEM((10 * HALF, KEYS), F32),
        ],
        24 << 20,
    )
    images, outgoing = render(replies, hot, mark, keys, target)
    incoming = exchange(outgoing)
    scatter = pl.pallas_call(
        scatter_kernel,
        name="scatter",
        out_shape=shape(splat_params.shape, F32),
        in_specs=[vmem(), vmem(), vmem()],
        out_specs=hbm(),
        scratch_shapes=staging
        + [pltpu.VMEM((DEVS // BLOCK, 128, 128), F32), pltpu.VMEM(splat_params.shape, F32), sems]
        + [table] * CHAINS,
        compiler_params=pltpu.CompilerParams(vmem_limit_bytes=56 << 20),
    )
    return (images, scatter(numbers, groups, incoming))


def solution(mesh):
    in_specs = (
        P(None, AXES),
        P(AXES, None, None),
        P(AXES, None),
        P(AXES),
        P(None, AXES, None),
    )
    out_specs = (P(None, AXES, None), P(None, AXES))
    return jax.shard_map(body, mesh=mesh, in_specs=in_specs, out_specs=out_specs, check_vma=False)
```

```python
import jax
import jax.numpy as jnp
from jax import lax
from jax.experimental import pallas as pl
from jax.experimental.pallas import tpu as pltpu
from jax.sharding import PartitionSpec as P

AXES = ("row", "col")
DEVS = 128
RANKS = 64
TILES = 4
SEGS = 128
STEPS = 8
ROWS = TILES * STEPS
WIRE = 5
GROUP = 16
BLOCK = 16
TIERS = ((0, 48), (48, RANKS))
LOOK_UNROLL = 2
ADD_UNROLL = 1
STRETCH = 1024
UNROLL = 4
ROUTE_LIMIT = 63 << 20
SPLIT_UNROLL = 2
FORE = 4
FETCH = 4096
SPREAD = 4096
BACK = 8
CHAINS = 6
LOG2E = 1.4426950408889634
F32 = jnp.float32
BF16 = jnp.bfloat16


def iota(shape, dim):
    return lax.broadcasted_iota(jnp.int32, shape, dim)


def dot(a, b):
    return lax.dot_general(a, b, (((1,), (0,)), ((), ())), preferred_element_type=F32)


def dot_nt(a, b):
    return lax.dot_general(a, b, (((1,), (1,)), ((), ())), preferred_element_type=F32)


def split(x, parts):
    out = []
    for _ in range(parts - 1):
        head = x.astype(BF16)
        out.append(head)
        x = x - head.astype(F32)
    out.append(x.astype(BF16))
    return out


def onehot_rows(row, count):
    wide = jnp.broadcast_to(row, (count, row.shape[1]))
    return wide == iota(wide.shape, 0).astype(F32)


def route_kernel(
    length_hbm, owner_hbm, slot_hbm, request_ref, owner_out, rank_out, length_ref, owner_ref, slot_ref, sems
):
    pairs = ((length_hbm, length_ref), (owner_hbm, owner_ref), (slot_hbm, slot_ref))
    copies = [pltpu.make_async_copy(a, b, sems.at[i]) for i, (a, b) in enumerate(pairs)]
    for copy in copies:
        copy.start()
    for copy in copies:
        copy.wait()
    lane = iota((STEPS, SEGS), 1)
    step = iota((STEPS, SEGS), 0)
    picks = (lane & (STEPS - 1)) == step
    pieces = []
    for r in range(STEPS):
        rows = []
        slot_rows = []
        for t in range(TILES):
            own = jnp.broadcast_to(owner_ref[t * STEPS + r : t * STEPS + r + 1, :], (STEPS, SEGS))
            rows.append(jnp.where(picks, own, 0))
            slot = slot_ref[t : t + 1, r * SEGS : (r + 1) * SEGS]
            slot_rows.append(jnp.where(picks, jnp.broadcast_to(slot, (STEPS, SEGS)), 0))
        rows += [s >> 8 for s in slot_rows] + [s & 255 for s in slot_rows]
        pieces.append(jnp.concatenate(rows, axis=0).astype(F32).astype(BF16))
    spread = jnp.concatenate(pieces, axis=1)
    place = ((iota((STEPS * SEGS, SEGS), 0) >> 3) == iota((STEPS * SEGS, SEGS), 1)).astype(F32)
    moved = dot(spread, place.astype(BF16))
    lane = iota((ROWS, SEGS), 1)
    row = iota((ROWS, SEGS), 0)
    length = jnp.full((ROWS, SEGS), length_ref[0], jnp.int32)
    for t in range(1, TILES):
        length = jnp.where((row >> 3) == t, length_ref[t], length)
    live = (lane * STEPS + (row & (STEPS - 1))) < length
    owners = jnp.where(live, moved[0:ROWS], -1.0)
    high = moved[ROWS : 2 * ROWS]
    low = moved[2 * ROWS : 3 * ROWS]
    owner_out[...] = owners
    before = (iota((256, 256), 0) < iota((256, 256), 1)).astype(F32).astype(BF16)
    before = jnp.concatenate([before, jnp.ones((256, 256), BF16)], axis=1)
    rank_of = (iota((2 * RANKS, 256), 0) & (RANKS - 1)).astype(F32)
    upper = iota((2 * RANKS, 256), 0) < RANKS
    carry = jnp.zeros((DEVS, 256), F32)
    request = jnp.zeros((2 * RANKS, DEVS), F32)
    for n in range(ROWS // 2):
        pair = lambda x: jnp.concatenate([x[2 * n : 2 * n + 1], x[2 * n + 1 : 2 * n + 2]], axis=1)
        hot = onehot_rows(pair(owners), DEVS)
        hot16 = hot.astype(F32).astype(BF16)
        counted = dot(hot16, before)
        rank = jnp.sum(jnp.where(hot, counted[:, :256] + carry, 0.0), axis=0, keepdims=True)
        carry = carry + counted[:, 256:]
        rank_out[2 * n : 2 * n + 1, :] = rank[:, :SEGS]
        rank_out[2 * n + 1 : 2 * n + 2, :] = rank[:, SEGS:]
        values = jnp.where(upper, pair(high), pair(low))
        values = jnp.where(rank_of == rank, values, 0.0)
        request = request + dot_nt(values.astype(BF16), hot16)
    slots = request[:RANKS] * 256.0 + request[RANKS:]
    slots = jnp.concatenate([slots, slots], axis=0).T
    full = jnp.where(iota((DEVS, DEVS), 1) < RANKS, slots, carry[:, :DEVS])
    request_ref[...] = full.astype(jnp.int32)


def pack_kernel(params_hbm, out_hbm, params_ref, out_ref, in_sems, out_sem):
    width = 8 * STRETCH
    steps = params_ref.shape[1] // width
    pad = jnp.zeros((GROUP - 10, 128), F32)

    def read(i):
        at = pl.ds(pl.multiple_of(i * width, width), width)
        return pltpu.make_async_copy(params_hbm.at[:, at], params_ref.at[:, at], in_sems.at[i])

    for i in range(steps):
        read(i).start()

    def step(i, carry):
        read(i).wait()
        mine_ref = params_ref.at[:, pl.ds(pl.multiple_of(i * width, width), width)]
        rows = pl.ds(pl.multiple_of(i * STRETCH, STRETCH), STRETCH)
        done_ref = out_ref.at[rows]
        for n in range(STRETCH // 128):
            blocks = []
            for g in range(8):
                at = g * STRETCH + n * 128
                blocks += [mine_ref[:, at : at + 128], pad]
            done_ref[n * 128 : (n + 1) * 128, :] = jnp.concatenate(blocks, axis=0).T
        pltpu.make_async_copy(done_ref, out_hbm.at[rows], out_sem).start()
        return carry

    lax.fori_loop(0, steps, step, 0)
    pltpu.make_async_copy(out_ref, out_hbm, out_sem).wait()


def bit_clear(shift):
    return (iota((RANKS, 128), 1) & shift) == 0


def merge_groups(xs):
    xs = [xs[q] for q in (0, 4, 2, 6, 1, 5, 3, 7)]
    for shift in (16, 32, 64):
        half = len(xs) // 2
        low = bit_clear(shift)
        xs = [
            jnp.where(low, x, y) + pltpu.roll(jnp.where(low, y, x), shift, 1)
            for x, y in zip(xs[:half], xs[half:])
        ]
    return xs[0]


def spread_groups(x):
    xs = [x]
    for shift in (64, 32, 16):
        low = bit_clear(shift)
        nexts = []
        for y in xs:
            z = pltpu.roll(y, shift, 1)
            nexts += [jnp.where(low, y, z), jnp.where(low, z, y)]
        xs = nexts
    return xs


def prepare(asked_ref, row_number_ref, number_ref, number_sem, group_ref):
    asked = asked_ref[...]
    lane = iota((DEVS, 128), 1)
    row = ((asked >> 13) << 10) | (asked & (STRETCH - 1))
    row_number_ref[...] = jnp.where(lane < RANKS, row, asked)
    copy = pltpu.make_async_copy(row_number_ref, number_ref, number_sem)
    copy.start()
    group = jnp.where(lane < pltpu.roll(asked, RANKS, 1), (asked >> 10) & 7, 8)
    groups = group.astype(F32).T[:RANKS]
    for b in range(DEVS // BLOCK):
        turned = groups if b == 0 else pltpu.roll(groups, DEVS - b * BLOCK, 1)
        group_ref[b * RANKS : (b + 1) * RANKS, :] = turned.astype(BF16)
    return copy


def fill_widen(widen_ref):
    for n in range(BLOCK):
        widen_ref[:, n * 128 : (n + 1) * 128] = (iota((DEVS, 128), 0) == n).astype(F32).astype(BF16)


def wide_groups(group_ref, widen_ref, b):
    at = pl.ds(pl.multiple_of(b * RANKS, RANKS), RANKS)
    return dot(group_ref[at, :], widen_ref[...])


def gather_kernel(
    asked_ref, table_hbm, out_ref, row_number_ref, group_ref, number_ref, widen_ref, row_ref, table_ref, sems
):
    left = iota((WIRE, 128), 1) < RANKS
    fill = pltpu.make_async_copy(table_hbm, table_ref, sems.at[1])
    fill.start()
    copy = prepare(asked_ref, row_number_ref, number_ref, sems.at[0], group_ref)
    fill_widen(widen_ref)
    copy.wait()
    fill.wait()

    def source(src, carry):
        mine_ref = row_ref.at[pl.ds(pl.multiple_of(src * RANKS, RANKS), RANKS)]
        count = number_ref[src, RANKS]
        for low, high in TIERS:

            @pl.when((count > low) & (count <= high))
            def _():
                for rank in range(high):
                    mine_ref[rank : rank + 1, :] = table_ref[pl.ds(number_ref[src, rank], 1), :]

        return carry

    lax.fori_loop(0, DEVS, source, 0, unroll=LOOK_UNROLL)

    def block(b, carry):
        base = pl.multiple_of(b * BLOCK * RANKS, BLOCK * RANKS)
        groups = wide_groups(group_ref, widen_ref, b)
        lane_group = (iota((RANKS, 128), 1) >> 4).astype(F32)
        halves = []
        for half in range(2):
            picked = []
            for n in range(half * 8, half * 8 + 8):
                rows = row_ref[pl.ds(base + n * RANKS, RANKS), :]
                picked.append(jnp.where(lane_group == groups[:, n * 128 : (n + 1) * 128], rows, 0.0))
            halves.append(merge_groups(picked))
        turned = jnp.concatenate(halves, axis=0).T
        evens, odds = [], []
        for q in range(8):
            first = turned[q * GROUP : q * GROUP + WIRE]
            second = turned[q * GROUP + WIRE : q * GROUP + 2 * WIRE]
            evens.append(jnp.where(left, first, pltpu.roll(second, RANKS, 1)))
            odds.append(jnp.where(left, pltpu.roll(first, RANKS, 1), second))
        at = pl.multiple_of(b * BLOCK * WIRE, 8)
        out_ref[pl.ds(at, BLOCK * WIRE), :] = jnp.concatenate(evens + odds, axis=0)
        return carry

    lax.fori_loop(0, DEVS // BLOCK, block, 0, unroll=UNROLL)


def scatter_kernel(
    row_number_ref, group_ref, wire_ref, out_hbm, number_ref, widen_ref, row_ref, turn_ref, out_ref, sems, *totals
):
    left = iota((WIRE, 128), 1) < RANKS
    table_rows = totals[0].shape[0]
    copy = pltpu.make_async_copy(row_number_ref, number_ref, sems.at[0])
    copy.start()
    fill_widen(widen_ref)
    turn_ref[...] = jnp.zeros(turn_ref.shape, F32)

    def clear(i, carry):
        for ref in totals:
            ref[pl.ds(pl.multiple_of(i * 256, 256), 256), :] = jnp.zeros((256, 128), F32)
        return carry

    lax.fori_loop(0, table_rows // 256, clear, 0)

    def block(b, carry):
        at = pl.multiple_of(b * BLOCK * WIRE, 8)
        base = pl.multiple_of(b * BLOCK * RANKS, BLOCK * RANKS)
        wire = wire_ref[pl.ds(at, BLOCK * WIRE), :]
        mine_ref = turn_ref.at[b]
        for q in range(8):
            even = wire[q * WIRE : (q + 1) * WIRE]
            odd = wire[(q + 8) * WIRE : (q + 9) * WIRE]
            mine_ref[q * GROUP : q * GROUP + WIRE, :] = jnp.where(left, even, pltpu.roll(odd, RANKS, 1))
            mine_ref[q * GROUP + WIRE : q * GROUP + 2 * WIRE, :] = jnp.where(left, pltpu.roll(even, RANKS, 1), odd)
        turned = mine_ref[...].T
        groups = wide_groups(group_ref, widen_ref, b)
        lane_group = (iota((RANKS, 128), 1) >> 4).astype(F32)
        for half in range(2):
            spreads = spread_groups(turned[half * RANKS : (half + 1) * RANKS])
            for q in range(8):
                n = half * 8 + q
                row_ref[pl.ds(base + n * RANKS, RANKS), :] = jnp.where(
                    lane_group == groups[:, n * 128 : (n + 1) * 128], spreads[q], 0.0
                )
        return carry

    lax.fori_loop(0, DEVS // BLOCK, block, 0, unroll=SPLIT_UNROLL)
    copy.wait()

    def source(src, carry):
        mine_ref = row_ref.at[pl.ds(pl.multiple_of(src * RANKS, RANKS), RANKS)]
        count = number_ref[src, RANKS]
        for low, high in TIERS:

            @pl.when((count > low) & (count <= high))
            def _():
                for start in range(0, high, CHAINS):
                    news = []
                    for i, ref in enumerate(totals[: high - start]):
                        row = number_ref[src, start + i]
                        news.append((row, mine_ref[start + i : start + i + 1, :] + ref[pl.ds(row, 1), :]))
                    for ref, (row, total) in zip(totals, news):
                        ref[pl.ds(row, 1), :] = total

        return carry

    lax.fori_loop(0, DEVS, source, 0, unroll=ADD_UNROLL)

    def close(i, carry):
        base = pl.multiple_of(i * STRETCH, STRETCH)
        lanes = pl.ds(pl.multiple_of(i * 8 * STRETCH, 8 * STRETCH), 8 * STRETCH)
        mine_ref = out_ref.at[:, lanes]
        for n in range(STRETCH // 128):
            at = pl.ds(base + n * 128, 128)
            total = totals[0][at, :]
            for ref in totals[1:]:
                total = total + ref[at, :]
            total = total.T
            for g in range(8):
                spot = g * STRETCH + n * 128
                mine_ref[:, spot : spot + 128] = total[g * GROUP : g * GROUP + 10]
        pltpu.make_async_copy(mine_ref, out_hbm.at[:, lanes], sems.at[1]).start()
        return carry

    lax.fori_loop(0, table_rows // STRETCH, close, 0)
    pltpu.make_async_copy(out_ref, out_hbm, sems.at[1]).wait()


HALF = RANKS // 2
KEYS = 2 * DEVS


def marks_kernel(owner_ref, rank_ref, after_ref, hot_ref, mark_ref, key_ref):
    rank = rank_ref[...].astype(jnp.int32)
    owner = owner_ref[...]
    key = jnp.where(owner < 0.0, -1.0, owner + ((rank >> 5) * DEVS).astype(F32))
    rest = (rank & (HALF - 1)).astype(F32)
    key_ref[...] = key
    for n in range(ROWS):
        at = slice(n * SEGS, (n + 1) * SEGS)
        hot_ref[:, at] = onehot_rows(key[n : n + 1], KEYS).astype(F32).astype(BF16)
        mark_ref[:, at] = onehot_rows(rest[n : n + 1], HALF).astype(F32).astype(BF16)


def render_kernel(
    wire_ref, hot_ref, mark_ref, key_ref, target_ref, image_ref, out_ref,
    turned_ref,    left_ref, value_ref, fall_ref, flow_ref, sum_ref, keep_ref, reach_ref, behind_ref,
    shade_ref, column_ref, picture_ref, across_ref, tilt_ref, grad_ref, spread_ref,
):
    for c in range(WIRE):
        block = wire_ref[pl.ds(c, DEVS, stride=WIRE), :].T
        parts = split(block, 3)
        for h in range(2):
            v = c + WIRE * h
            for half in range(2):
                rows = slice(h * RANKS + half * HALF, h * RANKS + (half + 1) * HALF)
                for n in range(3):
                    at = n * KEYS + half * DEVS
                    left_ref[v * HALF : (v + 1) * HALF, at : at + DEVS] = parts[n][rows]

    columns = jnp.concatenate([key_ref[...], jnp.zeros((128 - ROWS, SEGS), F32)], axis=0).T
    for n in range(ROWS):
        column = jnp.broadcast_to(columns[:, n : n + 1], (SEGS, KEYS))
        turned_ref[n * SEGS : (n + 1) * SEGS, :] = (column == iota((SEGS, KEYS), 1).astype(F32)).astype(F32).astype(BF16)

    def fetch(n, carry):
        at = pl.ds(pl.multiple_of(n * FETCH, FETCH), FETCH)
        hot = hot_ref[:, at]
        mark = mark_ref[:, at].astype(F32)
        found = dot(left_ref[...], jnp.concatenate([hot, hot, hot], axis=0))
        for v in range(10):
            got = jnp.sum(found[v * HALF : (v + 1) * HALF] * mark, axis=0, keepdims=True)
            for i in range(FETCH // SEGS):
                value_ref[v, pl.ds(n * (FETCH // SEGS) + i, 1), :] = got[:, i * SEGS : (i + 1) * SEGS]
        return carry

    lax.fori_loop(0, ROWS * SEGS // FETCH, fetch, 0)

    flat = jnp.concatenate([target_ref[ch] for ch in range(4)] + [jnp.zeros((112, 256), F32)], axis=0)
    column_ref[...] = jnp.concatenate([flat[:, :128].T, flat[:, 128:].T], axis=0)
    picture_ref[...] = jnp.zeros((256, 128), F32)
    earlier = (iota((128, 128), 0) < iota((128, 128), 1)).astype(F32).astype(BF16)
    later = (iota((128, 128), 0) > iota((128, 128), 1)).astype(F32).astype(BF16)
    ones = jnp.ones((256, 128), BF16)
    earlier = jnp.concatenate([earlier, earlier, earlier], axis=0)
    later = jnp.concatenate([later, later], axis=0)
    pixel_x = iota((16, SEGS), 0).astype(F32) + 0.5

    def tile(t, carry):
        first = t * STEPS
        for k in range(STEPS):
            value = lambda v: value_ref[v, pl.ds(first + k, 1), :]
            offset_x = pixel_x - value(0)
            across_ref[k] = (-0.5 * LOG2E) * value(2) * offset_x * offset_x
            tilt_ref[k] = -LOG2E * value(3) * offset_x

        def forward(n, carry):
            for half in range(2):
                y = 2 * n + half
                pixel_y = y.astype(F32) + 0.5
                keep = jnp.ones((16, SEGS), F32)
                sums = [jnp.zeros((16, SEGS), F32) for _ in range(4)]
                at = pl.ds(pl.multiple_of(y * 16, 16), 16)
                for k in range(STEPS):
                    value = lambda v: value_ref[v, pl.ds(first + k, 1), :]
                    offset_y = pixel_y - value(1)
                    down = (-0.5 * LOG2E) * value(4) * offset_y * offset_y
                    fall = jnp.exp2(across_ref[k] + down + tilt_ref[k] * offset_y)
                    flow = fall * keep
                    weight = value(5) * flow
                    keep = keep - weight
                    for ch in range(4):
                        sums[ch] = sums[ch] + value(6 + ch) * weight
                    fall_ref[k, at, :] = fall
                    flow_ref[k, at, :] = flow
                keep_ref[at, :] = keep
                for ch in range(4):
                    sum_ref[ch, at, :] = sums[ch]
            return carry

        lax.fori_loop(0, 8, forward, 0, unroll=FORE)

        keep = keep_ref[...]
        logs = jnp.concatenate(split(jnp.log(keep), 3), axis=1)
        reach = jnp.exp(dot(logs, earlier))
        reach_ref[...] = reach
        spent = jnp.zeros((256, SEGS), F32)
        for ch in range(4):
            part = sum_ref[ch] * reach
            rendered = dot(jnp.concatenate(split(part, 2), axis=1), ones)
            here = iota((256, 128), 1) == ch * TILES + t
            wanted = jnp.sum(jnp.where(here, column_ref[...], 0.0), axis=1, keepdims=True)
            shade = 2.0 * (rendered - wanted)
            picture_ref[...] = jnp.where(here, rendered, picture_ref[...])
            shade_ref[ch] = shade
            spent = spent + shade * part
        rest = dot(jnp.concatenate(split(spent, 2), axis=1), later)
        behind_ref[...] = rest / (reach * keep)

        for k in reversed(range(STEPS)):
            value = lambda v: value_ref[v, pl.ds(first + k, 1), :]
            mean_y = jnp.broadcast_to(value(1), (8, SEGS))
            opacity = jnp.broadcast_to(value(5), (8, SEGS))
            colours = [jnp.broadcast_to(value(6 + ch), (8, SEGS)) for ch in range(4)]

            def backward(n, sums):
                zero, one, two, tints = sums
                zero, one, two, tints = list(zero), list(one), list(two), list(tints)
                for quarter in range(2):
                    y = 2 * n + quarter
                    offset_y = y.astype(F32) + 0.5 - mean_y
                    for half in range(2):
                        at = pl.ds(pl.multiple_of(y * 16 + half * 8, 8), 8)
                        shades = [shade_ref[ch, at, :] for ch in range(4)]
                        flow = flow_ref[k, at, :] * reach_ref[at, :]
                        lit = (shades[0] * colours[0] + shades[1] * colours[1]) + (
                            shades[2] * colours[2] + shades[3] * colours[3]
                        )
                        behind = behind_ref[at, :]
                        gap = lit - behind
                        behind_ref[at, :] = behind + opacity * fall_ref[k, at, :] * gap
                        grad = flow * gap
                        slope = grad * offset_y
                        zero[half] = zero[half] + grad
                        one[half] = one[half] + slope
                        two[half] = two[half] + slope * offset_y
                        for ch in range(4):
                            tints[ch] = tints[ch] + flow * shades[ch]
                return (tuple(zero), tuple(one), tuple(two), tuple(tints))

            blank = jnp.zeros((8, SEGS), F32)
            zero, one, two, tints = lax.fori_loop(
                0, 8, backward, ((blank,) * 2, (blank,) * 2, (blank,) * 2, (blank,) * 4), unroll=BACK
            )
            total = lambda x: jnp.sum(x, axis=0, keepdims=True)
            offset_x = pixel_x - value(0)
            near, far = offset_x[:8], offset_x[8:]
            sum_0 = total(zero[0] + zero[1])
            slope_x = (near * zero[0], far * zero[1])
            sum_x = total(slope_x[0] + slope_x[1])
            sum_xx = total(near * slope_x[0] + far * slope_x[1])
            sum_y = total(one[0] + one[1])
            sum_xy = total(near * one[0] + far * one[1])
            sum_yy = total(two[0] + two[1])
            opacity = value(5)
            grads = [
                opacity * (value(2) * sum_x + value(3) * sum_y),
                opacity * (value(4) * sum_y + value(3) * sum_x),
                -0.5 * opacity * sum_xx,
                -opacity * sum_xy,
                -0.5 * opacity * sum_yy,
                sum_0,
            ] + [opacity * total(tint) for tint in tints]
            for v in range(10):
                grad_ref[v, pl.ds(first + k, 1), :] = grads[v]
        return carry

    lax.fori_loop(0, TILES, tile, 0)

    picture = picture_ref[...]
    picture = jnp.concatenate([picture[:128].T, picture[128:].T], axis=1)
    for ch in range(4):
        image_ref[ch] = picture[ch * TILES : (ch + 1) * TILES, :]

    spread_ref[...] = jnp.zeros((10 * HALF, KEYS), F32)

    def spread(n, carry):
        at = pl.ds(pl.multiple_of(n * SPREAD, SPREAD), SPREAD)
        mark = mark_ref[:, at].astype(F32)
        heads, tails = [], []
        for v in range(10):
            count = SPREAD // SEGS
            grad = jnp.concatenate([grad_ref[v, pl.ds(count * n + i, 1), :] for i in range(count)], axis=1)
            head, tail = split(grad * mark, 2)
            heads.append(head)
            tails.append(tail)
        turned = turned_ref[at, :]
        both = jnp.concatenate([jnp.concatenate(heads, axis=0), jnp.concatenate(tails, axis=0)], axis=1)
        spread_ref[...] += dot(both, jnp.concatenate([turned, turned], axis=0))
        return carry

    lax.fori_loop(0, ROWS * SEGS // SPREAD, spread, 0)
    for c in range(WIRE):
        rows = []
        for h in range(2):
            for half in range(2):
                v = c + WIRE * h
                rows.append(spread_ref[v * HALF : (v + 1) * HALF, half * DEVS : (half + 1) * DEVS])
        out_ref[pl.ds(c, DEVS, stride=WIRE), :] = jnp.concatenate(rows, axis=0).T


def vmem():
    return pl.BlockSpec(memory_space=pltpu.VMEM)


def hbm():
    return pl.BlockSpec(memory_space=pltpu.HBM)


def smem():
    return pl.BlockSpec(memory_space=pltpu.SMEM)


def call(kernel, name, in_specs, outs, scratch, limit):
    return pl.pallas_call(
        kernel,
        name=name,
        out_shape=outs,
        in_specs=in_specs,
        out_specs=jax.tree.map(lambda _: vmem(), outs),
        scratch_shapes=scratch,
        compiler_params=pltpu.CompilerParams(vmem_limit_bytes=limit),
    )


def exchange(x):
    width = x.shape[0] * x.shape[1] // DEVS
    moved = lax.all_to_all(x.reshape(DEVS, 1, width), AXES, split_axis=0, concat_axis=0, tiled=True)
    return moved.reshape(x.shape)


def body(splat_params, list_owner, list_slot, list_length, target):
    shape = jax.ShapeDtypeStruct
    wire = shape((DEVS * WIRE, 128), F32)
    route = call(
        route_kernel, "route", [hbm(), hbm(), hbm()],
        (shape((DEVS, 128), jnp.int32), shape((ROWS, SEGS), F32), shape((ROWS, SEGS), F32)),
        [
            pltpu.SMEM(list_length.shape, jnp.int32), pltpu.VMEM((ROWS, SEGS), jnp.int32),
            pltpu.VMEM(list_slot.shape, jnp.int32), pltpu.SemaphoreType.DMA((3,)),
        ],
        ROUTE_LIMIT,
    )
    request, owners, ranks = route(list_length, list_owner.reshape(ROWS, SEGS), list_slot)
    asked = exchange(request)
    rows = splat_params.shape[1] // 8
    packed = pl.pallas_call(
        pack_kernel,
        name="pack",
        out_shape=shape((rows, 128), F32),
        in_specs=[hbm()],
        out_specs=hbm(),
        scratch_shapes=[
            pltpu.VMEM(splat_params.shape, F32), pltpu.VMEM((rows, 128), F32),
            pltpu.SemaphoreType.DMA((rows // STRETCH,)), pltpu.SemaphoreType.DMA,
        ],
        compiler_params=pltpu.CompilerParams(vmem_limit_bytes=61 << 20),
    )(splat_params)
    staging = [
        pltpu.SMEM((DEVS, 128), jnp.int32), pltpu.VMEM((DEVS, BLOCK * 128), BF16),
        pltpu.VMEM((DEVS * RANKS, 128), F32),
    ]
    table = pltpu.VMEM((rows, 128), F32)
    sems = pltpu.SemaphoreType.DMA((2,))
    numbers = shape((DEVS, 128), jnp.int32)
    groups = shape((DEVS // BLOCK * RANKS, DEVS), BF16)
    gather = call(gather_kernel, "gather", [vmem(), hbm()], (wire, numbers, groups), staging + [table, sems], 60 << 20)
    found, numbers, groups = gather(asked, packed)
    replies = exchange(found)
    entries = ROWS * SEGS
    marks = call(
        marks_kernel, "marks", [vmem(), vmem(), hbm()],
        (shape((KEYS, entries), BF16), shape((HALF, entries), BF16), shape((ROWS, SEGS), F32)), [], 16 << 20,
    )
    hot, mark, keys = marks(owners, ranks, numbers)
    field = pltpu.VMEM((256, SEGS), F32)
    deep = pltpu.VMEM((STEPS, 256, SEGS), F32)
    render = call(
        render_kernel, "render", [vmem()] * 5, (shape(target.shape, F32), wire),
        [
            pltpu.VMEM((entries, KEYS), BF16), pltpu.VMEM((10 * HALF, 3 * KEYS), BF16),
            pltpu.VMEM((10, ROWS, SEGS), F32), deep, deep, pltpu.VMEM((4, 256, SEGS), F32), field, field, field,
            pltpu.VMEM((4, 256, SEGS), F32), field, field,
            pltpu.VMEM((STEPS, 16, SEGS), F32), pltpu.VMEM((STEPS, 16, SEGS), F32),
            pltpu.VMEM((10, ROWS, SEGS), F32), pltpu.VMEM((10 * HALF, KEYS), F32),
        ],
        24 << 20,
    )
    images, outgoing = render(replies, hot, mark, keys, target)
    incoming = exchange(outgoing)
    scatter = pl.pallas_call(
        scatter_kernel,
        name="scatter",
        out_shape=shape(splat_params.shape, F32),
        in_specs=[vmem(), vmem(), vmem()],
        out_specs=hbm(),
        scratch_shapes=staging
        + [pltpu.VMEM((DEVS // BLOCK, 128, 128), F32), pltpu.VMEM(splat_params.shape, F32), sems]
        + [table] * CHAINS,
        compiler_params=pltpu.CompilerParams(vmem_limit_bytes=44 << 20),
    )
    return (images, scatter(numbers, groups, incoming))


def solution(mesh):
    in_specs = (
        P(None, AXES),
        P(AXES, None, None),
        P(AXES, None),
        P(AXES),
        P(None, AXES, None),
    )
    out_specs = (P(None, AXES, None), P(None, AXES))
    return jax.shard_map(body, mesh=mesh, in_specs=in_specs, out_specs=out_specs, check_vma=False)
```

```python
import jax
import jax.numpy as jnp
from jax import lax
from jax.experimental import pallas as pl
from jax.experimental.pallas import tpu as pltpu
from jax.sharding import PartitionSpec as P

AXES = ("row", "col")
DEVS = 128
RANKS = 64
TILES = 4
SEGS = 128
STEPS = 8
ROWS = TILES * STEPS
WIRE = 5
GROUP = 16
BLOCK = 16
TIERS = ((0, 48), (48, RANKS))
LOOK_UNROLL = 2
ADD_UNROLL = 1
STRETCH = 1024
UNROLL = 4
ROUTE_LIMIT = 63 << 20
SPLIT_UNROLL = 2
FORE = 4
FETCH = 4096
SPREAD = 4096
BACK = 8
CHAINS = 6
LOG2E = 1.4426950408889634
F32 = jnp.float32
BF16 = jnp.bfloat16


def iota(shape, dim):
    return lax.broadcasted_iota(jnp.int32, shape, dim)


def dot(a, b):
    return lax.dot_general(a, b, (((1,), (0,)), ((), ())), preferred_element_type=F32)


def dot_nt(a, b):
    return lax.dot_general(a, b, (((1,), (1,)), ((), ())), preferred_element_type=F32)


def split(x, parts):
    out = []
    for _ in range(parts - 1):
        head = x.astype(BF16)
        out.append(head)
        x = x - head.astype(F32)
    out.append(x.astype(BF16))
    return out


def onehot_rows(row, count):
    wide = jnp.broadcast_to(row, (count, row.shape[1]))
    return wide == iota(wide.shape, 0).astype(F32)


def route_kernel(
    length_hbm, owner_hbm, slot_hbm, request_ref, owner_out, rank_out, length_ref, owner_ref, slot_ref, sems
):
    pairs = ((length_hbm, length_ref), (owner_hbm, owner_ref), (slot_hbm, slot_ref))
    copies = [pltpu.make_async_copy(a, b, sems.at[i]) for i, (a, b) in enumerate(pairs)]
    for copy in copies:
        copy.start()
    for copy in copies:
        copy.wait()
    lane = iota((STEPS, SEGS), 1)
    step = iota((STEPS, SEGS), 0)
    picks = (lane & (STEPS - 1)) == step
    pieces = []
    for r in range(STEPS):
        rows = []
        slot_rows = []
        for t in range(TILES):
            own = jnp.broadcast_to(owner_ref[t * STEPS + r : t * STEPS + r + 1, :], (STEPS, SEGS))
            rows.append(jnp.where(picks, own, 0))
            slot = slot_ref[t : t + 1, r * SEGS : (r + 1) * SEGS]
            slot_rows.append(jnp.where(picks, jnp.broadcast_to(slot, (STEPS, SEGS)), 0))
        rows += [s >> 8 for s in slot_rows] + [s & 255 for s in slot_rows]
        pieces.append(jnp.concatenate(rows, axis=0).astype(F32).astype(BF16))
    spread = jnp.concatenate(pieces, axis=1)
    place = ((iota((STEPS * SEGS, SEGS), 0) >> 3) == iota((STEPS * SEGS, SEGS), 1)).astype(F32)
    moved = dot(spread, place.astype(BF16))
    lane = iota((ROWS, SEGS), 1)
    row = iota((ROWS, SEGS), 0)
    length = jnp.full((ROWS, SEGS), length_ref[0], jnp.int32)
    for t in range(1, TILES):
        length = jnp.where((row >> 3) == t, length_ref[t], length)
    live = (lane * STEPS + (row & (STEPS - 1))) < length
    owners = jnp.where(live, moved[0:ROWS], -1.0)
    high = moved[ROWS : 2 * ROWS]
    low = moved[2 * ROWS : 3 * ROWS]
    owner_out[...] = owners
    before = (iota((256, 256), 0) < iota((256, 256), 1)).astype(F32).astype(BF16)
    before = jnp.concatenate([before, jnp.ones((256, 256), BF16)], axis=1)
    rank_of = (iota((2 * RANKS, 256), 0) & (RANKS - 1)).astype(F32)
    upper = iota((2 * RANKS, 256), 0) < RANKS
    carry = jnp.zeros((DEVS, 256), F32)
    request = jnp.zeros((2 * RANKS, DEVS), F32)
    for n in range(ROWS // 2):
        pair = lambda x: jnp.concatenate([x[2 * n : 2 * n + 1], x[2 * n + 1 : 2 * n + 2]], axis=1)
        hot = onehot_rows(pair(owners), DEVS)
        hot16 = hot.astype(F32).astype(BF16)
        counted = dot(hot16, before)
        rank = jnp.sum(jnp.where(hot, counted[:, :256] + carry, 0.0), axis=0, keepdims=True)
        carry = carry + counted[:, 256:]
        rank_out[2 * n : 2 * n + 1, :] = rank[:, :SEGS]
        rank_out[2 * n + 1 : 2 * n + 2, :] = rank[:, SEGS:]
        values = jnp.where(upper, pair(high), pair(low))
        values = jnp.where(rank_of == rank, values, 0.0)
        request = request + dot_nt(values.astype(BF16), hot16)
    slots = request[:RANKS] * 256.0 + request[RANKS:]
    slots = jnp.concatenate([slots, slots], axis=0).T
    full = jnp.where(iota((DEVS, DEVS), 1) < RANKS, slots, carry[:, :DEVS])
    request_ref[...] = full.astype(jnp.int32)


def pack_kernel(params_hbm, out_hbm, params_ref, out_ref, in_sems, out_sem):
    width = 8 * STRETCH
    steps = params_ref.shape[1] // width
    pad = jnp.zeros((GROUP - 10, 128), F32)

    def read(i):
        at = pl.ds(pl.multiple_of(i * width, width), width)
        return pltpu.make_async_copy(params_hbm.at[:, at], params_ref.at[:, at], in_sems.at[i])

    for i in range(steps):
        read(i).start()

    def step(i, carry):
        read(i).wait()
        mine_ref = params_ref.at[:, pl.ds(pl.multiple_of(i * width, width), width)]
        rows = pl.ds(pl.multiple_of(i * STRETCH, STRETCH), STRETCH)
        done_ref = out_ref.at[rows]
        for n in range(STRETCH // 128):
            blocks = []
            for g in range(8):
                at = g * STRETCH + n * 128
                blocks += [mine_ref[:, at : at + 128], pad]
            done_ref[n * 128 : (n + 1) * 128, :] = jnp.concatenate(blocks, axis=0).T
        pltpu.make_async_copy(done_ref, out_hbm.at[rows], out_sem).start()
        return carry

    lax.fori_loop(0, steps, step, 0)
    pltpu.make_async_copy(out_ref, out_hbm, out_sem).wait()


def bit_clear(shift):
    return (iota((RANKS, 128), 1) & shift) == 0


def merge_groups(xs):
    xs = [xs[q] for q in (0, 4, 2, 6, 1, 5, 3, 7)]
    for shift in (16, 32, 64):
        half = len(xs) // 2
        low = bit_clear(shift)
        xs = [
            jnp.where(low, x, y) + pltpu.roll(jnp.where(low, y, x), shift, 1)
            for x, y in zip(xs[:half], xs[half:])
        ]
    return xs[0]


def spread_groups(x):
    xs = [x]
    for shift in (64, 32, 16):
        low = bit_clear(shift)
        nexts = []
        for y in xs:
            z = pltpu.roll(y, shift, 1)
            nexts += [jnp.where(low, y, z), jnp.where(low, z, y)]
        xs = nexts
    return xs


def prepare(asked_ref, row_number_ref, number_ref, number_sem, group_ref):
    asked = asked_ref[...]
    lane = iota((DEVS, 128), 1)
    row = ((asked >> 13) << 10) | (asked & (STRETCH - 1))
    row_number_ref[...] = jnp.where(lane < RANKS, row, asked)
    copy = pltpu.make_async_copy(row_number_ref, number_ref, number_sem)
    copy.start()
    group = jnp.where(lane < pltpu.roll(asked, RANKS, 1), (asked >> 10) & 7, 8)
    groups = group.astype(F32).T[:RANKS]
    for b in range(DEVS // BLOCK):
        turned = groups if b == 0 else pltpu.roll(groups, DEVS - b * BLOCK, 1)
        group_ref[b * RANKS : (b + 1) * RANKS, :] = turned.astype(BF16)
    return copy


def fill_widen(widen_ref):
    for n in range(BLOCK):
        widen_ref[:, n * 128 : (n + 1) * 128] = (iota((DEVS, 128), 0) == n).astype(F32).astype(BF16)


def wide_groups(group_ref, widen_ref, b):
    at = pl.ds(pl.multiple_of(b * RANKS, RANKS), RANKS)
    return dot(group_ref[at, :], widen_ref[...])


def gather_kernel(
    asked_ref, table_hbm, out_ref, row_number_ref, group_ref, number_ref, widen_ref, row_ref, table_ref, sems
):
    left = iota((WIRE, 128), 1) < RANKS
    fill = pltpu.make_async_copy(table_hbm, table_ref, sems.at[1])
    fill.start()
    copy = prepare(asked_ref, row_number_ref, number_ref, sems.at[0], group_ref)
    fill_widen(widen_ref)
    copy.wait()
    fill.wait()

    def source(src, carry):
        mine_ref = row_ref.at[pl.ds(pl.multiple_of(src * RANKS, RANKS), RANKS)]
        count = number_ref[src, RANKS]
        for low, high in TIERS:

            @pl.when((count > low) & (count <= high))
            def _():
                for rank in range(high):
                    mine_ref[rank : rank + 1, :] = table_ref[pl.ds(number_ref[src, rank], 1), :]

        return carry

    lax.fori_loop(0, DEVS, source, 0, unroll=LOOK_UNROLL)

    def block(b, carry):
        base = pl.multiple_of(b * BLOCK * RANKS, BLOCK * RANKS)
        groups = wide_groups(group_ref, widen_ref, b)
        lane_group = (iota((RANKS, 128), 1) >> 4).astype(F32)
        halves = []
        for half in range(2):
            picked = []
            for n in range(half * 8, half * 8 + 8):
                rows = row_ref[pl.ds(base + n * RANKS, RANKS), :]
                picked.append(jnp.where(lane_group == groups[:, n * 128 : (n + 1) * 128], rows, 0.0))
            halves.append(merge_groups(picked))
        turned = jnp.concatenate(halves, axis=0).T
        evens, odds = [], []
        for q in range(8):
            first = turned[q * GROUP : q * GROUP + WIRE]
            second = turned[q * GROUP + WIRE : q * GROUP + 2 * WIRE]
            evens.append(jnp.where(left, first, pltpu.roll(second, RANKS, 1)))
            odds.append(jnp.where(left, pltpu.roll(first, RANKS, 1), second))
        at = pl.multiple_of(b * BLOCK * WIRE, 8)
        out_ref[pl.ds(at, BLOCK * WIRE), :] = jnp.concatenate(evens + odds, axis=0)
        return carry

    lax.fori_loop(0, DEVS // BLOCK, block, 0, unroll=UNROLL)


def scatter_kernel(
    row_number_ref, group_ref, wire_ref, out_hbm, number_ref, widen_ref, row_ref, turn_ref, out_ref, sems, *totals
):
    left = iota((WIRE, 128), 1) < RANKS
    table_rows = totals[0].shape[0]
    copy = pltpu.make_async_copy(row_number_ref, number_ref, sems.at[0])
    copy.start()
    fill_widen(widen_ref)
    turn_ref[...] = jnp.zeros(turn_ref.shape, F32)

    def clear(i, carry):
        for ref in totals:
            ref[pl.ds(pl.multiple_of(i * 256, 256), 256), :] = jnp.zeros((256, 128), F32)
        return carry

    lax.fori_loop(0, table_rows // 256, clear, 0)

    def block(b, carry):
        at = pl.multiple_of(b * BLOCK * WIRE, 8)
        base = pl.multiple_of(b * BLOCK * RANKS, BLOCK * RANKS)
        wire = wire_ref[pl.ds(at, BLOCK * WIRE), :]
        mine_ref = turn_ref.at[b]
        for q in range(8):
            even = wire[q * WIRE : (q + 1) * WIRE]
            odd = wire[(q + 8) * WIRE : (q + 9) * WIRE]
            mine_ref[q * GROUP : q * GROUP + WIRE, :] = jnp.where(left, even, pltpu.roll(odd, RANKS, 1))
            mine_ref[q * GROUP + WIRE : q * GROUP + 2 * WIRE, :] = jnp.where(left, pltpu.roll(even, RANKS, 1), odd)
        turned = mine_ref[...].T
        groups = wide_groups(group_ref, widen_ref, b)
        lane_group = (iota((RANKS, 128), 1) >> 4).astype(F32)
        for half in range(2):
            spreads = spread_groups(turned[half * RANKS : (half + 1) * RANKS])
            for q in range(8):
                n = half * 8 + q
                row_ref[pl.ds(base + n * RANKS, RANKS), :] = jnp.where(
                    lane_group == groups[:, n * 128 : (n + 1) * 128], spreads[q], 0.0
                )
        return carry

    lax.fori_loop(0, DEVS // BLOCK, block, 0, unroll=SPLIT_UNROLL)
    copy.wait()

    def source(src, carry):
        mine_ref = row_ref.at[pl.ds(pl.multiple_of(src * RANKS, RANKS), RANKS)]
        count = number_ref[src, RANKS]
        for low, high in TIERS:

            @pl.when((count > low) & (count <= high))
            def _():
                for start in range(0, high, CHAINS):
                    news = []
                    for i, ref in enumerate(totals[: high - start]):
                        row = number_ref[src, start + i]
                        news.append((row, mine_ref[start + i : start + i + 1, :] + ref[pl.ds(row, 1), :]))
                    for ref, (row, total) in zip(totals, news):
                        ref[pl.ds(row, 1), :] = total

        return carry

    lax.fori_loop(0, DEVS, source, 0, unroll=ADD_UNROLL)

    def close(i, carry):
        base = pl.multiple_of(i * STRETCH, STRETCH)
        lanes = pl.ds(pl.multiple_of(i * 8 * STRETCH, 8 * STRETCH), 8 * STRETCH)
        mine_ref = out_ref.at[:, lanes]
        for n in range(STRETCH // 128):
            at = pl.ds(base + n * 128, 128)
            total = totals[0][at, :]
            for ref in totals[1:]:
                total = total + ref[at, :]
            total = total.T
            for g in range(8):
                spot = g * STRETCH + n * 128
                mine_ref[:, spot : spot + 128] = total[g * GROUP : g * GROUP + 10]
        pltpu.make_async_copy(mine_ref, out_hbm.at[:, lanes], sems.at[1]).start()
        return carry

    lax.fori_loop(0, table_rows // STRETCH, close, 0)
    pltpu.make_async_copy(out_ref, out_hbm, sems.at[1]).wait()


HALF = RANKS // 2
KEYS = 2 * DEVS


def marks_kernel(owner_ref, rank_ref, after_ref, hot_ref, mark_ref, key_ref):
    rank = rank_ref[...].astype(jnp.int32)
    owner = owner_ref[...]
    key = jnp.where(owner < 0.0, -1.0, owner + ((rank >> 5) * DEVS).astype(F32))
    rest = (rank & (HALF - 1)).astype(F32)
    key_ref[...] = key
    for n in range(ROWS):
        at = slice(n * SEGS, (n + 1) * SEGS)
        hot_ref[:, at] = onehot_rows(key[n : n + 1], KEYS).astype(F32).astype(BF16)
        mark_ref[:, at] = onehot_rows(rest[n : n + 1], HALF).astype(F32).astype(BF16)


def render_kernel(
    wire_ref, hot_ref, mark_ref, key_ref, target_ref, image_ref, out_ref,
    turned_ref,    left_ref, value_ref, fall_ref, flow_ref, sum_ref, keep_ref, reach_ref, behind_ref,
    shade_ref, column_ref, picture_ref, across_ref, tilt_ref, grad_ref, spread_ref,
):
    for c in range(WIRE):
        block = wire_ref[pl.ds(c, DEVS, stride=WIRE), :].T
        parts = split(block, 3)
        for h in range(2):
            v = c + WIRE * h
            for half in range(2):
                rows = slice(h * RANKS + half * HALF, h * RANKS + (half + 1) * HALF)
                for n in range(3):
                    at = n * KEYS + half * DEVS
                    left_ref[v * HALF : (v + 1) * HALF, at : at + DEVS] = parts[n][rows]

    columns = jnp.concatenate([key_ref[...], jnp.zeros((128 - ROWS, SEGS), F32)], axis=0).T
    for n in range(ROWS):
        column = jnp.broadcast_to(columns[:, n : n + 1], (SEGS, KEYS))
        turned_ref[n * SEGS : (n + 1) * SEGS, :] = (column == iota((SEGS, KEYS), 1).astype(F32)).astype(F32).astype(BF16)

    def fetch(n, carry):
        at = pl.ds(pl.multiple_of(n * FETCH, FETCH), FETCH)
        hot = hot_ref[:, at]
        mark = mark_ref[:, at].astype(F32)
        found = dot(left_ref[...], jnp.concatenate([hot, hot, hot], axis=0))
        for v in range(10):
            got = jnp.sum(found[v * HALF : (v + 1) * HALF] * mark, axis=0, keepdims=True)
            for i in range(FETCH // SEGS):
                value_ref[v, pl.ds(n * (FETCH // SEGS) + i, 1), :] = got[:, i * SEGS : (i + 1) * SEGS]
        return carry

    lax.fori_loop(0, ROWS * SEGS // FETCH, fetch, 0)

    flat = jnp.concatenate([target_ref[ch] for ch in range(4)] + [jnp.zeros((112, 256), F32)], axis=0)
    column_ref[...] = jnp.concatenate([flat[:, :128].T, flat[:, 128:].T], axis=0)
    picture_ref[...] = jnp.zeros((256, 128), F32)
    earlier = (iota((128, 128), 0) < iota((128, 128), 1)).astype(F32).astype(BF16)
    later = (iota((128, 128), 0) > iota((128, 128), 1)).astype(F32).astype(BF16)
    ones = jnp.ones((256, 128), BF16)
    earlier = jnp.concatenate([earlier, earlier, earlier], axis=0)
    later = jnp.concatenate([later, later], axis=0)
    pixel_x = iota((16, SEGS), 0).astype(F32) + 0.5

    def tile(t, carry):
        first = t * STEPS
        for k in range(STEPS):
            value = lambda v: value_ref[v, pl.ds(first + k, 1), :]
            offset_x = pixel_x - value(0)
            across_ref[k] = (-0.5 * LOG2E) * value(2) * offset_x * offset_x
            tilt_ref[k] = -LOG2E * value(3) * offset_x

        def forward(n, carry):
            for half in range(2):
                y = 2 * n + half
                pixel_y = y.astype(F32) + 0.5
                keep = jnp.ones((16, SEGS), F32)
                sums = [jnp.zeros((16, SEGS), F32) for _ in range(4)]
                at = pl.ds(pl.multiple_of(y * 16, 16), 16)
                for k in range(STEPS):
                    value = lambda v: value_ref[v, pl.ds(first + k, 1), :]
                    offset_y = pixel_y - value(1)
                    down = (-0.5 * LOG2E) * value(4) * offset_y * offset_y
                    fall = jnp.exp2(across_ref[k] + down + tilt_ref[k] * offset_y)
                    flow = fall * keep
                    weight = value(5) * flow
                    keep = keep - weight
                    for ch in range(4):
                        sums[ch] = sums[ch] + value(6 + ch) * weight
                    fall_ref[k, at, :] = fall
                    flow_ref[k, at, :] = flow
                keep_ref[at, :] = keep
                for ch in range(4):
                    sum_ref[ch, at, :] = sums[ch]
            return carry

        lax.fori_loop(0, 8, forward, 0, unroll=FORE)

        keep = keep_ref[...]
        logs = jnp.concatenate(split(jnp.log(keep), 3), axis=1)
        reach = jnp.exp(dot(logs, earlier))
        reach_ref[...] = reach
        spent = jnp.zeros((256, SEGS), F32)
        for ch in range(4):
            part = sum_ref[ch] * reach
            rendered = dot(jnp.concatenate(split(part, 2), axis=1), ones)
            here = iota((256, 128), 1) == ch * TILES + t
            wanted = jnp.sum(jnp.where(here, column_ref[...], 0.0), axis=1, keepdims=True)
            shade = 2.0 * (rendered - wanted)
            picture_ref[...] = jnp.where(here, rendered, picture_ref[...])
            shade_ref[ch] = shade
            spent = spent + shade * part
        rest = dot(jnp.concatenate(split(spent, 2), axis=1), later)
        behind_ref[...] = rest / (reach * keep)

        for k in reversed(range(STEPS)):
            value = lambda v: value_ref[v, pl.ds(first + k, 1), :]
            mean_y = jnp.broadcast_to(value(1), (8, SEGS))
            opacity = jnp.broadcast_to(value(5), (8, SEGS))
            colours = [jnp.broadcast_to(value(6 + ch), (8, SEGS)) for ch in range(4)]

            def backward(n, sums):
                zero, one, two, tints = sums
                zero, one, two, tints = list(zero), list(one), list(two), list(tints)
                for quarter in range(2):
                    y = 2 * n + quarter
                    offset_y = y.astype(F32) + 0.5 - mean_y
                    for half in range(2):
                        at = pl.ds(pl.multiple_of(y * 16 + half * 8, 8), 8)
                        shades = [shade_ref[ch, at, :] for ch in range(4)]
                        flow = flow_ref[k, at, :] * reach_ref[at, :]
                        lit = (shades[0] * colours[0] + shades[1] * colours[1]) + (
                            shades[2] * colours[2] + shades[3] * colours[3]
                        )
                        behind = behind_ref[at, :]
                        gap = lit - behind
                        behind_ref[at, :] = behind + opacity * fall_ref[k, at, :] * gap
                        grad = flow * gap
                        slope = grad * offset_y
                        zero[half] = zero[half] + grad
                        one[half] = one[half] + slope
                        two[half] = two[half] + slope * offset_y
                        for ch in range(4):
                            tints[ch] = tints[ch] + flow * shades[ch]
                return (tuple(zero), tuple(one), tuple(two), tuple(tints))

            blank = jnp.zeros((8, SEGS), F32)
            zero, one, two, tints = lax.fori_loop(
                0, 8, backward, ((blank,) * 2, (blank,) * 2, (blank,) * 2, (blank,) * 4), unroll=BACK
            )
            total = lambda x: jnp.sum(x, axis=0, keepdims=True)
            offset_x = pixel_x - value(0)
            near, far = offset_x[:8], offset_x[8:]
            sum_0 = total(zero[0] + zero[1])
            slope_x = (near * zero[0], far * zero[1])
            sum_x = total(slope_x[0] + slope_x[1])
            sum_xx = total(near * slope_x[0] + far * slope_x[1])
            sum_y = total(one[0] + one[1])
            sum_xy = total(near * one[0] + far * one[1])
            sum_yy = total(two[0] + two[1])
            opacity = value(5)
            grads = [
                opacity * (value(2) * sum_x + value(3) * sum_y),
                opacity * (value(4) * sum_y + value(3) * sum_x),
                -0.5 * opacity * sum_xx,
                -opacity * sum_xy,
                -0.5 * opacity * sum_yy,
                sum_0,
            ] + [opacity * total(tint) for tint in tints]
            for v in range(10):
                grad_ref[v, pl.ds(first + k, 1), :] = grads[v]
        return carry

    lax.fori_loop(0, TILES, tile, 0)

    picture = picture_ref[...]
    picture = jnp.concatenate([picture[:128].T, picture[128:].T], axis=1)
    for ch in range(4):
        image_ref[ch] = picture[ch * TILES : (ch + 1) * TILES, :]

    spread_ref[...] = jnp.zeros((10 * HALF, KEYS), F32)

    def spread(n, carry):
        at = pl.ds(pl.multiple_of(n * SPREAD, SPREAD), SPREAD)
        mark = mark_ref[:, at].astype(F32)
        heads, tails = [], []
        for v in range(10):
            count = SPREAD // SEGS
            grad = jnp.concatenate([grad_ref[v, pl.ds(count * n + i, 1), :] for i in range(count)], axis=1)
            head, tail = split(grad * mark, 2)
            heads.append(head)
            tails.append(tail)
        turned = turned_ref[at, :]
        both = jnp.concatenate([jnp.concatenate(heads, axis=0), jnp.concatenate(tails, axis=0)], axis=1)
        spread_ref[...] += dot(both, jnp.concatenate([turned, turned], axis=0))
        return carry

    lax.fori_loop(0, ROWS * SEGS // SPREAD, spread, 0)
    for c in range(WIRE):
        rows = []
        for h in range(2):
            for half in range(2):
                v = c + WIRE * h
                rows.append(spread_ref[v * HALF : (v + 1) * HALF, half * DEVS : (half + 1) * DEVS])
        out_ref[pl.ds(c, DEVS, stride=WIRE), :] = jnp.concatenate(rows, axis=0).T


def vmem():
    return pl.BlockSpec(memory_space=pltpu.VMEM)


def hbm():
    return pl.BlockSpec(memory_space=pltpu.HBM)


def smem():
    return pl.BlockSpec(memory_space=pltpu.SMEM)


def call(kernel, name, in_specs, outs, scratch, limit):
    return pl.pallas_call(
        kernel,
        name=name,
        out_shape=outs,
        in_specs=in_specs,
        out_specs=jax.tree.map(lambda _: vmem(), outs),
        scratch_shapes=scratch,
        compiler_params=pltpu.CompilerParams(vmem_limit_bytes=limit),
    )


def exchange(x):
    width = x.shape[0] * x.shape[1] // DEVS
    moved = lax.all_to_all(x.reshape(DEVS, 1, width), AXES, split_axis=0, concat_axis=0, tiled=True)
    return moved.reshape(x.shape)


def body(splat_params, list_owner, list_slot, list_length, target):
    shape = jax.ShapeDtypeStruct
    wire = shape((DEVS * WIRE, 128), F32)
    route = call(
        route_kernel, "route", [hbm(), hbm(), hbm()],
        (shape((DEVS, 128), jnp.int32), shape((ROWS, SEGS), F32), shape((ROWS, SEGS), F32)),
        [
            pltpu.SMEM(list_length.shape, jnp.int32), pltpu.VMEM((ROWS, SEGS), jnp.int32),
            pltpu.VMEM(list_slot.shape, jnp.int32), pltpu.SemaphoreType.DMA((3,)),
        ],
        ROUTE_LIMIT,
    )
    request, owners, ranks = route(list_length, list_owner.reshape(ROWS, SEGS), list_slot)
    asked = exchange(request)
    rows = splat_params.shape[1] // 8
    packed = pl.pallas_call(
        pack_kernel,
        name="pack",
        out_shape=shape((rows, 128), F32),
        in_specs=[hbm()],
        out_specs=hbm(),
        scratch_shapes=[
            pltpu.VMEM(splat_params.shape, F32), pltpu.VMEM((rows, 128), F32),
            pltpu.SemaphoreType.DMA((rows // STRETCH,)), pltpu.SemaphoreType.DMA,
        ],
        compiler_params=pltpu.CompilerParams(vmem_limit_bytes=61 << 20),
    )(splat_params)
    staging = [
        pltpu.SMEM((DEVS, 128), jnp.int32), pltpu.VMEM((DEVS, BLOCK * 128), BF16),
        pltpu.VMEM((DEVS * RANKS, 128), F32),
    ]
    table = pltpu.VMEM((rows, 128), F32)
    sems = pltpu.SemaphoreType.DMA((2,))
    numbers = shape((DEVS, 128), jnp.int32)
    groups = shape((DEVS // BLOCK * RANKS, DEVS), BF16)
    gather = call(gather_kernel, "gather", [vmem(), hbm()], (wire, numbers, groups), staging + [table, sems], 51 << 20)
    found, numbers, groups = gather(asked, packed)
    replies = exchange(found)
    entries = ROWS * SEGS
    marks = call(
        marks_kernel, "marks", [vmem(), vmem(), hbm()],
        (shape((KEYS, entries), BF16), shape((HALF, entries), BF16), shape((ROWS, SEGS), F32)), [], 16 << 20,
    )
    hot, mark, keys = marks(owners, ranks, numbers)
    field = pltpu.VMEM((256, SEGS), F32)
    deep = pltpu.VMEM((STEPS, 256, SEGS), F32)
    render = call(
        render_kernel, "render", [vmem()] * 5, (shape(target.shape, F32), wire),
        [
            pltpu.VMEM((entries, KEYS), BF16), pltpu.VMEM((10 * HALF, 3 * KEYS), BF16),
            pltpu.VMEM((10, ROWS, SEGS), F32), deep, deep, pltpu.VMEM((4, 256, SEGS), F32), field, field, field,
            pltpu.VMEM((4, 256, SEGS), F32), field, field,
            pltpu.VMEM((STEPS, 16, SEGS), F32), pltpu.VMEM((STEPS, 16, SEGS), F32),
            pltpu.VMEM((10, ROWS, SEGS), F32), pltpu.VMEM((10 * HALF, KEYS), F32),
        ],
        24 << 20,
    )
    images, outgoing = render(replies, hot, mark, keys, target)
    incoming = exchange(outgoing)
    scatter = pl.pallas_call(
        scatter_kernel,
        name="scatter",
        out_shape=shape(splat_params.shape, F32),
        in_specs=[vmem(), vmem(), vmem()],
        out_specs=hbm(),
        scratch_shapes=staging
        + [pltpu.VMEM((DEVS // BLOCK, 128, 128), F32), pltpu.VMEM(splat_params.shape, F32), sems]
        + [table] * CHAINS,
        compiler_params=pltpu.CompilerParams(vmem_limit_bytes=44 << 20),
    )
    return (images, scatter(numbers, groups, incoming))


def solution(mesh):
    in_specs = (
        P(None, AXES),
        P(AXES, None, None),
        P(AXES, None),
        P(AXES),
        P(None, AXES, None),
    )
    out_specs = (P(None, AXES, None), P(None, AXES))
    return jax.shard_map(body, mesh=mesh, in_specs=in_specs, out_specs=out_specs, check_vma=False)
```

```python
import jax
import jax.numpy as jnp
from jax import lax
from jax.experimental import pallas as pl
from jax.experimental.pallas import tpu as pltpu
from jax.sharding import PartitionSpec as P

AXES = ("row", "col")
DEVS = 128
RANKS = 64
TILES = 4
SEGS = 128
STEPS = 8
ROWS = TILES * STEPS
WIRE = 5
GROUP = 16
BLOCK = 16
TIERS = ((0, 48), (48, RANKS))
LOOK_UNROLL = 8
ADD_UNROLL = 4
STRETCH = 1024
UNROLL = 4
ROUTE_LIMIT = 63 << 20
SPLIT_UNROLL = 2
FORE = 4
FETCH = 4096
SPREAD = 4096
BACK = 8
CHAINS = 6
LOG2E = 1.4426950408889634
F32 = jnp.float32
BF16 = jnp.bfloat16


def iota(shape, dim):
    return lax.broadcasted_iota(jnp.int32, shape, dim)


def dot(a, b):
    return lax.dot_general(a, b, (((1,), (0,)), ((), ())), preferred_element_type=F32)


def dot_nt(a, b):
    return lax.dot_general(a, b, (((1,), (1,)), ((), ())), preferred_element_type=F32)


def split(x, parts):
    out = []
    for _ in range(parts - 1):
        head = x.astype(BF16)
        out.append(head)
        x = x - head.astype(F32)
    out.append(x.astype(BF16))
    return out


def onehot_rows(row, count):
    wide = jnp.broadcast_to(row, (count, row.shape[1]))
    return wide == iota(wide.shape, 0).astype(F32)


def route_kernel(
    length_hbm, owner_hbm, slot_hbm, request_ref, owner_out, rank_out, length_ref, owner_ref, slot_ref, sems
):
    pairs = ((length_hbm, length_ref), (owner_hbm, owner_ref), (slot_hbm, slot_ref))
    copies = [pltpu.make_async_copy(a, b, sems.at[i]) for i, (a, b) in enumerate(pairs)]
    for copy in copies:
        copy.start()
    for copy in copies:
        copy.wait()
    lane = iota((STEPS, SEGS), 1)
    step = iota((STEPS, SEGS), 0)
    picks = (lane & (STEPS - 1)) == step
    pieces = []
    for r in range(STEPS):
        rows = []
        slot_rows = []
        for t in range(TILES):
            own = jnp.broadcast_to(owner_ref[t * STEPS + r : t * STEPS + r + 1, :], (STEPS, SEGS))
            rows.append(jnp.where(picks, own, 0))
            slot = slot_ref[t : t + 1, r * SEGS : (r + 1) * SEGS]
            slot_rows.append(jnp.where(picks, jnp.broadcast_to(slot, (STEPS, SEGS)), 0))
        rows += [s >> 8 for s in slot_rows] + [s & 255 for s in slot_rows]
        pieces.append(jnp.concatenate(rows, axis=0).astype(F32).astype(BF16))
    spread = jnp.concatenate(pieces, axis=1)
    place = ((iota((STEPS * SEGS, SEGS), 0) >> 3) == iota((STEPS * SEGS, SEGS), 1)).astype(F32)
    moved = dot(spread, place.astype(BF16))
    lane = iota((ROWS, SEGS), 1)
    row = iota((ROWS, SEGS), 0)
    length = jnp.full((ROWS, SEGS), length_ref[0], jnp.int32)
    for t in range(1, TILES):
        length = jnp.where((row >> 3) == t, length_ref[t], length)
    live = (lane * STEPS + (row & (STEPS - 1))) < length
    owners = jnp.where(live, moved[0:ROWS], -1.0)
    high = moved[ROWS : 2 * ROWS]
    low = moved[2 * ROWS : 3 * ROWS]
    owner_out[...] = owners
    before = (iota((256, 256), 0) < iota((256, 256), 1)).astype(F32).astype(BF16)
    before = jnp.concatenate([before, jnp.ones((256, 256), BF16)], axis=1)
    rank_of = (iota((2 * RANKS, 256), 0) & (RANKS - 1)).astype(F32)
    upper = iota((2 * RANKS, 256), 0) < RANKS
    carry = jnp.zeros((DEVS, 256), F32)
    request = jnp.zeros((2 * RANKS, DEVS), F32)
    for n in range(ROWS // 2):
        pair = lambda x: jnp.concatenate([x[2 * n : 2 * n + 1], x[2 * n + 1 : 2 * n + 2]], axis=1)
        hot = onehot_rows(pair(owners), DEVS)
        hot16 = hot.astype(F32).astype(BF16)
        counted = dot(hot16, before)
        rank = jnp.sum(jnp.where(hot, counted[:, :256] + carry, 0.0), axis=0, keepdims=True)
        carry = carry + counted[:, 256:]
        rank_out[2 * n : 2 * n + 1, :] = rank[:, :SEGS]
        rank_out[2 * n + 1 : 2 * n + 2, :] = rank[:, SEGS:]
        values = jnp.where(upper, pair(high), pair(low))
        values = jnp.where(rank_of == rank, values, 0.0)
        request = request + dot_nt(values.astype(BF16), hot16)
    slots = request[:RANKS] * 256.0 + request[RANKS:]
    slots = jnp.concatenate([slots, slots], axis=0).T
    full = jnp.where(iota((DEVS, DEVS), 1) < RANKS, slots, carry[:, :DEVS])
    request_ref[...] = full.astype(jnp.int32)


def pack_kernel(params_hbm, out_hbm, params_ref, out_ref, in_sems, out_sem):
    width = 8 * STRETCH
    steps = params_ref.shape[1] // width
    pad = jnp.zeros((GROUP - 10, 128), F32)

    def read(i):
        at = pl.ds(pl.multiple_of(i * width, width), width)
        return pltpu.make_async_copy(params_hbm.at[:, at], params_ref.at[:, at], in_sems.at[i])

    for i in range(steps):
        read(i).start()

    def step(i, carry):
        read(i).wait()
        mine_ref = params_ref.at[:, pl.ds(pl.multiple_of(i * width, width), width)]
        rows = pl.ds(pl.multiple_of(i * STRETCH, STRETCH), STRETCH)
        done_ref = out_ref.at[rows]
        for n in range(STRETCH // 128):
            blocks = []
            for g in range(8):
                at = g * STRETCH + n * 128
                blocks += [mine_ref[:, at : at + 128], pad]
            done_ref[n * 128 : (n + 1) * 128, :] = jnp.concatenate(blocks, axis=0).T
        pltpu.make_async_copy(done_ref, out_hbm.at[rows], out_sem).start()
        return carry

    lax.fori_loop(0, steps, step, 0)
    pltpu.make_async_copy(out_ref, out_hbm, out_sem).wait()


def bit_clear(shift):
    return (iota((RANKS, 128), 1) & shift) == 0


def merge_groups(xs):
    xs = [xs[q] for q in (0, 4, 2, 6, 1, 5, 3, 7)]
    for shift in (16, 32, 64):
        half = len(xs) // 2
        low = bit_clear(shift)
        xs = [
            jnp.where(low, x, y) + pltpu.roll(jnp.where(low, y, x), shift, 1)
            for x, y in zip(xs[:half], xs[half:])
        ]
    return xs[0]


def spread_groups(x):
    xs = [x]
    for shift in (64, 32, 16):
        low = bit_clear(shift)
        nexts = []
        for y in xs:
            z = pltpu.roll(y, shift, 1)
            nexts += [jnp.where(low, y, z), jnp.where(low, z, y)]
        xs = nexts
    return xs


def prepare(asked_ref, row_number_ref, number_ref, number_sem, group_ref):
    asked = asked_ref[...]
    lane = iota((DEVS, 128), 1)
    row = ((asked >> 13) << 10) | (asked & (STRETCH - 1))
    row_number_ref[...] = jnp.where(lane < RANKS, row, asked)
    copy = pltpu.make_async_copy(row_number_ref, number_ref, number_sem)
    copy.start()
    group = jnp.where(lane < pltpu.roll(asked, RANKS, 1), (asked >> 10) & 7, 8)
    groups = group.astype(F32).T[:RANKS]
    for b in range(DEVS // BLOCK):
        turned = groups if b == 0 else pltpu.roll(groups, DEVS - b * BLOCK, 1)
        group_ref[b * RANKS : (b + 1) * RANKS, :] = turned.astype(BF16)
    return copy


def fill_widen(widen_ref):
    for n in range(BLOCK):
        widen_ref[:, n * 128 : (n + 1) * 128] = (iota((DEVS, 128), 0) == n).astype(F32).astype(BF16)


def wide_groups(group_ref, widen_ref, b):
    at = pl.ds(pl.multiple_of(b * RANKS, RANKS), RANKS)
    return dot(group_ref[at, :], widen_ref[...])


def gather_kernel(
    asked_ref, table_hbm, out_ref, row_number_ref, group_ref, number_ref, widen_ref, row_ref, table_ref, sems
):
    left = iota((WIRE, 128), 1) < RANKS
    fill = pltpu.make_async_copy(table_hbm, table_ref, sems.at[1])
    fill.start()
    copy = prepare(asked_ref, row_number_ref, number_ref, sems.at[0], group_ref)
    fill_widen(widen_ref)
    copy.wait()
    fill.wait()

    def source(src, carry):
        mine_ref = row_ref.at[pl.ds(pl.multiple_of(src * RANKS, RANKS), RANKS)]
        count = number_ref[src, RANKS]
        for low, high in TIERS:

            @pl.when((count > low) & (count <= high))
            def _():
                for rank in range(high):
                    mine_ref[rank : rank + 1, :] = table_ref[pl.ds(number_ref[src, rank], 1), :]

        return carry

    lax.fori_loop(0, DEVS, source, 0, unroll=LOOK_UNROLL)

    def block(b, carry):
        base = pl.multiple_of(b * BLOCK * RANKS, BLOCK * RANKS)
        groups = wide_groups(group_ref, widen_ref, b)
        lane_group = (iota((RANKS, 128), 1) >> 4).astype(F32)
        halves = []
        for half in range(2):
            picked = []
            for n in range(half * 8, half * 8 + 8):
                rows = row_ref[pl.ds(base + n * RANKS, RANKS), :]
                picked.append(jnp.where(lane_group == groups[:, n * 128 : (n + 1) * 128], rows, 0.0))
            halves.append(merge_groups(picked))
        turned = jnp.concatenate(halves, axis=0).T
        evens, odds = [], []
        for q in range(8):
            first = turned[q * GROUP : q * GROUP + WIRE]
            second = turned[q * GROUP + WIRE : q * GROUP + 2 * WIRE]
            evens.append(jnp.where(left, first, pltpu.roll(second, RANKS, 1)))
            odds.append(jnp.where(left, pltpu.roll(first, RANKS, 1), second))
        at = pl.multiple_of(b * BLOCK * WIRE, 8)
        out_ref[pl.ds(at, BLOCK * WIRE), :] = jnp.concatenate(evens + odds, axis=0)
        return carry

    lax.fori_loop(0, DEVS // BLOCK, block, 0, unroll=UNROLL)


def scatter_kernel(
    row_number_ref, group_ref, wire_ref, out_hbm, number_ref, widen_ref, row_ref, turn_ref, out_ref, sems, *totals
):
    left = iota((WIRE, 128), 1) < RANKS
    table_rows = totals[0].shape[0]
    copy = pltpu.make_async_copy(row_number_ref, number_ref, sems.at[0])
    copy.start()
    fill_widen(widen_ref)
    turn_ref[...] = jnp.zeros(turn_ref.shape, F32)

    def clear(i, carry):
        for ref in totals:
            ref[pl.ds(pl.multiple_of(i * 256, 256), 256), :] = jnp.zeros((256, 128), F32)
        return carry

    lax.fori_loop(0, table_rows // 256, clear, 0)

    def block(b, carry):
        at = pl.multiple_of(b * BLOCK * WIRE, 8)
        base = pl.multiple_of(b * BLOCK * RANKS, BLOCK * RANKS)
        wire = wire_ref[pl.ds(at, BLOCK * WIRE), :]
        mine_ref = turn_ref.at[b]
        for q in range(8):
            even = wire[q * WIRE : (q + 1) * WIRE]
            odd = wire[(q + 8) * WIRE : (q + 9) * WIRE]
            mine_ref[q * GROUP : q * GROUP + WIRE, :] = jnp.where(left, even, pltpu.roll(odd, RANKS, 1))
            mine_ref[q * GROUP + WIRE : q * GROUP + 2 * WIRE, :] = jnp.where(left, pltpu.roll(even, RANKS, 1), odd)
        turned = mine_ref[...].T
        groups = wide_groups(group_ref, widen_ref, b)
        lane_group = (iota((RANKS, 128), 1) >> 4).astype(F32)
        for half in range(2):
            spreads = spread_groups(turned[half * RANKS : (half + 1) * RANKS])
            for q in range(8):
                n = half * 8 + q
                row_ref[pl.ds(base + n * RANKS, RANKS), :] = jnp.where(
                    lane_group == groups[:, n * 128 : (n + 1) * 128], spreads[q], 0.0
                )
        return carry

    lax.fori_loop(0, DEVS // BLOCK, block, 0, unroll=SPLIT_UNROLL)
    copy.wait()

    def source(src, carry):
        mine_ref = row_ref.at[pl.ds(pl.multiple_of(src * RANKS, RANKS), RANKS)]
        count = number_ref[src, RANKS]
        for low, high in TIERS:

            @pl.when((count > low) & (count <= high))
            def _():
                for start in range(0, high, CHAINS):
                    news = []
                    for i, ref in enumerate(totals[: high - start]):
                        row = number_ref[src, start + i]
                        news.append((row, mine_ref[start + i : start + i + 1, :] + ref[pl.ds(row, 1), :]))
                    for ref, (row, total) in zip(totals, news):
                        ref[pl.ds(row, 1), :] = total

        return carry

    lax.fori_loop(0, DEVS, source, 0, unroll=ADD_UNROLL)

    def close(i, carry):
        base = pl.multiple_of(i * STRETCH, STRETCH)
        lanes = pl.ds(pl.multiple_of(i * 8 * STRETCH, 8 * STRETCH), 8 * STRETCH)
        mine_ref = out_ref.at[:, lanes]
        for n in range(STRETCH // 128):
            at = pl.ds(base + n * 128, 128)
            total = totals[0][at, :]
            for ref in totals[1:]:
                total = total + ref[at, :]
            total = total.T
            for g in range(8):
                spot = g * STRETCH + n * 128
                mine_ref[:, spot : spot + 128] = total[g * GROUP : g * GROUP + 10]
        pltpu.make_async_copy(mine_ref, out_hbm.at[:, lanes], sems.at[1]).start()
        return carry

    lax.fori_loop(0, table_rows // STRETCH, close, 0)
    pltpu.make_async_copy(out_ref, out_hbm, sems.at[1]).wait()


HALF = RANKS // 2
KEYS = 2 * DEVS


def marks_kernel(owner_ref, rank_ref, after_ref, hot_ref, mark_ref, key_ref):
    rank = rank_ref[...].astype(jnp.int32)
    owner = owner_ref[...]
    key = jnp.where(owner < 0.0, -1.0, owner + ((rank >> 5) * DEVS).astype(F32))
    rest = (rank & (HALF - 1)).astype(F32)
    key_ref[...] = key
    for n in range(ROWS):
        at = slice(n * SEGS, (n + 1) * SEGS)
        hot_ref[:, at] = onehot_rows(key[n : n + 1], KEYS).astype(F32).astype(BF16)
        mark_ref[:, at] = onehot_rows(rest[n : n + 1], HALF).astype(F32).astype(BF16)


def render_kernel(
    wire_ref, hot_ref, mark_ref, key_ref, target_ref, image_ref, out_ref,
    turned_ref,    left_ref, value_ref, fall_ref, flow_ref, sum_ref, keep_ref, reach_ref, behind_ref,
    shade_ref, column_ref, picture_ref, across_ref, tilt_ref, grad_ref, spread_ref,
):
    for c in range(WIRE):
        block = wire_ref[pl.ds(c, DEVS, stride=WIRE), :].T
        parts = split(block, 3)
        for h in range(2):
            v = c + WIRE * h
            for half in range(2):
                rows = slice(h * RANKS + half * HALF, h * RANKS + (half + 1) * HALF)
                for n in range(3):
                    at = n * KEYS + half * DEVS
                    left_ref[v * HALF : (v + 1) * HALF, at : at + DEVS] = parts[n][rows]

    columns = jnp.concatenate([key_ref[...], jnp.zeros((128 - ROWS, SEGS), F32)], axis=0).T
    for n in range(ROWS):
        column = jnp.broadcast_to(columns[:, n : n + 1], (SEGS, KEYS))
        turned_ref[n * SEGS : (n + 1) * SEGS, :] = (column == iota((SEGS, KEYS), 1).astype(F32)).astype(F32).astype(BF16)

    def fetch(n, carry):
        at = pl.ds(pl.multiple_of(n * FETCH, FETCH), FETCH)
        hot = hot_ref[:, at]
        mark = mark_ref[:, at].astype(F32)
        found = dot(left_ref[...], jnp.concatenate([hot, hot, hot], axis=0))
        for v in range(10):
            got = jnp.sum(found[v * HALF : (v + 1) * HALF] * mark, axis=0, keepdims=True)
            for i in range(FETCH // SEGS):
                value_ref[v, pl.ds(n * (FETCH // SEGS) + i, 1), :] = got[:, i * SEGS : (i + 1) * SEGS]
        return carry

    lax.fori_loop(0, ROWS * SEGS // FETCH, fetch, 0)

    flat = jnp.concatenate([target_ref[ch] for ch in range(4)] + [jnp.zeros((112, 256), F32)], axis=0)
    column_ref[...] = jnp.concatenate([flat[:, :128].T, flat[:, 128:].T], axis=0)
    picture_ref[...] = jnp.zeros((256, 128), F32)
    earlier = (iota((128, 128), 0) < iota((128, 128), 1)).astype(F32).astype(BF16)
    later = (iota((128, 128), 0) > iota((128, 128), 1)).astype(F32).astype(BF16)
    ones = jnp.ones((256, 128), BF16)
    earlier = jnp.concatenate([earlier, earlier, earlier], axis=0)
    later = jnp.concatenate([later, later], axis=0)
    pixel_x = iota((16, SEGS), 0).astype(F32) + 0.5

    def tile(t, carry):
        first = t * STEPS
        for k in range(STEPS):
            value = lambda v: value_ref[v, pl.ds(first + k, 1), :]
            offset_x = pixel_x - value(0)
            across_ref[k] = (-0.5 * LOG2E) * value(2) * offset_x * offset_x
            tilt_ref[k] = -LOG2E * value(3) * offset_x

        def forward(n, carry):
            for half in range(2):
                y = 2 * n + half
                pixel_y = y.astype(F32) + 0.5
                keep = jnp.ones((16, SEGS), F32)
                sums = [jnp.zeros((16, SEGS), F32) for _ in range(4)]
                at = pl.ds(pl.multiple_of(y * 16, 16), 16)
                for k in range(STEPS):
                    value = lambda v: value_ref[v, pl.ds(first + k, 1), :]
                    offset_y = pixel_y - value(1)
                    down = (-0.5 * LOG2E) * value(4) * offset_y * offset_y
                    fall = jnp.exp2(across_ref[k] + down + tilt_ref[k] * offset_y)
                    flow = fall * keep
                    weight = value(5) * flow
                    keep = keep - weight
                    for ch in range(4):
                        sums[ch] = sums[ch] + value(6 + ch) * weight
                    fall_ref[k, at, :] = fall
                    flow_ref[k, at, :] = flow
                keep_ref[at, :] = keep
                for ch in range(4):
                    sum_ref[ch, at, :] = sums[ch]
            return carry

        lax.fori_loop(0, 8, forward, 0, unroll=FORE)

        keep = keep_ref[...]
        logs = jnp.concatenate(split(jnp.log(keep), 3), axis=1)
        reach = jnp.exp(dot(logs, earlier))
        reach_ref[...] = reach
        spent = jnp.zeros((256, SEGS), F32)
        for ch in range(4):
            part = sum_ref[ch] * reach
            rendered = dot(jnp.concatenate(split(part, 2), axis=1), ones)
            here = iota((256, 128), 1) == ch * TILES + t
            wanted = jnp.sum(jnp.where(here, column_ref[...], 0.0), axis=1, keepdims=True)
            shade = 2.0 * (rendered - wanted)
            picture_ref[...] = jnp.where(here, rendered, picture_ref[...])
            shade_ref[ch] = shade
            spent = spent + shade * part
        rest = dot(jnp.concatenate(split(spent, 2), axis=1), later)
        behind_ref[...] = rest / (reach * keep)

        for k in reversed(range(STEPS)):
            value = lambda v: value_ref[v, pl.ds(first + k, 1), :]
            mean_y = jnp.broadcast_to(value(1), (8, SEGS))
            opacity = jnp.broadcast_to(value(5), (8, SEGS))
            colours = [jnp.broadcast_to(value(6 + ch), (8, SEGS)) for ch in range(4)]

            def backward(n, sums):
                zero, one, two, tints = sums
                zero, one, two, tints = list(zero), list(one), list(two), list(tints)
                for quarter in range(2):
                    y = 2 * n + quarter
                    offset_y = y.astype(F32) + 0.5 - mean_y
                    for half in range(2):
                        at = pl.ds(pl.multiple_of(y * 16 + half * 8, 8), 8)
                        shades = [shade_ref[ch, at, :] for ch in range(4)]
                        flow = flow_ref[k, at, :] * reach_ref[at, :]
                        lit = (shades[0] * colours[0] + shades[1] * colours[1]) + (
                            shades[2] * colours[2] + shades[3] * colours[3]
                        )
                        behind = behind_ref[at, :]
                        gap = lit - behind
                        behind_ref[at, :] = behind + opacity * fall_ref[k, at, :] * gap
                        grad = flow * gap
                        slope = grad * offset_y
                        zero[half] = zero[half] + grad
                        one[half] = one[half] + slope
                        two[half] = two[half] + slope * offset_y
                        for ch in range(4):
                            tints[ch] = tints[ch] + flow * shades[ch]
                return (tuple(zero), tuple(one), tuple(two), tuple(tints))

            blank = jnp.zeros((8, SEGS), F32)
            zero, one, two, tints = lax.fori_loop(
                0, 8, backward, ((blank,) * 2, (blank,) * 2, (blank,) * 2, (blank,) * 4), unroll=BACK
            )
            total = lambda x: jnp.sum(x, axis=0, keepdims=True)
            offset_x = pixel_x - value(0)
            near, far = offset_x[:8], offset_x[8:]
            sum_0 = total(zero[0] + zero[1])
            slope_x = (near * zero[0], far * zero[1])
            sum_x = total(slope_x[0] + slope_x[1])
            sum_xx = total(near * slope_x[0] + far * slope_x[1])
            sum_y = total(one[0] + one[1])
            sum_xy = total(near * one[0] + far * one[1])
            sum_yy = total(two[0] + two[1])
            opacity = value(5)
            grads = [
                opacity * (value(2) * sum_x + value(3) * sum_y),
                opacity * (value(4) * sum_y + value(3) * sum_x),
                -0.5 * opacity * sum_xx,
                -opacity * sum_xy,
                -0.5 * opacity * sum_yy,
                sum_0,
            ] + [opacity * total(tint) for tint in tints]
            for v in range(10):
                grad_ref[v, pl.ds(first + k, 1), :] = grads[v]
        return carry

    lax.fori_loop(0, TILES, tile, 0)

    picture = picture_ref[...]
    picture = jnp.concatenate([picture[:128].T, picture[128:].T], axis=1)
    for ch in range(4):
        image_ref[ch] = picture[ch * TILES : (ch + 1) * TILES, :]

    spread_ref[...] = jnp.zeros((10 * HALF, KEYS), F32)

    def spread(n, carry):
        at = pl.ds(pl.multiple_of(n * SPREAD, SPREAD), SPREAD)
        mark = mark_ref[:, at].astype(F32)
        heads, tails = [], []
        for v in range(10):
            count = SPREAD // SEGS
            grad = jnp.concatenate([grad_ref[v, pl.ds(count * n + i, 1), :] for i in range(count)], axis=1)
            head, tail = split(grad * mark, 2)
            heads.append(head)
            tails.append(tail)
        turned = turned_ref[at, :]
        both = jnp.concatenate([jnp.concatenate(heads, axis=0), jnp.concatenate(tails, axis=0)], axis=1)
        spread_ref[...] += dot(both, jnp.concatenate([turned, turned], axis=0))
        return carry

    lax.fori_loop(0, ROWS * SEGS // SPREAD, spread, 0)
    for c in range(WIRE):
        rows = []
        for h in range(2):
            for half in range(2):
                v = c + WIRE * h
                rows.append(spread_ref[v * HALF : (v + 1) * HALF, half * DEVS : (half + 1) * DEVS])
        out_ref[pl.ds(c, DEVS, stride=WIRE), :] = jnp.concatenate(rows, axis=0).T


def vmem():
    return pl.BlockSpec(memory_space=pltpu.VMEM)


def hbm():
    return pl.BlockSpec(memory_space=pltpu.HBM)


def smem():
    return pl.BlockSpec(memory_space=pltpu.SMEM)


def call(kernel, name, in_specs, outs, scratch, limit):
    return pl.pallas_call(
        kernel,
        name=name,
        out_shape=outs,
        in_specs=in_specs,
        out_specs=jax.tree.map(lambda _: vmem(), outs),
        scratch_shapes=scratch,
        compiler_params=pltpu.CompilerParams(vmem_limit_bytes=limit),
    )


def exchange(x):
    width = x.shape[0] * x.shape[1] // DEVS
    moved = lax.all_to_all(x.reshape(DEVS, 1, width), AXES, split_axis=0, concat_axis=0, tiled=True)
    return moved.reshape(x.shape)


def body(splat_params, list_owner, list_slot, list_length, target):
    shape = jax.ShapeDtypeStruct
    wire = shape((DEVS * WIRE, 128), F32)
    route = call(
        route_kernel, "route", [hbm(), hbm(), hbm()],
        (shape((DEVS, 128), jnp.int32), shape((ROWS, SEGS), F32), shape((ROWS, SEGS), F32)),
        [
            pltpu.SMEM(list_length.shape, jnp.int32), pltpu.VMEM((ROWS, SEGS), jnp.int32),
            pltpu.VMEM(list_slot.shape, jnp.int32), pltpu.SemaphoreType.DMA((3,)),
        ],
        ROUTE_LIMIT,
    )
    request, owners, ranks = route(list_length, list_owner.reshape(ROWS, SEGS), list_slot)
    asked = exchange(request)
    rows = splat_params.shape[1] // 8
    packed = pl.pallas_call(
        pack_kernel,
        name="pack",
        out_shape=shape((rows, 128), F32),
        in_specs=[hbm()],
        out_specs=hbm(),
        scratch_shapes=[
            pltpu.VMEM(splat_params.shape, F32), pltpu.VMEM((rows, 128), F32),
            pltpu.SemaphoreType.DMA((rows // STRETCH,)), pltpu.SemaphoreType.DMA,
        ],
        compiler_params=pltpu.CompilerParams(vmem_limit_bytes=61 << 20),
    )(splat_params)
    staging = [
        pltpu.SMEM((DEVS, 128), jnp.int32), pltpu.VMEM((DEVS, BLOCK * 128), BF16),
        pltpu.VMEM((DEVS * RANKS, 128), F32),
    ]
    table = pltpu.VMEM((rows, 128), F32)
    sems = pltpu.SemaphoreType.DMA((2,))
    numbers = shape((DEVS, 128), jnp.int32)
    groups = shape((DEVS // BLOCK * RANKS, DEVS), BF16)
    gather = call(gather_kernel, "gather", [vmem(), hbm()], (wire, numbers, groups), staging + [table, sems], 51 << 20)
    found, numbers, groups = gather(asked, packed)
    replies = exchange(found)
    entries = ROWS * SEGS
    marks = call(
        marks_kernel, "marks", [vmem(), vmem(), hbm()],
        (shape((KEYS, entries), BF16), shape((HALF, entries), BF16), shape((ROWS, SEGS), F32)), [], 16 << 20,
    )
    hot, mark, keys = marks(owners, ranks, numbers)
    field = pltpu.VMEM((256, SEGS), F32)
    deep = pltpu.VMEM((STEPS, 256, SEGS), F32)
    render = call(
        render_kernel, "render", [vmem()] * 5, (shape(target.shape, F32), wire),
        [
            pltpu.VMEM((entries, KEYS), BF16), pltpu.VMEM((10 * HALF, 3 * KEYS), BF16),
            pltpu.VMEM((10, ROWS, SEGS), F32), deep, deep, pltpu.VMEM((4, 256, SEGS), F32), field, field, field,
            pltpu.VMEM((4, 256, SEGS), F32), field, field,
            pltpu.VMEM((STEPS, 16, SEGS), F32), pltpu.VMEM((STEPS, 16, SEGS), F32),
            pltpu.VMEM((10, ROWS, SEGS), F32), pltpu.VMEM((10 * HALF, KEYS), F32),
        ],
        24 << 20,
    )
    images, outgoing = render(replies, hot, mark, keys, target)
    incoming = exchange(outgoing)
    scatter = pl.pallas_call(
        scatter_kernel,
        name="scatter",
        out_shape=shape(splat_params.shape, F32),
        in_specs=[vmem(), vmem(), vmem()],
        out_specs=hbm(),
        scratch_shapes=staging
        + [pltpu.VMEM((DEVS // BLOCK, 128, 128), F32), pltpu.VMEM(splat_params.shape, F32), sems]
        + [table] * CHAINS,
        compiler_params=pltpu.CompilerParams(vmem_limit_bytes=44 << 20),
    )
    return (images, scatter(numbers, groups, incoming))


def solution(mesh):
    in_specs = (
        P(None, AXES),
        P(AXES, None, None),
        P(AXES, None),
        P(AXES),
        P(None, AXES, None),
    )
    out_specs = (P(None, AXES, None), P(None, AXES))
    return jax.shard_map(body, mesh=mesh, in_specs=in_specs, out_specs=out_specs, check_vma=False)
```

```python
import jax
import jax.numpy as jnp
from jax import lax
from jax.experimental import pallas as pl
from jax.experimental.pallas import tpu as pltpu
from jax.sharding import PartitionSpec as P

AXES = ("row", "col")
DEVS = 128
RANKS = 64
TILES = 4
SEGS = 128
STEPS = 8
ROWS = TILES * STEPS
WIRE = 5
GROUP = 16
BLOCK = 16
TIERS = ((0, 48), (48, RANKS))
LOOK_UNROLL = 8
ADD_UNROLL = 4
STRETCH = 1024
UNROLL = 4
ROUTE_LIMIT = 63 << 20
SPLIT_UNROLL = 2
FORE = 4
FETCH = 4096
SPREAD = 4096
BACK = 8
CHAINS = 8
LOG2E = 1.4426950408889634
F32 = jnp.float32
BF16 = jnp.bfloat16


def iota(shape, dim):
    return lax.broadcasted_iota(jnp.int32, shape, dim)


def dot(a, b):
    return lax.dot_general(a, b, (((1,), (0,)), ((), ())), preferred_element_type=F32)


def dot_nt(a, b):
    return lax.dot_general(a, b, (((1,), (1,)), ((), ())), preferred_element_type=F32)


def split(x, parts):
    out = []
    for _ in range(parts - 1):
        head = x.astype(BF16)
        out.append(head)
        x = x - head.astype(F32)
    out.append(x.astype(BF16))
    return out


def onehot_rows(row, count):
    wide = jnp.broadcast_to(row, (count, row.shape[1]))
    return wide == iota(wide.shape, 0).astype(F32)


def route_kernel(
    length_hbm, owner_hbm, slot_hbm, request_ref, owner_out, rank_out, length_ref, owner_ref, slot_ref, sems
):
    pairs = ((length_hbm, length_ref), (owner_hbm, owner_ref), (slot_hbm, slot_ref))
    copies = [pltpu.make_async_copy(a, b, sems.at[i]) for i, (a, b) in enumerate(pairs)]
    for copy in copies:
        copy.start()
    for copy in copies:
        copy.wait()
    lane = iota((STEPS, SEGS), 1)
    step = iota((STEPS, SEGS), 0)
    picks = (lane & (STEPS - 1)) == step
    pieces = []
    for r in range(STEPS):
        rows = []
        slot_rows = []
        for t in range(TILES):
            own = jnp.broadcast_to(owner_ref[t * STEPS + r : t * STEPS + r + 1, :], (STEPS, SEGS))
            rows.append(jnp.where(picks, own, 0))
            slot = slot_ref[t : t + 1, r * SEGS : (r + 1) * SEGS]
            slot_rows.append(jnp.where(picks, jnp.broadcast_to(slot, (STEPS, SEGS)), 0))
        rows += [s >> 8 for s in slot_rows] + [s & 255 for s in slot_rows]
        pieces.append(jnp.concatenate(rows, axis=0).astype(F32).astype(BF16))
    spread = jnp.concatenate(pieces, axis=1)
    place = ((iota((STEPS * SEGS, SEGS), 0) >> 3) == iota((STEPS * SEGS, SEGS), 1)).astype(F32)
    moved = dot(spread, place.astype(BF16))
    lane = iota((ROWS, SEGS), 1)
    row = iota((ROWS, SEGS), 0)
    length = jnp.full((ROWS, SEGS), length_ref[0], jnp.int32)
    for t in range(1, TILES):
        length = jnp.where((row >> 3) == t, length_ref[t], length)
    live = (lane * STEPS + (row & (STEPS - 1))) < length
    owners = jnp.where(live, moved[0:ROWS], -1.0)
    high = moved[ROWS : 2 * ROWS]
    low = moved[2 * ROWS : 3 * ROWS]
    owner_out[...] = owners
    before = (iota((256, 256), 0) < iota((256, 256), 1)).astype(F32).astype(BF16)
    before = jnp.concatenate([before, jnp.ones((256, 256), BF16)], axis=1)
    rank_of = (iota((2 * RANKS, 256), 0) & (RANKS - 1)).astype(F32)
    upper = iota((2 * RANKS, 256), 0) < RANKS
    carry = jnp.zeros((DEVS, 256), F32)
    request = jnp.zeros((2 * RANKS, DEVS), F32)
    for n in range(ROWS // 2):
        pair = lambda x: jnp.concatenate([x[2 * n : 2 * n + 1], x[2 * n + 1 : 2 * n + 2]], axis=1)
        hot = onehot_rows(pair(owners), DEVS)
        hot16 = hot.astype(F32).astype(BF16)
        counted = dot(hot16, before)
        rank = jnp.sum(jnp.where(hot, counted[:, :256] + carry, 0.0), axis=0, keepdims=True)
        carry = carry + counted[:, 256:]
        rank_out[2 * n : 2 * n + 1, :] = rank[:, :SEGS]
        rank_out[2 * n + 1 : 2 * n + 2, :] = rank[:, SEGS:]
        values = jnp.where(upper, pair(high), pair(low))
        values = jnp.where(rank_of == rank, values, 0.0)
        request = request + dot_nt(values.astype(BF16), hot16)
    slots = request[:RANKS] * 256.0 + request[RANKS:]
    slots = jnp.concatenate([slots, slots], axis=0).T
    full = jnp.where(iota((DEVS, DEVS), 1) < RANKS, slots, carry[:, :DEVS])
    request_ref[...] = full.astype(jnp.int32)


def pack_kernel(params_hbm, out_hbm, params_ref, out_ref, in_sems, out_sem):
    width = 8 * STRETCH
    steps = params_ref.shape[1] // width
    pad = jnp.zeros((GROUP - 10, 128), F32)

    def read(i):
        at = pl.ds(pl.multiple_of(i * width, width), width)
        return pltpu.make_async_copy(params_hbm.at[:, at], params_ref.at[:, at], in_sems.at[i])

    for i in range(steps):
        read(i).start()

    def step(i, carry):
        read(i).wait()
        mine_ref = params_ref.at[:, pl.ds(pl.multiple_of(i * width, width), width)]
        rows = pl.ds(pl.multiple_of(i * STRETCH, STRETCH), STRETCH)
        done_ref = out_ref.at[rows]
        for n in range(STRETCH // 128):
            blocks = []
            for g in range(8):
                at = g * STRETCH + n * 128
                blocks += [mine_ref[:, at : at + 128], pad]
            done_ref[n * 128 : (n + 1) * 128, :] = jnp.concatenate(blocks, axis=0).T
        pltpu.make_async_copy(done_ref, out_hbm.at[rows], out_sem).start()
        return carry

    lax.fori_loop(0, steps, step, 0)
    pltpu.make_async_copy(out_ref, out_hbm, out_sem).wait()


def bit_clear(shift):
    return (iota((RANKS, 128), 1) & shift) == 0


def merge_groups(xs):
    xs = [xs[q] for q in (0, 4, 2, 6, 1, 5, 3, 7)]
    for shift in (16, 32, 64):
        half = len(xs) // 2
        low = bit_clear(shift)
        xs = [
            jnp.where(low, x, y) + pltpu.roll(jnp.where(low, y, x), shift, 1)
            for x, y in zip(xs[:half], xs[half:])
        ]
    return xs[0]


def spread_groups(x):
    xs = [x]
    for shift in (64, 32, 16):
        low = bit_clear(shift)
        nexts = []
        for y in xs:
            z = pltpu.roll(y, shift, 1)
            nexts += [jnp.where(low, y, z), jnp.where(low, z, y)]
        xs = nexts
    return xs


def prepare(asked_ref, row_number_ref, number_ref, number_sem, group_ref):
    asked = asked_ref[...]
    lane = iota((DEVS, 128), 1)
    row = ((asked >> 13) << 10) | (asked & (STRETCH - 1))
    row_number_ref[...] = jnp.where(lane < RANKS, row, asked)
    copy = pltpu.make_async_copy(row_number_ref, number_ref, number_sem)
    copy.start()
    group = jnp.where(lane < pltpu.roll(asked, RANKS, 1), (asked >> 10) & 7, 8)
    groups = group.astype(F32).T[:RANKS]
    for b in range(DEVS // BLOCK):
        turned = groups if b == 0 else pltpu.roll(groups, DEVS - b * BLOCK, 1)
        group_ref[b * RANKS : (b + 1) * RANKS, :] = turned.astype(BF16)
    return copy


def fill_widen(widen_ref):
    for n in range(BLOCK):
        widen_ref[:, n * 128 : (n + 1) * 128] = (iota((DEVS, 128), 0) == n).astype(F32).astype(BF16)


def wide_groups(group_ref, widen_ref, b):
    at = pl.ds(pl.multiple_of(b * RANKS, RANKS), RANKS)
    return dot(group_ref[at, :], widen_ref[...])


def gather_kernel(
    asked_ref, table_hbm, out_ref, row_number_ref, group_ref, number_ref, widen_ref, row_ref, table_ref, sems
):
    left = iota((WIRE, 128), 1) < RANKS
    fill = pltpu.make_async_copy(table_hbm, table_ref, sems.at[1])
    fill.start()
    copy = prepare(asked_ref, row_number_ref, number_ref, sems.at[0], group_ref)
    fill_widen(widen_ref)
    copy.wait()
    fill.wait()

    def source(src, carry):
        mine_ref = row_ref.at[pl.ds(pl.multiple_of(src * RANKS, RANKS), RANKS)]
        count = number_ref[src, RANKS]
        for low, high in TIERS:

            @pl.when((count > low) & (count <= high))
            def _():
                for rank in range(high):
                    mine_ref[rank : rank + 1, :] = table_ref[pl.ds(number_ref[src, rank], 1), :]

        return carry

    lax.fori_loop(0, DEVS, source, 0, unroll=LOOK_UNROLL)

    def block(b, carry):
        base = pl.multiple_of(b * BLOCK * RANKS, BLOCK * RANKS)
        groups = wide_groups(group_ref, widen_ref, b)
        lane_group = (iota((RANKS, 128), 1) >> 4).astype(F32)
        halves = []
        for half in range(2):
            picked = []
            for n in range(half * 8, half * 8 + 8):
                rows = row_ref[pl.ds(base + n * RANKS, RANKS), :]
                picked.append(jnp.where(lane_group == groups[:, n * 128 : (n + 1) * 128], rows, 0.0))
            halves.append(merge_groups(picked))
        turned = jnp.concatenate(halves, axis=0).T
        evens, odds = [], []
        for q in range(8):
            first = turned[q * GROUP : q * GROUP + WIRE]
            second = turned[q * GROUP + WIRE : q * GROUP + 2 * WIRE]
            evens.append(jnp.where(left, first, pltpu.roll(second, RANKS, 1)))
            odds.append(jnp.where(left, pltpu.roll(first, RANKS, 1), second))
        at = pl.multiple_of(b * BLOCK * WIRE, 8)
        out_ref[pl.ds(at, BLOCK * WIRE), :] = jnp.concatenate(evens + odds, axis=0)
        return carry

    lax.fori_loop(0, DEVS // BLOCK, block, 0, unroll=UNROLL)


def scatter_kernel(
    row_number_ref, group_ref, wire_ref, out_hbm, number_ref, widen_ref, row_ref, turn_ref, out_ref, sems, *totals
):
    left = iota((WIRE, 128), 1) < RANKS
    table_rows = totals[0].shape[0]
    copy = pltpu.make_async_copy(row_number_ref, number_ref, sems.at[0])
    copy.start()
    fill_widen(widen_ref)
    turn_ref[...] = jnp.zeros(turn_ref.shape, F32)

    def clear(i, carry):
        for ref in totals:
            ref[pl.ds(pl.multiple_of(i * 256, 256), 256), :] = jnp.zeros((256, 128), F32)
        return carry

    lax.fori_loop(0, table_rows // 256, clear, 0)

    def block(b, carry):
        at = pl.multiple_of(b * BLOCK * WIRE, 8)
        base = pl.multiple_of(b * BLOCK * RANKS, BLOCK * RANKS)
        wire = wire_ref[pl.ds(at, BLOCK * WIRE), :]
        mine_ref = turn_ref.at[b]
        for q in range(8):
            even = wire[q * WIRE : (q + 1) * WIRE]
            odd = wire[(q + 8) * WIRE : (q + 9) * WIRE]
            mine_ref[q * GROUP : q * GROUP + WIRE, :] = jnp.where(left, even, pltpu.roll(odd, RANKS, 1))
            mine_ref[q * GROUP + WIRE : q * GROUP + 2 * WIRE, :] = jnp.where(left, pltpu.roll(even, RANKS, 1), odd)
        turned = mine_ref[...].T
        groups = wide_groups(group_ref, widen_ref, b)
        lane_group = (iota((RANKS, 128), 1) >> 4).astype(F32)
        for half in range(2):
            spreads = spread_groups(turned[half * RANKS : (half + 1) * RANKS])
            for q in range(8):
                n = half * 8 + q
                row_ref[pl.ds(base + n * RANKS, RANKS), :] = jnp.where(
                    lane_group == groups[:, n * 128 : (n + 1) * 128], spreads[q], 0.0
                )
        return carry

    lax.fori_loop(0, DEVS // BLOCK, block, 0, unroll=SPLIT_UNROLL)
    copy.wait()

    def source(src, carry):
        mine_ref = row_ref.at[pl.ds(pl.multiple_of(src * RANKS, RANKS), RANKS)]
        count = number_ref[src, RANKS]
        for low, high in TIERS:

            @pl.when((count > low) & (count <= high))
            def _():
                for start in range(0, high, CHAINS):
                    news = []
                    for i, ref in enumerate(totals[: high - start]):
                        row = number_ref[src, start + i]
                        news.append((row, mine_ref[start + i : start + i + 1, :] + ref[pl.ds(row, 1), :]))
                    for ref, (row, total) in zip(totals, news):
                        ref[pl.ds(row, 1), :] = total

        return carry

    lax.fori_loop(0, DEVS, source, 0, unroll=ADD_UNROLL)

    def close(i, carry):
        base = pl.multiple_of(i * STRETCH, STRETCH)
        lanes = pl.ds(pl.multiple_of(i * 8 * STRETCH, 8 * STRETCH), 8 * STRETCH)
        mine_ref = out_ref.at[:, lanes]
        for n in range(STRETCH // 128):
            at = pl.ds(base + n * 128, 128)
            total = totals[0][at, :]
            for ref in totals[1:]:
                total = total + ref[at, :]
            total = total.T
            for g in range(8):
                spot = g * STRETCH + n * 128
                mine_ref[:, spot : spot + 128] = total[g * GROUP : g * GROUP + 10]
        pltpu.make_async_copy(mine_ref, out_hbm.at[:, lanes], sems.at[1]).start()
        return carry

    lax.fori_loop(0, table_rows // STRETCH, close, 0)
    pltpu.make_async_copy(out_ref, out_hbm, sems.at[1]).wait()


HALF = RANKS // 2
KEYS = 2 * DEVS


def marks_kernel(owner_ref, rank_ref, after_ref, hot_ref, mark_ref, key_ref):
    rank = rank_ref[...].astype(jnp.int32)
    owner = owner_ref[...]
    key = jnp.where(owner < 0.0, -1.0, owner + ((rank >> 5) * DEVS).astype(F32))
    rest = (rank & (HALF - 1)).astype(F32)
    key_ref[...] = key
    for n in range(ROWS):
        at = slice(n * SEGS, (n + 1) * SEGS)
        hot_ref[:, at] = onehot_rows(key[n : n + 1], KEYS).astype(F32).astype(BF16)
        mark_ref[:, at] = onehot_rows(rest[n : n + 1], HALF).astype(F32).astype(BF16)


def render_kernel(
    wire_ref, hot_ref, mark_ref, key_ref, target_ref, image_ref, out_ref,
    turned_ref,    left_ref, value_ref, fall_ref, flow_ref, sum_ref, keep_ref, reach_ref, behind_ref,
    shade_ref, column_ref, picture_ref, across_ref, tilt_ref, grad_ref, spread_ref,
):
    for c in range(WIRE):
        block = wire_ref[pl.ds(c, DEVS, stride=WIRE), :].T
        parts = split(block, 3)
        for h in range(2):
            v = c + WIRE * h
            for half in range(2):
                rows = slice(h * RANKS + half * HALF, h * RANKS + (half + 1) * HALF)
                for n in range(3):
                    at = n * KEYS + half * DEVS
                    left_ref[v * HALF : (v + 1) * HALF, at : at + DEVS] = parts[n][rows]

    columns = jnp.concatenate([key_ref[...], jnp.zeros((128 - ROWS, SEGS), F32)], axis=0).T
    for n in range(ROWS):
        column = jnp.broadcast_to(columns[:, n : n + 1], (SEGS, KEYS))
        turned_ref[n * SEGS : (n + 1) * SEGS, :] = (column == iota((SEGS, KEYS), 1).astype(F32)).astype(F32).astype(BF16)

    def fetch(n, carry):
        at = pl.ds(pl.multiple_of(n * FETCH, FETCH), FETCH)
        hot = hot_ref[:, at]
        mark = mark_ref[:, at].astype(F32)
        found = dot(left_ref[...], jnp.concatenate([hot, hot, hot], axis=0))
        for v in range(10):
            got = jnp.sum(found[v * HALF : (v + 1) * HALF] * mark, axis=0, keepdims=True)
            for i in range(FETCH // SEGS):
                value_ref[v, pl.ds(n * (FETCH // SEGS) + i, 1), :] = got[:, i * SEGS : (i + 1) * SEGS]
        return carry

    lax.fori_loop(0, ROWS * SEGS // FETCH, fetch, 0)

    flat = jnp.concatenate([target_ref[ch] for ch in range(4)] + [jnp.zeros((112, 256), F32)], axis=0)
    column_ref[...] = jnp.concatenate([flat[:, :128].T, flat[:, 128:].T], axis=0)
    picture_ref[...] = jnp.zeros((256, 128), F32)
    earlier = (iota((128, 128), 0) < iota((128, 128), 1)).astype(F32).astype(BF16)
    later = (iota((128, 128), 0) > iota((128, 128), 1)).astype(F32).astype(BF16)
    ones = jnp.ones((256, 128), BF16)
    earlier = jnp.concatenate([earlier, earlier, earlier], axis=0)
    later = jnp.concatenate([later, later], axis=0)
    pixel_x = iota((16, SEGS), 0).astype(F32) + 0.5

    def tile(t, carry):
        first = t * STEPS
        for k in range(STEPS):
            value = lambda v: value_ref[v, pl.ds(first + k, 1), :]
            offset_x = pixel_x - value(0)
            across_ref[k] = (-0.5 * LOG2E) * value(2) * offset_x * offset_x
            tilt_ref[k] = -LOG2E * value(3) * offset_x

        def forward(n, carry):
            for half in range(2):
                y = 2 * n + half
                pixel_y = y.astype(F32) + 0.5
                keep = jnp.ones((16, SEGS), F32)
                sums = [jnp.zeros((16, SEGS), F32) for _ in range(4)]
                at = pl.ds(pl.multiple_of(y * 16, 16), 16)
                for k in range(STEPS):
                    value = lambda v: value_ref[v, pl.ds(first + k, 1), :]
                    offset_y = pixel_y - value(1)
                    down = (-0.5 * LOG2E) * value(4) * offset_y * offset_y
                    fall = jnp.exp2(across_ref[k] + down + tilt_ref[k] * offset_y)
                    flow = fall * keep
                    weight = value(5) * flow
                    keep = keep - weight
                    for ch in range(4):
                        sums[ch] = sums[ch] + value(6 + ch) * weight
                    fall_ref[k, at, :] = fall
                    flow_ref[k, at, :] = flow
                keep_ref[at, :] = keep
                for ch in range(4):
                    sum_ref[ch, at, :] = sums[ch]
            return carry

        lax.fori_loop(0, 8, forward, 0, unroll=FORE)

        keep = keep_ref[...]
        logs = jnp.concatenate(split(jnp.log(keep), 3), axis=1)
        reach = jnp.exp(dot(logs, earlier))
        reach_ref[...] = reach
        spent = jnp.zeros((256, SEGS), F32)
        for ch in range(4):
            part = sum_ref[ch] * reach
            rendered = dot(jnp.concatenate(split(part, 2), axis=1), ones)
            here = iota((256, 128), 1) == ch * TILES + t
            wanted = jnp.sum(jnp.where(here, column_ref[...], 0.0), axis=1, keepdims=True)
            shade = 2.0 * (rendered - wanted)
            picture_ref[...] = jnp.where(here, rendered, picture_ref[...])
            shade_ref[ch] = shade
            spent = spent + shade * part
        rest = dot(jnp.concatenate(split(spent, 2), axis=1), later)
        behind_ref[...] = rest / (reach * keep)

        for k in reversed(range(STEPS)):
            value = lambda v: value_ref[v, pl.ds(first + k, 1), :]
            mean_y = jnp.broadcast_to(value(1), (8, SEGS))
            opacity = jnp.broadcast_to(value(5), (8, SEGS))
            colours = [jnp.broadcast_to(value(6 + ch), (8, SEGS)) for ch in range(4)]

            def backward(n, sums):
                zero, one, two, tints = sums
                zero, one, two, tints = list(zero), list(one), list(two), list(tints)
                for quarter in range(2):
                    y = 2 * n + quarter
                    offset_y = y.astype(F32) + 0.5 - mean_y
                    for half in range(2):
                        at = pl.ds(pl.multiple_of(y * 16 + half * 8, 8), 8)
                        shades = [shade_ref[ch, at, :] for ch in range(4)]
                        flow = flow_ref[k, at, :] * reach_ref[at, :]
                        lit = (shades[0] * colours[0] + shades[1] * colours[1]) + (
                            shades[2] * colours[2] + shades[3] * colours[3]
                        )
                        behind = behind_ref[at, :]
                        gap = lit - behind
                        behind_ref[at, :] = behind + opacity * fall_ref[k, at, :] * gap
                        grad = flow * gap
                        slope = grad * offset_y
                        zero[half] = zero[half] + grad
                        one[half] = one[half] + slope
                        two[half] = two[half] + slope * offset_y
                        for ch in range(4):
                            tints[ch] = tints[ch] + flow * shades[ch]
                return (tuple(zero), tuple(one), tuple(two), tuple(tints))

            blank = jnp.zeros((8, SEGS), F32)
            zero, one, two, tints = lax.fori_loop(
                0, 8, backward, ((blank,) * 2, (blank,) * 2, (blank,) * 2, (blank,) * 4), unroll=BACK
            )
            total = lambda x: jnp.sum(x, axis=0, keepdims=True)
            offset_x = pixel_x - value(0)
            near, far = offset_x[:8], offset_x[8:]
            sum_0 = total(zero[0] + zero[1])
            slope_x = (near * zero[0], far * zero[1])
            sum_x = total(slope_x[0] + slope_x[1])
            sum_xx = total(near * slope_x[0] + far * slope_x[1])
            sum_y = total(one[0] + one[1])
            sum_xy = total(near * one[0] + far * one[1])
            sum_yy = total(two[0] + two[1])
            opacity = value(5)
            grads = [
                opacity * (value(2) * sum_x + value(3) * sum_y),
                opacity * (value(4) * sum_y + value(3) * sum_x),
                -0.5 * opacity * sum_xx,
                -opacity * sum_xy,
                -0.5 * opacity * sum_yy,
                sum_0,
            ] + [opacity * total(tint) for tint in tints]
            for v in range(10):
                grad_ref[v, pl.ds(first + k, 1), :] = grads[v]
        return carry

    lax.fori_loop(0, TILES, tile, 0)

    picture = picture_ref[...]
    picture = jnp.concatenate([picture[:128].T, picture[128:].T], axis=1)
    for ch in range(4):
        image_ref[ch] = picture[ch * TILES : (ch + 1) * TILES, :]

    spread_ref[...] = jnp.zeros((10 * HALF, KEYS), F32)

    def spread(n, carry):
        at = pl.ds(pl.multiple_of(n * SPREAD, SPREAD), SPREAD)
        mark = mark_ref[:, at].astype(F32)
        heads, tails = [], []
        for v in range(10):
            count = SPREAD // SEGS
            grad = jnp.concatenate([grad_ref[v, pl.ds(count * n + i, 1), :] for i in range(count)], axis=1)
            head, tail = split(grad * mark, 2)
            heads.append(head)
            tails.append(tail)
        turned = turned_ref[at, :]
        both = jnp.concatenate([jnp.concatenate(heads, axis=0), jnp.concatenate(tails, axis=0)], axis=1)
        spread_ref[...] += dot(both, jnp.concatenate([turned, turned], axis=0))
        return carry

    lax.fori_loop(0, ROWS * SEGS // SPREAD, spread, 0)
    for c in range(WIRE):
        rows = []
        for h in range(2):
            for half in range(2):
                v = c + WIRE * h
                rows.append(spread_ref[v * HALF : (v + 1) * HALF, half * DEVS : (half + 1) * DEVS])
        out_ref[pl.ds(c, DEVS, stride=WIRE), :] = jnp.concatenate(rows, axis=0).T


def vmem():
    return pl.BlockSpec(memory_space=pltpu.VMEM)


def hbm():
    return pl.BlockSpec(memory_space=pltpu.HBM)


def smem():
    return pl.BlockSpec(memory_space=pltpu.SMEM)


def call(kernel, name, in_specs, outs, scratch, limit):
    return pl.pallas_call(
        kernel,
        name=name,
        out_shape=outs,
        in_specs=in_specs,
        out_specs=jax.tree.map(lambda _: vmem(), outs),
        scratch_shapes=scratch,
        compiler_params=pltpu.CompilerParams(vmem_limit_bytes=limit),
    )


def exchange(x):
    width = x.shape[0] * x.shape[1] // DEVS
    moved = lax.all_to_all(x.reshape(DEVS, 1, width), AXES, split_axis=0, concat_axis=0, tiled=True)
    return moved.reshape(x.shape)


def body(splat_params, list_owner, list_slot, list_length, target):
    shape = jax.ShapeDtypeStruct
    wire = shape((DEVS * WIRE, 128), F32)
    route = call(
        route_kernel, "route", [hbm(), hbm(), hbm()],
        (shape((DEVS, 128), jnp.int32), shape((ROWS, SEGS), F32), shape((ROWS, SEGS), F32)),
        [
            pltpu.SMEM(list_length.shape, jnp.int32), pltpu.VMEM((ROWS, SEGS), jnp.int32),
            pltpu.VMEM(list_slot.shape, jnp.int32), pltpu.SemaphoreType.DMA((3,)),
        ],
        ROUTE_LIMIT,
    )
    request, owners, ranks = route(list_length, list_owner.reshape(ROWS, SEGS), list_slot)
    asked = exchange(request)
    rows = splat_params.shape[1] // 8
    packed = pl.pallas_call(
        pack_kernel,
        name="pack",
        out_shape=shape((rows, 128), F32),
        in_specs=[hbm()],
        out_specs=hbm(),
        scratch_shapes=[
            pltpu.VMEM(splat_params.shape, F32), pltpu.VMEM((rows, 128), F32),
            pltpu.SemaphoreType.DMA((rows // STRETCH,)), pltpu.SemaphoreType.DMA,
        ],
        compiler_params=pltpu.CompilerParams(vmem_limit_bytes=61 << 20),
    )(splat_params)
    staging = [
        pltpu.SMEM((DEVS, 128), jnp.int32), pltpu.VMEM((DEVS, BLOCK * 128), BF16),
        pltpu.VMEM((DEVS * RANKS, 128), F32),
    ]
    table = pltpu.VMEM((rows, 128), F32)
    sems = pltpu.SemaphoreType.DMA((2,))
    numbers = shape((DEVS, 128), jnp.int32)
    groups = shape((DEVS // BLOCK * RANKS, DEVS), BF16)
    gather = call(gather_kernel, "gather", [vmem(), hbm()], (wire, numbers, groups), staging + [table, sems], 51 << 20)
    found, numbers, groups = gather(asked, packed)
    replies = exchange(found)
    entries = ROWS * SEGS
    marks = call(
        marks_kernel, "marks", [vmem(), vmem(), hbm()],
        (shape((KEYS, entries), BF16), shape((HALF, entries), BF16), shape((ROWS, SEGS), F32)), [], 16 << 20,
    )
    hot, mark, keys = marks(owners, ranks, numbers)
    field = pltpu.VMEM((256, SEGS), F32)
    deep = pltpu.VMEM((STEPS, 256, SEGS), F32)
    render = call(
        render_kernel, "render", [vmem()] * 5, (shape(target.shape, F32), wire),
        [
            pltpu.VMEM((entries, KEYS), BF16), pltpu.VMEM((10 * HALF, 3 * KEYS), BF16),
            pltpu.VMEM((10, ROWS, SEGS), F32), deep, deep, pltpu.VMEM((4, 256, SEGS), F32), field, field, field,
            pltpu.VMEM((4, 256, SEGS), F32), field, field,
            pltpu.VMEM((STEPS, 16, SEGS), F32), pltpu.VMEM((STEPS, 16, SEGS), F32),
            pltpu.VMEM((10, ROWS, SEGS), F32), pltpu.VMEM((10 * HALF, KEYS), F32),
        ],
        24 << 20,
    )
    images, outgoing = render(replies, hot, mark, keys, target)
    incoming = exchange(outgoing)
    scatter = pl.pallas_call(
        scatter_kernel,
        name="scatter",
        out_shape=shape(splat_params.shape, F32),
        in_specs=[vmem(), vmem(), vmem()],
        out_specs=hbm(),
        scratch_shapes=staging
        + [pltpu.VMEM((DEVS // BLOCK, 128, 128), F32), pltpu.VMEM(splat_params.shape, F32), sems]
        + [table] * CHAINS,
        compiler_params=pltpu.CompilerParams(vmem_limit_bytes=49 << 20),
    )
    return (images, scatter(numbers, groups, incoming))


def solution(mesh):
    in_specs = (
        P(None, AXES),
        P(AXES, None, None),
        P(AXES, None),
        P(AXES),
        P(None, AXES, None),
    )
    out_specs = (P(None, AXES, None), P(None, AXES))
    return jax.shard_map(body, mesh=mesh, in_specs=in_specs, out_specs=out_specs, check_vma=False)
```

```python
import jax
import jax.numpy as jnp
from jax import lax
from jax.experimental import pallas as pl
from jax.experimental.pallas import tpu as pltpu
from jax.sharding import PartitionSpec as P

AXES = ("row", "col")
DEVS = 128
RANKS = 64
TILES = 4
SEGS = 128
STEPS = 8
ROWS = TILES * STEPS
WIRE = 5
GROUP = 16
BLOCK = 16
TIERS = ((0, 48), (48, RANKS))
LOOK_UNROLL = 16
ADD_UNROLL = 8
STRETCH = 1024
UNROLL = 4
ROUTE_LIMIT = 63 << 20
SPLIT_UNROLL = 2
FORE = 4
FETCH = 4096
SPREAD = 4096
BACK = 8
CHAINS = 8
LOG2E = 1.4426950408889634
F32 = jnp.float32
BF16 = jnp.bfloat16


def iota(shape, dim):
    return lax.broadcasted_iota(jnp.int32, shape, dim)


def dot(a, b):
    return lax.dot_general(a, b, (((1,), (0,)), ((), ())), preferred_element_type=F32)


def dot_nt(a, b):
    return lax.dot_general(a, b, (((1,), (1,)), ((), ())), preferred_element_type=F32)


def split(x, parts):
    out = []
    for _ in range(parts - 1):
        head = x.astype(BF16)
        out.append(head)
        x = x - head.astype(F32)
    out.append(x.astype(BF16))
    return out


def onehot_rows(row, count):
    wide = jnp.broadcast_to(row, (count, row.shape[1]))
    return wide == iota(wide.shape, 0).astype(F32)


def route_kernel(
    length_hbm, owner_hbm, slot_hbm, request_ref, owner_out, rank_out, length_ref, owner_ref, slot_ref, sems
):
    pairs = ((length_hbm, length_ref), (owner_hbm, owner_ref), (slot_hbm, slot_ref))
    copies = [pltpu.make_async_copy(a, b, sems.at[i]) for i, (a, b) in enumerate(pairs)]
    for copy in copies:
        copy.start()
    for copy in copies:
        copy.wait()
    lane = iota((STEPS, SEGS), 1)
    step = iota((STEPS, SEGS), 0)
    picks = (lane & (STEPS - 1)) == step
    pieces = []
    for r in range(STEPS):
        rows = []
        slot_rows = []
        for t in range(TILES):
            own = jnp.broadcast_to(owner_ref[t * STEPS + r : t * STEPS + r + 1, :], (STEPS, SEGS))
            rows.append(jnp.where(picks, own, 0))
            slot = slot_ref[t : t + 1, r * SEGS : (r + 1) * SEGS]
            slot_rows.append(jnp.where(picks, jnp.broadcast_to(slot, (STEPS, SEGS)), 0))
        rows += [s >> 8 for s in slot_rows] + [s & 255 for s in slot_rows]
        pieces.append(jnp.concatenate(rows, axis=0).astype(F32).astype(BF16))
    spread = jnp.concatenate(pieces, axis=1)
    place = ((iota((STEPS * SEGS, SEGS), 0) >> 3) == iota((STEPS * SEGS, SEGS), 1)).astype(F32)
    moved = dot(spread, place.astype(BF16))
    lane = iota((ROWS, SEGS), 1)
    row = iota((ROWS, SEGS), 0)
    length = jnp.full((ROWS, SEGS), length_ref[0], jnp.int32)
    for t in range(1, TILES):
        length = jnp.where((row >> 3) == t, length_ref[t], length)
    live = (lane * STEPS + (row & (STEPS - 1))) < length
    owners = jnp.where(live, moved[0:ROWS], -1.0)
    high = moved[ROWS : 2 * ROWS]
    low = moved[2 * ROWS : 3 * ROWS]
    owner_out[...] = owners
    before = (iota((256, 256), 0) < iota((256, 256), 1)).astype(F32).astype(BF16)
    before = jnp.concatenate([before, jnp.ones((256, 256), BF16)], axis=1)
    rank_of = (iota((2 * RANKS, 256), 0) & (RANKS - 1)).astype(F32)
    upper = iota((2 * RANKS, 256), 0) < RANKS
    carry = jnp.zeros((DEVS, 256), F32)
    request = jnp.zeros((2 * RANKS, DEVS), F32)
    for n in range(ROWS // 2):
        pair = lambda x: jnp.concatenate([x[2 * n : 2 * n + 1], x[2 * n + 1 : 2 * n + 2]], axis=1)
        hot = onehot_rows(pair(owners), DEVS)
        hot16 = hot.astype(F32).astype(BF16)
        counted = dot(hot16, before)
        rank = jnp.sum(jnp.where(hot, counted[:, :256] + carry, 0.0), axis=0, keepdims=True)
        carry = carry + counted[:, 256:]
        rank_out[2 * n : 2 * n + 1, :] = rank[:, :SEGS]
        rank_out[2 * n + 1 : 2 * n + 2, :] = rank[:, SEGS:]
        values = jnp.where(upper, pair(high), pair(low))
        values = jnp.where(rank_of == rank, values, 0.0)
        request = request + dot_nt(values.astype(BF16), hot16)
    slots = request[:RANKS] * 256.0 + request[RANKS:]
    slots = jnp.concatenate([slots, slots], axis=0).T
    full = jnp.where(iota((DEVS, DEVS), 1) < RANKS, slots, carry[:, :DEVS])
    request_ref[...] = full.astype(jnp.int32)


def pack_kernel(params_hbm, out_hbm, params_ref, out_ref, in_sems, out_sem):
    width = 8 * STRETCH
    steps = params_ref.shape[1] // width
    pad = jnp.zeros((GROUP - 10, 128), F32)

    def read(i):
        at = pl.ds(pl.multiple_of(i * width, width), width)
        return pltpu.make_async_copy(params_hbm.at[:, at], params_ref.at[:, at], in_sems.at[i])

    for i in range(steps):
        read(i).start()

    def step(i, carry):
        read(i).wait()
        mine_ref = params_ref.at[:, pl.ds(pl.multiple_of(i * width, width), width)]
        rows = pl.ds(pl.multiple_of(i * STRETCH, STRETCH), STRETCH)
        done_ref = out_ref.at[rows]
        for n in range(STRETCH // 128):
            blocks = []
            for g in range(8):
                at = g * STRETCH + n * 128
                blocks += [mine_ref[:, at : at + 128], pad]
            done_ref[n * 128 : (n + 1) * 128, :] = jnp.concatenate(blocks, axis=0).T
        pltpu.make_async_copy(done_ref, out_hbm.at[rows], out_sem).start()
        return carry

    lax.fori_loop(0, steps, step, 0)
    pltpu.make_async_copy(out_ref, out_hbm, out_sem).wait()


def bit_clear(shift):
    return (iota((RANKS, 128), 1) & shift) == 0


def merge_groups(xs):
    xs = [xs[q] for q in (0, 4, 2, 6, 1, 5, 3, 7)]
    for shift in (16, 32, 64):
        half = len(xs) // 2
        low = bit_clear(shift)
        xs = [
            jnp.where(low, x, y) + pltpu.roll(jnp.where(low, y, x), shift, 1)
            for x, y in zip(xs[:half], xs[half:])
        ]
    return xs[0]


def spread_groups(x):
    xs = [x]
    for shift in (64, 32, 16):
        low = bit_clear(shift)
        nexts = []
        for y in xs:
            z = pltpu.roll(y, shift, 1)
            nexts += [jnp.where(low, y, z), jnp.where(low, z, y)]
        xs = nexts
    return xs


def prepare(asked_ref, row_number_ref, number_ref, number_sem, group_ref):
    asked = asked_ref[...]
    lane = iota((DEVS, 128), 1)
    row = ((asked >> 13) << 10) | (asked & (STRETCH - 1))
    row_number_ref[...] = jnp.where(lane < RANKS, row, asked)
    copy = pltpu.make_async_copy(row_number_ref, number_ref, number_sem)
    copy.start()
    group = jnp.where(lane < pltpu.roll(asked, RANKS, 1), (asked >> 10) & 7, 8)
    groups = group.astype(F32).T[:RANKS]
    for b in range(DEVS // BLOCK):
        turned = groups if b == 0 else pltpu.roll(groups, DEVS - b * BLOCK, 1)
        group_ref[b * RANKS : (b + 1) * RANKS, :] = turned.astype(BF16)
    return copy


def fill_widen(widen_ref):
    for n in range(BLOCK):
        widen_ref[:, n * 128 : (n + 1) * 128] = (iota((DEVS, 128), 0) == n).astype(F32).astype(BF16)


def wide_groups(group_ref, widen_ref, b):
    at = pl.ds(pl.multiple_of(b * RANKS, RANKS), RANKS)
    return dot(group_ref[at, :], widen_ref[...])


def gather_kernel(
    asked_ref, table_hbm, out_ref, row_number_ref, group_ref, number_ref, widen_ref, row_ref, table_ref, sems
):
    left = iota((WIRE, 128), 1) < RANKS
    fill = pltpu.make_async_copy(table_hbm, table_ref, sems.at[1])
    fill.start()
    copy = prepare(asked_ref, row_number_ref, number_ref, sems.at[0], group_ref)
    fill_widen(widen_ref)
    copy.wait()
    fill.wait()

    def source(src, carry):
        mine_ref = row_ref.at[pl.ds(pl.multiple_of(src * RANKS, RANKS), RANKS)]
        count = number_ref[src, RANKS]
        for low, high in TIERS:

            @pl.when((count > low) & (count <= high))
            def _():
                for rank in range(high):
                    mine_ref[rank : rank + 1, :] = table_ref[pl.ds(number_ref[src, rank], 1), :]

        return carry

    lax.fori_loop(0, DEVS, source, 0, unroll=LOOK_UNROLL)

    def block(b, carry):
        base = pl.multiple_of(b * BLOCK * RANKS, BLOCK * RANKS)
        groups = wide_groups(group_ref, widen_ref, b)
        lane_group = (iota((RANKS, 128), 1) >> 4).astype(F32)
        halves = []
        for half in range(2):
            picked = []
            for n in range(half * 8, half * 8 + 8):
                rows = row_ref[pl.ds(base + n * RANKS, RANKS), :]
                picked.append(jnp.where(lane_group == groups[:, n * 128 : (n + 1) * 128], rows, 0.0))
            halves.append(merge_groups(picked))
        turned = jnp.concatenate(halves, axis=0).T
        evens, odds = [], []
        for q in range(8):
            first = turned[q * GROUP : q * GROUP + WIRE]
            second = turned[q * GROUP + WIRE : q * GROUP + 2 * WIRE]
            evens.append(jnp.where(left, first, pltpu.roll(second, RANKS, 1)))
            odds.append(jnp.where(left, pltpu.roll(first, RANKS, 1), second))
        at = pl.multiple_of(b * BLOCK * WIRE, 8)
        out_ref[pl.ds(at, BLOCK * WIRE), :] = jnp.concatenate(evens + odds, axis=0)
        return carry

    lax.fori_loop(0, DEVS // BLOCK, block, 0, unroll=UNROLL)


def scatter_kernel(
    row_number_ref, group_ref, wire_ref, out_hbm, number_ref, widen_ref, row_ref, turn_ref, out_ref, sems, *totals
):
    left = iota((WIRE, 128), 1) < RANKS
    table_rows = totals[0].shape[0]
    copy = pltpu.make_async_copy(row_number_ref, number_ref, sems.at[0])
    copy.start()
    fill_widen(widen_ref)
    turn_ref[...] = jnp.zeros(turn_ref.shape, F32)

    def clear(i, carry):
        for ref in totals:
            ref[pl.ds(pl.multiple_of(i * 256, 256), 256), :] = jnp.zeros((256, 128), F32)
        return carry

    lax.fori_loop(0, table_rows // 256, clear, 0)

    def block(b, carry):
        at = pl.multiple_of(b * BLOCK * WIRE, 8)
        base = pl.multiple_of(b * BLOCK * RANKS, BLOCK * RANKS)
        wire = wire_ref[pl.ds(at, BLOCK * WIRE), :]
        mine_ref = turn_ref.at[b]
        for q in range(8):
            even = wire[q * WIRE : (q + 1) * WIRE]
            odd = wire[(q + 8) * WIRE : (q + 9) * WIRE]
            mine_ref[q * GROUP : q * GROUP + WIRE, :] = jnp.where(left, even, pltpu.roll(odd, RANKS, 1))
            mine_ref[q * GROUP + WIRE : q * GROUP + 2 * WIRE, :] = jnp.where(left, pltpu.roll(even, RANKS, 1), odd)
        turned = mine_ref[...].T
        groups = wide_groups(group_ref, widen_ref, b)
        lane_group = (iota((RANKS, 128), 1) >> 4).astype(F32)
        for half in range(2):
            spreads = spread_groups(turned[half * RANKS : (half + 1) * RANKS])
            for q in range(8):
                n = half * 8 + q
                row_ref[pl.ds(base + n * RANKS, RANKS), :] = jnp.where(
                    lane_group == groups[:, n * 128 : (n + 1) * 128], spreads[q], 0.0
                )
        return carry

    lax.fori_loop(0, DEVS // BLOCK, block, 0, unroll=SPLIT_UNROLL)
    copy.wait()

    def source(src, carry):
        mine_ref = row_ref.at[pl.ds(pl.multiple_of(src * RANKS, RANKS), RANKS)]
        count = number_ref[src, RANKS]
        for low, high in TIERS:

            @pl.when((count > low) & (count <= high))
            def _():
                for start in range(0, high, CHAINS):
                    news = []
                    for i, ref in enumerate(totals[: high - start]):
                        row = number_ref[src, start + i]
                        news.append((row, mine_ref[start + i : start + i + 1, :] + ref[pl.ds(row, 1), :]))
                    for ref, (row, total) in zip(totals, news):
                        ref[pl.ds(row, 1), :] = total

        return carry

    lax.fori_loop(0, DEVS, source, 0, unroll=ADD_UNROLL)

    def close(i, carry):
        base = pl.multiple_of(i * STRETCH, STRETCH)
        lanes = pl.ds(pl.multiple_of(i * 8 * STRETCH, 8 * STRETCH), 8 * STRETCH)
        mine_ref = out_ref.at[:, lanes]
        for n in range(STRETCH // 128):
            at = pl.ds(base + n * 128, 128)
            total = totals[0][at, :]
            for ref in totals[1:]:
                total = total + ref[at, :]
            total = total.T
            for g in range(8):
                spot = g * STRETCH + n * 128
                mine_ref[:, spot : spot + 128] = total[g * GROUP : g * GROUP + 10]
        pltpu.make_async_copy(mine_ref, out_hbm.at[:, lanes], sems.at[1]).start()
        return carry

    lax.fori_loop(0, table_rows // STRETCH, close, 0)
    pltpu.make_async_copy(out_ref, out_hbm, sems.at[1]).wait()


HALF = RANKS // 2
KEYS = 2 * DEVS


def marks_kernel(owner_ref, rank_ref, after_ref, hot_ref, mark_ref, key_ref):
    rank = rank_ref[...].astype(jnp.int32)
    owner = owner_ref[...]
    key = jnp.where(owner < 0.0, -1.0, owner + ((rank >> 5) * DEVS).astype(F32))
    rest = (rank & (HALF - 1)).astype(F32)
    key_ref[...] = key
    for n in range(ROWS):
        at = slice(n * SEGS, (n + 1) * SEGS)
        hot_ref[:, at] = onehot_rows(key[n : n + 1], KEYS).astype(F32).astype(BF16)
        mark_ref[:, at] = onehot_rows(rest[n : n + 1], HALF).astype(F32).astype(BF16)


def render_kernel(
    wire_ref, hot_ref, mark_ref, key_ref, target_ref, image_ref, out_ref,
    turned_ref,    left_ref, value_ref, fall_ref, flow_ref, sum_ref, keep_ref, reach_ref, behind_ref,
    shade_ref, column_ref, picture_ref, across_ref, tilt_ref, grad_ref, spread_ref,
):
    for c in range(WIRE):
        block = wire_ref[pl.ds(c, DEVS, stride=WIRE), :].T
        parts = split(block, 3)
        for h in range(2):
            v = c + WIRE * h
            for half in range(2):
                rows = slice(h * RANKS + half * HALF, h * RANKS + (half + 1) * HALF)
                for n in range(3):
                    at = n * KEYS + half * DEVS
                    left_ref[v * HALF : (v + 1) * HALF, at : at + DEVS] = parts[n][rows]

    columns = jnp.concatenate([key_ref[...], jnp.zeros((128 - ROWS, SEGS), F32)], axis=0).T
    for n in range(ROWS):
        column = jnp.broadcast_to(columns[:, n : n + 1], (SEGS, KEYS))
        turned_ref[n * SEGS : (n + 1) * SEGS, :] = (column == iota((SEGS, KEYS), 1).astype(F32)).astype(F32).astype(BF16)

    def fetch(n, carry):
        at = pl.ds(pl.multiple_of(n * FETCH, FETCH), FETCH)
        hot = hot_ref[:, at]
        mark = mark_ref[:, at].astype(F32)
        found = dot(left_ref[...], jnp.concatenate([hot, hot, hot], axis=0))
        for v in range(10):
            got = jnp.sum(found[v * HALF : (v + 1) * HALF] * mark, axis=0, keepdims=True)
            for i in range(FETCH // SEGS):
                value_ref[v, pl.ds(n * (FETCH // SEGS) + i, 1), :] = got[:, i * SEGS : (i + 1) * SEGS]
        return carry

    lax.fori_loop(0, ROWS * SEGS // FETCH, fetch, 0)

    flat = jnp.concatenate([target_ref[ch] for ch in range(4)] + [jnp.zeros((112, 256), F32)], axis=0)
    column_ref[...] = jnp.concatenate([flat[:, :128].T, flat[:, 128:].T], axis=0)
    picture_ref[...] = jnp.zeros((256, 128), F32)
    earlier = (iota((128, 128), 0) < iota((128, 128), 1)).astype(F32).astype(BF16)
    later = (iota((128, 128), 0) > iota((128, 128), 1)).astype(F32).astype(BF16)
    ones = jnp.ones((256, 128), BF16)
    earlier = jnp.concatenate([earlier, earlier, earlier], axis=0)
    later = jnp.concatenate([later, later], axis=0)
    pixel_x = iota((16, SEGS), 0).astype(F32) + 0.5

    def tile(t, carry):
        first = t * STEPS
        for k in range(STEPS):
            value = lambda v: value_ref[v, pl.ds(first + k, 1), :]
            offset_x = pixel_x - value(0)
            across_ref[k] = (-0.5 * LOG2E) * value(2) * offset_x * offset_x
            tilt_ref[k] = -LOG2E * value(3) * offset_x

        def forward(n, carry):
            for half in range(2):
                y = 2 * n + half
                pixel_y = y.astype(F32) + 0.5
                keep = jnp.ones((16, SEGS), F32)
                sums = [jnp.zeros((16, SEGS), F32) for _ in range(4)]
                at = pl.ds(pl.multiple_of(y * 16, 16), 16)
                for k in range(STEPS):
                    value = lambda v: value_ref[v, pl.ds(first + k, 1), :]
                    offset_y = pixel_y - value(1)
                    down = (-0.5 * LOG2E) * value(4) * offset_y * offset_y
                    fall = jnp.exp2(across_ref[k] + down + tilt_ref[k] * offset_y)
                    flow = fall * keep
                    weight = value(5) * flow
                    keep = keep - weight
                    for ch in range(4):
                        sums[ch] = sums[ch] + value(6 + ch) * weight
                    fall_ref[k, at, :] = fall
                    flow_ref[k, at, :] = flow
                keep_ref[at, :] = keep
                for ch in range(4):
                    sum_ref[ch, at, :] = sums[ch]
            return carry

        lax.fori_loop(0, 8, forward, 0, unroll=FORE)

        keep = keep_ref[...]
        logs = jnp.concatenate(split(jnp.log(keep), 3), axis=1)
        reach = jnp.exp(dot(logs, earlier))
        reach_ref[...] = reach
        spent = jnp.zeros((256, SEGS), F32)
        for ch in range(4):
            part = sum_ref[ch] * reach
            rendered = dot(jnp.concatenate(split(part, 2), axis=1), ones)
            here = iota((256, 128), 1) == ch * TILES + t
            wanted = jnp.sum(jnp.where(here, column_ref[...], 0.0), axis=1, keepdims=True)
            shade = 2.0 * (rendered - wanted)
            picture_ref[...] = jnp.where(here, rendered, picture_ref[...])
            shade_ref[ch] = shade
            spent = spent + shade * part
        rest = dot(jnp.concatenate(split(spent, 2), axis=1), later)
        behind_ref[...] = rest / (reach * keep)

        for k in reversed(range(STEPS)):
            value = lambda v: value_ref[v, pl.ds(first + k, 1), :]
            mean_y = jnp.broadcast_to(value(1), (8, SEGS))
            opacity = jnp.broadcast_to(value(5), (8, SEGS))
            colours = [jnp.broadcast_to(value(6 + ch), (8, SEGS)) for ch in range(4)]

            def backward(n, sums):
                zero, one, two, tints = sums
                zero, one, two, tints = list(zero), list(one), list(two), list(tints)
                for quarter in range(2):
                    y = 2 * n + quarter
                    offset_y = y.astype(F32) + 0.5 - mean_y
                    for half in range(2):
                        at = pl.ds(pl.multiple_of(y * 16 + half * 8, 8), 8)
                        shades = [shade_ref[ch, at, :] for ch in range(4)]
                        flow = flow_ref[k, at, :] * reach_ref[at, :]
                        lit = (shades[0] * colours[0] + shades[1] * colours[1]) + (
                            shades[2] * colours[2] + shades[3] * colours[3]
                        )
                        behind = behind_ref[at, :]
                        gap = lit - behind
                        behind_ref[at, :] = behind + opacity * fall_ref[k, at, :] * gap
                        grad = flow * gap
                        slope = grad * offset_y
                        zero[half] = zero[half] + grad
                        one[half] = one[half] + slope
                        two[half] = two[half] + slope * offset_y
                        for ch in range(4):
                            tints[ch] = tints[ch] + flow * shades[ch]
                return (tuple(zero), tuple(one), tuple(two), tuple(tints))

            blank = jnp.zeros((8, SEGS), F32)
            zero, one, two, tints = lax.fori_loop(
                0, 8, backward, ((blank,) * 2, (blank,) * 2, (blank,) * 2, (blank,) * 4), unroll=BACK
            )
            total = lambda x: jnp.sum(x, axis=0, keepdims=True)
            offset_x = pixel_x - value(0)
            near, far = offset_x[:8], offset_x[8:]
            sum_0 = total(zero[0] + zero[1])
            slope_x = (near * zero[0], far * zero[1])
            sum_x = total(slope_x[0] + slope_x[1])
            sum_xx = total(near * slope_x[0] + far * slope_x[1])
            sum_y = total(one[0] + one[1])
            sum_xy = total(near * one[0] + far * one[1])
            sum_yy = total(two[0] + two[1])
            opacity = value(5)
            grads = [
                opacity * (value(2) * sum_x + value(3) * sum_y),
                opacity * (value(4) * sum_y + value(3) * sum_x),
                -0.5 * opacity * sum_xx,
                -opacity * sum_xy,
                -0.5 * opacity * sum_yy,
                sum_0,
            ] + [opacity * total(tint) for tint in tints]
            for v in range(10):
                grad_ref[v, pl.ds(first + k, 1), :] = grads[v]
        return carry

    lax.fori_loop(0, TILES, tile, 0)

    picture = picture_ref[...]
    picture = jnp.concatenate([picture[:128].T, picture[128:].T], axis=1)
    for ch in range(4):
        image_ref[ch] = picture[ch * TILES : (ch + 1) * TILES, :]

    spread_ref[...] = jnp.zeros((10 * HALF, KEYS), F32)

    def spread(n, carry):
        at = pl.ds(pl.multiple_of(n * SPREAD, SPREAD), SPREAD)
        mark = mark_ref[:, at].astype(F32)
        heads, tails = [], []
        for v in range(10):
            count = SPREAD // SEGS
            grad = jnp.concatenate([grad_ref[v, pl.ds(count * n + i, 1), :] for i in range(count)], axis=1)
            head, tail = split(grad * mark, 2)
            heads.append(head)
            tails.append(tail)
        turned = turned_ref[at, :]
        both = jnp.concatenate([jnp.concatenate(heads, axis=0), jnp.concatenate(tails, axis=0)], axis=1)
        spread_ref[...] += dot(both, jnp.concatenate([turned, turned], axis=0))
        return carry

    lax.fori_loop(0, ROWS * SEGS // SPREAD, spread, 0)
    for c in range(WIRE):
        rows = []
        for h in range(2):
            for half in range(2):
                v = c + WIRE * h
                rows.append(spread_ref[v * HALF : (v + 1) * HALF, half * DEVS : (half + 1) * DEVS])
        out_ref[pl.ds(c, DEVS, stride=WIRE), :] = jnp.concatenate(rows, axis=0).T


def vmem():
    return pl.BlockSpec(memory_space=pltpu.VMEM)


def hbm():
    return pl.BlockSpec(memory_space=pltpu.HBM)


def smem():
    return pl.BlockSpec(memory_space=pltpu.SMEM)


def call(kernel, name, in_specs, outs, scratch, limit):
    return pl.pallas_call(
        kernel,
        name=name,
        out_shape=outs,
        in_specs=in_specs,
        out_specs=jax.tree.map(lambda _: vmem(), outs),
        scratch_shapes=scratch,
        compiler_params=pltpu.CompilerParams(vmem_limit_bytes=limit),
    )


def exchange(x):
    width = x.shape[0] * x.shape[1] // DEVS
    moved = lax.all_to_all(x.reshape(DEVS, 1, width), AXES, split_axis=0, concat_axis=0, tiled=True)
    return moved.reshape(x.shape)


def body(splat_params, list_owner, list_slot, list_length, target):
    shape = jax.ShapeDtypeStruct
    wire = shape((DEVS * WIRE, 128), F32)
    route = call(
        route_kernel, "route", [hbm(), hbm(), hbm()],
        (shape((DEVS, 128), jnp.int32), shape((ROWS, SEGS), F32), shape((ROWS, SEGS), F32)),
        [
            pltpu.SMEM(list_length.shape, jnp.int32), pltpu.VMEM((ROWS, SEGS), jnp.int32),
            pltpu.VMEM(list_slot.shape, jnp.int32), pltpu.SemaphoreType.DMA((3,)),
        ],
        ROUTE_LIMIT,
    )
    request, owners, ranks = route(list_length, list_owner.reshape(ROWS, SEGS), list_slot)
    asked = exchange(request)
    rows = splat_params.shape[1] // 8
    packed = pl.pallas_call(
        pack_kernel,
        name="pack",
        out_shape=shape((rows, 128), F32),
        in_specs=[hbm()],
        out_specs=hbm(),
        scratch_shapes=[
            pltpu.VMEM(splat_params.shape, F32), pltpu.VMEM((rows, 128), F32),
            pltpu.SemaphoreType.DMA((rows // STRETCH,)), pltpu.SemaphoreType.DMA,
        ],
        compiler_params=pltpu.CompilerParams(vmem_limit_bytes=61 << 20),
    )(splat_params)
    staging = [
        pltpu.SMEM((DEVS, 128), jnp.int32), pltpu.VMEM((DEVS, BLOCK * 128), BF16),
        pltpu.VMEM((DEVS * RANKS, 128), F32),
    ]
    table = pltpu.VMEM((rows, 128), F32)
    sems = pltpu.SemaphoreType.DMA((2,))
    numbers = shape((DEVS, 128), jnp.int32)
    groups = shape((DEVS // BLOCK * RANKS, DEVS), BF16)
    gather = call(gather_kernel, "gather", [vmem(), hbm()], (wire, numbers, groups), staging + [table, sems], 51 << 20)
    found, numbers, groups = gather(asked, packed)
    replies = exchange(found)
    entries = ROWS * SEGS
    marks = call(
        marks_kernel, "marks", [vmem(), vmem(), hbm()],
        (shape((KEYS, entries), BF16), shape((HALF, entries), BF16), shape((ROWS, SEGS), F32)), [], 16 << 20,
    )
    hot, mark, keys = marks(owners, ranks, numbers)
    field = pltpu.VMEM((256, SEGS), F32)
    deep = pltpu.VMEM((STEPS, 256, SEGS), F32)
    render = call(
        render_kernel, "render", [vmem()] * 5, (shape(target.shape, F32), wire),
        [
            pltpu.VMEM((entries, KEYS), BF16), pltpu.VMEM((10 * HALF, 3 * KEYS), BF16),
            pltpu.VMEM((10, ROWS, SEGS), F32), deep, deep, pltpu.VMEM((4, 256, SEGS), F32), field, field, field,
            pltpu.VMEM((4, 256, SEGS), F32), field, field,
            pltpu.VMEM((STEPS, 16, SEGS), F32), pltpu.VMEM((STEPS, 16, SEGS), F32),
            pltpu.VMEM((10, ROWS, SEGS), F32), pltpu.VMEM((10 * HALF, KEYS), F32),
        ],
        24 << 20,
    )
    images, outgoing = render(replies, hot, mark, keys, target)
    incoming = exchange(outgoing)
    scatter = pl.pallas_call(
        scatter_kernel,
        name="scatter",
        out_shape=shape(splat_params.shape, F32),
        in_specs=[vmem(), vmem(), vmem()],
        out_specs=hbm(),
        scratch_shapes=staging
        + [pltpu.VMEM((DEVS // BLOCK, 128, 128), F32), pltpu.VMEM(splat_params.shape, F32), sems]
        + [table] * CHAINS,
        compiler_params=pltpu.CompilerParams(vmem_limit_bytes=49 << 20),
    )
    return (images, scatter(numbers, groups, incoming))


def solution(mesh):
    in_specs = (
        P(None, AXES),
        P(AXES, None, None),
        P(AXES, None),
        P(AXES),
        P(None, AXES, None),
    )
    out_specs = (P(None, AXES, None), P(None, AXES))
    return jax.shard_map(body, mesh=mesh, in_specs=in_specs, out_specs=out_specs, check_vma=False)
```
